32 devices in a mesh: dom: 16 (over z, x, core), feat: 2 (over y).
Axes of the slice: x: 2, y: 2, z: 4, core: 2. Of those that a mesh axis runs over, the one named last changes fastest.
Arguments:
- fine_latent: bfloat16 [256, 262144], P('feat', 'dom'), may hold values from -6 to 6
- coarse_latent: bfloat16 [256, 131072], P('feat', 'dom'), may hold values from -6 to 6
- parents: int32 [4, 262144], P(None, 'dom'), may hold values from 0 to 24575, as said below
- interp_weights: float32 [4, 262144], P(None, 'dom'), may hold values from 0.1 to 1
- live_rows: int32 [16], P('dom'), may hold values from 8192 to 16384, as said below
- w_fine: bfloat16 [256, 256], replicated, may hold values from -0.25 to 0.25
- w_parent: bfloat16 [256, 256], replicated, may hold values from -0.25 to 0.25
- w_edge_out: bfloat16 [256, 256], replicated, may hold values from -0.375 to 0.375
- w_node_fine: bfloat16 [256, 256], replicated, may hold values from -0.25 to 0.25
- w_node_agg: bfloat16 [256, 256], replicated, may hold values from -0.25 to 0.25
- w_node_out: bfloat16 [256, 256], replicated, may hold values from -0.375 to 0.375
- edge_bias: float32 [256], replicated, may hold values from -3 to 3
- node_bias: float32 [256], replicated, may hold values from -3 to 3
- norm_gain: float32 [256], replicated, may hold values from 0.1 to 1.9
- norm_bias: float32 [256], replicated, may hold values from -2 to 2
Outputs:
- fine_out: bfloat16 [256, 262144], P('feat', 'dom')
The draws below stay inside these ranges and needn't reach their ends.
Inputs may be any that keep to these rules, and one draw needn't show every extreme that they name: `parents`: a parent slot s of a fine node of block b names coarse node (b - 1) * 8192 + s, block b holding coarse nodes b * 8192 to (b + 1) * 8192 - 1; slots of block 0 are at least 8192, slots of the last block under 2 * 8192. `live_rows`: fine node slots of a block at or beyond its count are padding; at least one block is full.
All inputs are finite; a program needn't handle non-finite values.
Results may differ from the reference program's by a relative error of at most 0.0042.
Values may be sent and summed in bfloat16 or wider, within the bound.
No kernel may reach another device: no remote copies, remote signals or barrier semaphores. Data moves between devices by JAX's collectives and lax.ppermute only.
A program may use at most 128 MiB of HBM per device.

```python
import math
import jax
import jax.numpy as jnp
from jax import lax

D = 256
PARENTS = 4
FINE_DEV = 16384
COARSE_DEV = 8192
DOMAINS = 16
FINE = 262144
COARSE = 131072


def draw_parents(key, part):
    first_key, second_key, third_key = jax.random.split(jax.random.fold_in(key, 11), 3)
    blocks = jnp.broadcast_to((jnp.arange(FINE, dtype=jnp.int32) // FINE_DEV)[None, :], (PARENTS, FINE))
    offsets = jax.random.randint(first_key, (PARENTS, FINE), 0, COARSE_DEV)
    remote = jax.random.randint(second_key, (PARENTS, FINE), 0, 10) < 3
    sides = jax.random.randint(third_key, (PARENTS, FINE), 0, 2) * 2 - 1
    sides = jnp.where(blocks == 0, 1, jnp.where(blocks == DOMAINS - 1, -1, sides))
    window = 1 + jnp.where(remote, sides, 0)
    return (window * COARSE_DEV + offsets).astype(jnp.int32)


def draw_live_rows(key, part):
    first_key, second_key = jax.random.split(jax.random.fold_in(key, 23))
    counts = jax.random.randint(first_key, (DOMAINS,), FINE_DEV // 2, FINE_DEV + 1)
    full_block = jax.random.randint(second_key, (), 0, DOMAINS)
    return jnp.where(jnp.arange(DOMAINS) == full_block, FINE_DEV, counts).astype(jnp.int32)


def shard_levels(own_key, shape, cuts, smallest, top_value):
    gain, own = 1.0, jax.random.fold_in(own_key, 6)
    for dim, shards_of in cuts:
        draws = jnp.exp(jax.random.uniform(jax.random.fold_in(own, dim), (shards_of,), jnp.float32, smallest / len(cuts), top_value / len(cuts)))
        gain = gain * jnp.repeat(draws, shape[dim] // shards_of).reshape([-1 if axis == dim else 1 for axis in range(len(shape))])
    return gain


def scatter_about(key, dims, scale, bound, cuts=(), kind=jnp.bfloat16):
    values = scale * jax.random.normal(key, dims, jnp.float32)
    if cuts:
        values = values * shard_levels(key, dims, cuts, -0.22, 0.18)
    return jnp.clip(values, -bound, bound).astype(kind)


def setup_inputs(seed: int = 0) -> dict:
    streams_of = jax.random.split(jax.random.key(seed), 16)
    fine_latent = scatter_about(streams_of[0], (D, FINE), 1.0, 6.0, ((0, 2), (1, 16)))
    coarse_latent = scatter_about(streams_of[1], (D, COARSE), 1.0, 6.0, ((0, 2), (1, 16)))
    parents = draw_parents(jax.random.fold_in(streams_of[15], 71), 0)
    interp_weights = jnp.clip(jnp.exp(math.log(1.0) - 2.3025851 * jax.random.uniform(streams_of[3], (PARENTS, FINE), jnp.float32) ** shard_levels(streams_of[3], (PARENTS, FINE), ((1, 16),), -0.2, 0.2)), 0.1, 1.0)
    live_rows = draw_live_rows(jax.random.fold_in(streams_of[15], 71), 0)
    w_fine = scatter_about(streams_of[5], (D, D), (2 * D) ** -0.5, 0.25)
    w_parent = scatter_about(streams_of[6], (D, D), (2 * D) ** -0.5, 0.25)
    w_edge_out = scatter_about(streams_of[7], (D, D), D ** -0.5, 0.375)
    w_node_fine = scatter_about(streams_of[8], (D, D), (2 * D) ** -0.5, 0.25)
    w_node_agg = scatter_about(streams_of[9], (D, D), (2 * D) ** -0.5, 0.25)
    w_node_out = scatter_about(streams_of[10], (D, D), D ** -0.5, 0.375)
    edge_bias = scatter_about(streams_of[11], (D,), 0.5, 3.0, (), jnp.float32)
    node_bias = scatter_about(streams_of[12], (D,), 0.5, 3.0, (), jnp.float32)
    norm_gain = jnp.clip(1.0 + 0.18 * jax.random.normal(streams_of[13], (D,), jnp.float32), 0.1, 1.9)
    norm_bias = scatter_about(streams_of[14], (D,), 0.3, 2.0, (), jnp.float32)
    return {"fine_latent": fine_latent, "coarse_latent": coarse_latent, "parents": parents, "interp_weights": interp_weights, "live_rows": live_rows, "w_fine": w_fine, "w_parent": w_parent, "w_edge_out": w_edge_out, "w_node_fine": w_node_fine, "w_node_agg": w_node_agg, "w_node_out": w_node_out, "edge_bias": edge_bias, "node_bias": node_bias, "norm_gain": norm_gain, "norm_bias": norm_bias}


def update(latent, parent_rows, weights, params):
    w_fine, w_edge_out, w_node_fine, w_node_agg, w_node_out, edge_bias, node_bias, norm_gain, norm_bias = params
    fine_part = jnp.dot(latent, w_fine, preferred_element_type=jnp.float32) + edge_bias
    edge_hidden = jnp.maximum(fine_part[None] + parent_rows.astype(jnp.float32), 0.0).astype(jnp.bfloat16)
    width = edge_hidden.shape[2]
    message = jnp.dot(edge_hidden.reshape(-1, width), w_edge_out, preferred_element_type=jnp.float32).reshape(edge_hidden.shape)
    aggregate = lax.optimization_barrier(jnp.sum(weights[:, :, None] * message, axis=0)).astype(jnp.bfloat16)
    node_pre = jnp.dot(latent, w_node_fine, preferred_element_type=jnp.float32) + jnp.dot(aggregate, w_node_agg, preferred_element_type=jnp.float32) + node_bias
    node_hidden = jnp.maximum(node_pre, 0.0).astype(jnp.bfloat16)
    output = jnp.dot(node_hidden, w_node_out, preferred_element_type=jnp.float32)
    centre = lax.optimization_barrier(jnp.mean(output, axis=-1, keepdims=True))
    centered = output - centre
    spread = lax.optimization_barrier(jnp.mean(centered * centered, axis=-1, keepdims=True))
    normed = centered * lax.rsqrt(spread + 1e-05) * norm_gain + norm_bias
    return (latent.astype(jnp.float32) + normed).astype(jnp.bfloat16)

def reference(fine_latent, coarse_latent, parents, interp_weights, live_rows, w_fine, w_parent, w_edge_out, w_node_fine, w_node_agg, w_node_out, edge_bias, node_bias, norm_gain, norm_bias):
    params = (w_fine, w_edge_out, w_node_fine, w_node_agg, w_node_out, edge_bias, node_bias, norm_gain, norm_bias)
    projected = jnp.dot(coarse_latent.T, w_parent, preferred_element_type=jnp.float32).astype(jnp.bfloat16)
    latent_blocks = fine_latent.T.reshape(DOMAINS, FINE_DEV, D)
    parent_blocks = parents.reshape(PARENTS, DOMAINS, FINE_DEV).transpose(1, 0, 2)
    weight_blocks = interp_weights.reshape(PARENTS, DOMAINS, FINE_DEV).transpose(1, 0, 2)
    block_ids = jnp.arange(DOMAINS, dtype=jnp.int32)

    def one_block(packed):
        latent, parent_ids, weights, live_count, block = packed
        global_ids = (parent_ids + (block - 1) * COARSE_DEV).astype(jnp.int32)
        parent_rows = jnp.take(projected, global_ids, axis=0)
        updated = update(latent, parent_rows, weights, params)
        keep_rows = jnp.arange(FINE_DEV, dtype=jnp.int32) < live_count
        return jnp.where(keep_rows[:, None], updated, latent)
    result = lax.map(one_block, (latent_blocks, parent_blocks, weight_blocks, live_rows, block_ids))
    return result.reshape(FINE, D).T
```

```python
import functools

import jax
import jax.numpy as jnp
from jax import lax
from jax.experimental import pallas as pl
from jax.experimental.pallas import tpu as pltpu
from jax.sharding import PartitionSpec as P

F32 = jnp.float32
BF16 = jnp.bfloat16
PAD = 8
CHUNKS = 2


def dot(a, b, ca, cb):
    return lax.dot_general(a, b, (((ca,), (cb,)), ((), ())), preferred_element_type=F32)


def table_kernel(count, step, *refs):
    pieces, (weight, table, landed, sems) = refs[:-4], refs[-4:]
    blocks = len(pieces) // count
    rows = pieces[0].shape[1]
    steps = rows // step
    table[pl.ds(0, PAD), :] = jnp.zeros((PAD, 128), F32)
    table[pl.ds(PAD + 2 * blocks * rows, PAD), :] = jnp.zeros((PAD, 128), F32)

    def copies(block, i, slot):
        at = pl.multiple_of(i * step, step)
        features = pieces[0].shape[0]
        return [
            pltpu.make_async_copy(
                pieces[block * count + p].at[:, pl.ds(at, step)],
                landed.at[block % 2, slot, pl.ds(p * features, features), :],
                sems.at[block % 2, slot, p],
            )
            for p in range(count)
        ]

    for copy in copies(0, 0, 0):
        copy.start()
    for block in range(blocks):
        if block + 1 < blocks:
            for copy in copies(block + 1, 0, 0):
                copy.start()

        def one(i, carry, block=block):
            slot = lax.rem(i, 2)

            @pl.when(i + 1 < steps)
            def _():
                for copy in copies(block, i + 1, 1 - slot):
                    copy.start()

            for copy in copies(block, i, slot):
                copy.wait()
            projected = dot(landed[block % 2, slot], weight[...], 0, 0)
            base = pl.multiple_of(PAD + 2 * (block * rows + i * step), 8)
            table[pl.ds(base, step, stride=2), :] = projected[:, :128]
            table[pl.ds(base + 1, step, stride=2), :] = projected[:, 128:]
            return carry

        lax.fori_loop(0, steps, one, 0)


def update_kernel(count, step, live, slots, *refs):
    pieces = refs[:count]
    table, scales, w_latent, w_edge, w_agg, w_out_t, bias, gain, shift = refs[count : count + 9]
    outs = refs[count + 9 : 2 * count + 9]
    fine, total, spread_out, scale_rows = refs[2 * count + 9 :]
    parents = slots.shape[0]
    nodes = pieces[0].shape[1]
    sublane = lax.broadcasted_iota(jnp.int32, (8, 128), 0)
    owns = [sublane >= 2 * j for j in range(4)]

    def one_step(i, carry):
        at = pl.multiple_of(i * step, step)
        latent = jnp.concatenate([piece[:, pl.ds(at, step)] for piece in pieces], axis=0)
        first = dot(latent, w_latent[...], 0, 0) + bias[...]
        width = first.shape[1] // 2
        scale_rows[...] = scales[:, pl.ds(pl.multiple_of(2 * at, 2 * step), 2 * step)].T
        fine[pl.ds(0, step, stride=2), :] = first[:, :128]
        fine[pl.ds(1, step, stride=2), :] = first[:, 128:width]
        spread_out[...] = first[:, width:]

        def four_nodes(g, inner):
            base = pl.multiple_of(g * 8, 8)
            node = at + g * 4
            part = fine[pl.ds(base, 8), :]
            scale = scale_rows[pl.ds(base, 8), :]
            acc = None
            for k in range(parents):
                rows = None
                for j in range(4):
                    loaded = table[pl.ds(slots[k, node + j] + (PAD - 2 * j), 8), :]
                    rows = loaded if rows is None else jnp.where(owns[j], loaded, rows)
                hidden = jnp.maximum(part + rows, 0.0) * scale[:, k : k + 1]
                acc = hidden if acc is None else acc + hidden
            total[pl.ds(base, 8), :] = acc
            return inner

        lax.fori_loop(0, step // 4, four_nodes, 0, unroll=8)
        summed = jnp.concatenate(
            [total[pl.ds(0, step, stride=2), :], total[pl.ds(1, step, stride=2), :]], axis=1
        ).astype(BF16)
        aggregate = dot(summed, w_edge[...], 1, 0).astype(BF16)
        node_hidden = jnp.maximum(spread_out[...] + dot(aggregate, w_agg[...], 1, 0), 0.0).astype(BF16)
        output = dot(w_out_t[...], node_hidden, 1, 1)
        centered = output - jnp.mean(output, axis=0, keepdims=True)
        spread = jnp.mean(centered * centered, axis=0, keepdims=True)
        normed = centered * lax.rsqrt(spread + 1e-05) * gain[...] + shift[...]
        column = at + lax.broadcasted_iota(jnp.int32, (1, step), 1)
        moved = jnp.where(column < live[0], normed, 0.0)
        result = (latent.astype(F32) + moved).astype(BF16)
        part_rows = result.shape[0] // count
        for r in range(count):
            outs[r][:, pl.ds(at, step)] = result[r * part_rows : (r + 1) * part_rows]
        return carry

    lax.fori_loop(0, nodes // step, one_step, 0)


def build_table(pieces, weight, count):
    rows = pieces[0].shape[1] * len(pieces) // count
    step = min(512, pieces[0].shape[1])
    vmem = pl.BlockSpec(memory_space=pltpu.VMEM)
    return pl.pallas_call(
        functools.partial(table_kernel, count, step),
        out_shape=jax.ShapeDtypeStruct((2 * rows + 2 * PAD, 128), F32),
        in_specs=[pl.BlockSpec(memory_space=pl.ANY)] * len(pieces) + [vmem],
        out_specs=vmem,
        scratch_shapes=[
            pltpu.VMEM((2, 2, weight.shape[0], step), BF16),
            pltpu.SemaphoreType.DMA((2, 2, count)),
        ],
        compiler_params=pltpu.CompilerParams(vmem_limit_bytes=8 << 20),
        cost_estimate=pl.CostEstimate(flops=2 * rows * 65536, bytes_accessed=rows * 1536, transcendentals=0),
    )(*pieces, weight)


def update(live, slots, pieces, table, scales, params):
    count, nodes = len(pieces), pieces[0].shape[1]
    step = min(256, nodes)
    vmem = pl.BlockSpec(memory_space=pltpu.VMEM)
    smem = pl.BlockSpec(memory_space=pltpu.SMEM)
    return pl.pallas_call(
        functools.partial(update_kernel, count, step),
        out_shape=[jax.ShapeDtypeStruct(piece.shape, BF16) for piece in pieces],
        in_specs=[smem] * 2 + [vmem] * (count + 2 + len(params)),
        out_specs=[vmem] * count,
        scratch_shapes=[
            pltpu.VMEM((2 * step, 128), F32),
            pltpu.VMEM((2 * step, 128), F32),
            pltpu.VMEM((step, 256), F32),
            pltpu.VMEM((2 * step, 8), F32),
        ],
        compiler_params=pltpu.CompilerParams(vmem_limit_bytes=8 << 20),
        cost_estimate=pl.CostEstimate(flops=nodes * 700000, bytes_accessed=nodes * 2048, transcendentals=nodes),
    )(live, slots, *pieces, table, scales, *params)


def shards(
    fine_latent,
    coarse_latent,
    parents,
    interp_weights,
    live_rows,
    w_fine,
    w_parent,
    w_edge_out,
    w_node_fine,
    w_node_agg,
    w_node_out,
    edge_bias,
    node_bias,
    norm_gain,
    norm_bias,
):
    groups, domains = lax.axis_size("feat"), lax.axis_size("dom")
    rank = lax.axis_index("feat")
    own_features = fine_latent.shape[0]
    per_device = fine_latent.shape[1] // groups
    length = per_device // CHUNKS
    forward = [(i, i + 1) for i in range(domains - 1)]
    backward = [(i + 1, i) for i in range(domains - 1)]

    def turn(value, r):
        return lax.ppermute(value, "feat", [(i, (i + r) % groups) for i in range(groups)])

    owners = [(rank - r) % groups for r in range(groups)]
    own_block = [coarse_latent] + [turn(coarse_latent, r) for r in range(1, groups)]
    low = [lax.ppermute(piece, "dom", forward) for piece in own_block]
    high = [lax.ppermute(piece, "dom", backward) for piece in own_block]

    def ordered(weight, axis):
        parts = [lax.dynamic_slice_in_dim(weight, o * own_features, own_features, axis) for o in owners]
        return jnp.concatenate(parts, axis=axis)

    first_row = rank * per_device
    chunk_pieces = []
    for c in range(CHUNKS):
        pieces = [lax.dynamic_slice_in_dim(fine_latent, first_row + c * length, length, 1)]
        for r in range(1, groups):
            at = ((rank + r) % groups) * per_device + c * length
            part = lax.dynamic_slice_in_dim(fine_latent, at, length, 1)
            part, _ = lax.optimization_barrier((part, own_block[-1]))
            pieces.append(turn(part, r))
        chunk_pieces.append(pieces)

    table = build_table(low + own_block + high, ordered(w_parent, 0), groups)
    params = (
        jnp.concatenate([ordered(w_fine, 0), ordered(w_node_fine, 0)], axis=1),
        w_edge_out,
        w_node_agg,
        ordered(w_node_out, 1).T,
        jnp.concatenate([edge_bias, node_bias])[None],
        ordered(norm_gain, 0)[:, None],
        ordered(norm_bias, 0)[:, None],
    )
    slots = 2 * lax.dynamic_slice_in_dim(parents, first_row, per_device, 1)
    weights = lax.dynamic_slice_in_dim(interp_weights, first_row, per_device, 1)
    scales = jnp.pad(jnp.repeat(weights, 2, axis=1), ((0, 8 - weights.shape[0]), (0, 0)))
    result = fine_latent
    arrived = []
    for c in range(CHUNKS):
        start = c * length
        outs = update(
            live_rows - first_row - start,
            slots[:, start : start + length],
            chunk_pieces[c],
            table,
            scales[:, 2 * start : 2 * (start + length)],
            params,
        )
        result = lax.dynamic_update_slice_in_dim(result, outs[0], first_row + start, 1)
        for r in range(1, groups):
            arrived.append((turn(outs[r], -r), ((rank + r) % groups) * per_device + start))
    for part, at in arrived:
        result = lax.dynamic_update_slice_in_dim(result, part, at, 1)
    return result


def solution(mesh):
    in_specs = (P("feat", "dom"), P("feat", "dom"), P(None, "dom"), P(None, "dom"), P("dom")) + (P(),) * 10
    return jax.shard_map(shards, mesh=mesh, in_specs=in_specs, out_specs=P("feat", "dom"), check_vma=False)
```

```python
import functools

import jax
import jax.numpy as jnp
from jax import lax
from jax.experimental import pallas as pl
from jax.experimental.pallas import tpu as pltpu
from jax.sharding import PartitionSpec as P

F32 = jnp.float32
BF16 = jnp.bfloat16
PAD = 8
CHUNKS = 2
GROUPS = 16


def dot(a, b, ca, cb):
    return lax.dot_general(a, b, (((ca,), (cb,)), ((), ())), preferred_element_type=F32)


def table_kernel(count, step, *refs):
    pieces, (weight, table, landed, sems) = refs[:-4], refs[-4:]
    blocks = len(pieces) // count
    rows = pieces[0].shape[1]
    steps = rows // step
    table[pl.ds(0, PAD), :] = jnp.zeros((PAD, 128), F32)
    table[pl.ds(PAD + 2 * blocks * rows, PAD), :] = jnp.zeros((PAD, 128), F32)

    def copies(block, i, slot):
        at = pl.multiple_of(i * step, step)
        features = pieces[0].shape[0]
        return [
            pltpu.make_async_copy(
                pieces[block * count + p].at[:, pl.ds(at, step)],
                landed.at[block % 2, slot, pl.ds(p * features, features), :],
                sems.at[block % 2, slot, p],
            )
            for p in range(count)
        ]

    for copy in copies(0, 0, 0):
        copy.start()
    for block in range(blocks):
        if block + 1 < blocks:
            for copy in copies(block + 1, 0, 0):
                copy.start()

        def one(i, carry, block=block):
            slot = lax.rem(i, 2)

            @pl.when(i + 1 < steps)
            def _():
                for copy in copies(block, i + 1, 1 - slot):
                    copy.start()

            for copy in copies(block, i, slot):
                copy.wait()
            projected = dot(landed[block % 2, slot], weight[...], 0, 0)
            base = pl.multiple_of(PAD + 2 * (block * rows + i * step), 8)
            table[pl.ds(base, step, stride=2), :] = projected[:, :128]
            table[pl.ds(base + 1, step, stride=2), :] = projected[:, 128:]
            return carry

        lax.fori_loop(0, steps, one, 0)


def update_kernel(count, step, live, slots, *refs):
    pieces = refs[:count]
    table, scales, w_latent, w_edge, w_agg, w_out_t, bias, gain, shift = refs[count : count + 9]
    outs = refs[count + 9 : 2 * count + 9]
    fine, total, spread_out, scale_rows = refs[2 * count + 9 :]
    parents = slots.shape[0]
    nodes = pieces[0].shape[1]
    sublane = lax.broadcasted_iota(jnp.int32, (8, 128), 0)
    owns = [sublane >= 2 * j for j in range(4)]

    def one_step(i, carry):
        at = pl.multiple_of(i * step, step)
        latent = jnp.concatenate([piece[:, pl.ds(at, step)] for piece in pieces], axis=0)
        first = dot(latent, w_latent[...], 0, 0) + bias[...]
        width = first.shape[1] // 2
        scale_rows[...] = scales[:, pl.ds(pl.multiple_of(2 * at, 2 * step), 2 * step)].T
        fine[pl.ds(0, step, stride=2), :] = first[:, :128]
        fine[pl.ds(1, step, stride=2), :] = first[:, 128:width]
        spread_out[...] = first[:, width:]

        def group(g):
            base = pl.multiple_of(g * 8, 8)
            node = at + g * 4
            part = fine[pl.ds(base, 8), :]
            scale = scale_rows[pl.ds(base, 8), :]
            acc = None
            for k in range(parents):
                rows = None
                for j in range(4):
                    loaded = table[pl.ds(slots[k, node + j] + (PAD - 2 * j), 8), :]
                    rows = loaded if rows is None else jnp.where(owns[j], loaded, rows)
                hidden = jnp.maximum(part + rows, 0.0) * scale[:, k : k + 1]
                acc = hidden if acc is None else acc + hidden
            return acc

        def some_groups(b, inner):
            sums = [group(b * GROUPS + u) for u in range(GROUPS)]
            total[pl.ds(pl.multiple_of(b * GROUPS * 8, 8), GROUPS * 8), :] = jnp.concatenate(sums, axis=0)
            return inner

        lax.fori_loop(0, step // (4 * GROUPS), some_groups, 0)
        summed = jnp.concatenate(
            [total[pl.ds(0, step, stride=2), :], total[pl.ds(1, step, stride=2), :]], axis=1
        ).astype(BF16)
        aggregate = dot(summed, w_edge[...], 1, 0).astype(BF16)
        node_hidden = jnp.maximum(spread_out[...] + dot(aggregate, w_agg[...], 1, 0), 0.0).astype(BF16)
        output = dot(w_out_t[...], node_hidden, 1, 1)
        centered = output - jnp.mean(output, axis=0, keepdims=True)
        spread = jnp.mean(centered * centered, axis=0, keepdims=True)
        normed = centered * lax.rsqrt(spread + 1e-05) * gain[...] + shift[...]
        column = at + lax.broadcasted_iota(jnp.int32, (1, step), 1)
        moved = jnp.where(column < live[0], normed, 0.0)
        result = (latent.astype(F32) + moved).astype(BF16)
        part_rows = result.shape[0] // count
        for r in range(count):
            outs[r][:, pl.ds(at, step)] = result[r * part_rows : (r + 1) * part_rows]
        return carry

    lax.fori_loop(0, nodes // step, one_step, 0)


def build_table(pieces, weight, count):
    rows = pieces[0].shape[1] * len(pieces) // count
    step = min(2048, pieces[0].shape[1])
    vmem = pl.BlockSpec(memory_space=pltpu.VMEM)
    return pl.pallas_call(
        functools.partial(table_kernel, count, step),
        out_shape=jax.ShapeDtypeStruct((2 * rows + 2 * PAD, 128), F32),
        in_specs=[pl.BlockSpec(memory_space=pl.ANY)] * len(pieces) + [vmem],
        out_specs=vmem,
        scratch_shapes=[
            pltpu.VMEM((2, 2, weight.shape[0], step), BF16),
            pltpu.SemaphoreType.DMA((2, 2, count)),
        ],
        compiler_params=pltpu.CompilerParams(vmem_limit_bytes=10 << 20),
        cost_estimate=pl.CostEstimate(flops=2 * rows * 65536, bytes_accessed=rows * 1536, transcendentals=0),
    )(*pieces, weight)


def update(live, slots, pieces, table, scales, params):
    count, nodes = len(pieces), pieces[0].shape[1]
    step = min(512, nodes)
    vmem = pl.BlockSpec(memory_space=pltpu.VMEM)
    smem = pl.BlockSpec(memory_space=pltpu.SMEM)
    return pl.pallas_call(
        functools.partial(update_kernel, count, step),
        out_shape=[jax.ShapeDtypeStruct(piece.shape, BF16) for piece in pieces],
        in_specs=[smem] * 2 + [vmem] * (count + 2 + len(params)),
        out_specs=[vmem] * count,
        scratch_shapes=[
            pltpu.VMEM((2 * step, 128), F32),
            pltpu.VMEM((2 * step, 128), F32),
            pltpu.VMEM((step, 256), F32),
            pltpu.VMEM((2 * step, 8), F32),
        ],
        compiler_params=pltpu.CompilerParams(vmem_limit_bytes=10 << 20),
        cost_estimate=pl.CostEstimate(flops=nodes * 700000, bytes_accessed=nodes * 2048, transcendentals=nodes),
    )(live, slots, *pieces, table, scales, *params)


def shards(
    fine_latent,
    coarse_latent,
    parents,
    interp_weights,
    live_rows,
    w_fine,
    w_parent,
    w_edge_out,
    w_node_fine,
    w_node_agg,
    w_node_out,
    edge_bias,
    node_bias,
    norm_gain,
    norm_bias,
):
    groups, domains = lax.axis_size("feat"), lax.axis_size("dom")
    rank = lax.axis_index("feat")
    own_features = fine_latent.shape[0]
    per_device = fine_latent.shape[1] // groups
    length = per_device // CHUNKS
    forward = [(i, i + 1) for i in range(domains - 1)]
    backward = [(i + 1, i) for i in range(domains - 1)]

    def turn(value, r):
        return lax.ppermute(value, "feat", [(i, (i + r) % groups) for i in range(groups)])

    owners = [(rank - r) % groups for r in range(groups)]
    own_block = [coarse_latent] + [turn(coarse_latent, r) for r in range(1, groups)]
    low = [lax.ppermute(piece, "dom", forward) for piece in own_block]
    high = [lax.ppermute(piece, "dom", backward) for piece in own_block]

    def ordered(weight, axis):
        parts = [lax.dynamic_slice_in_dim(weight, o * own_features, own_features, axis) for o in owners]
        return jnp.concatenate(parts, axis=axis)

    first_row = rank * per_device
    chunk_pieces = []
    for c in range(CHUNKS):
        pieces = [lax.dynamic_slice_in_dim(fine_latent, first_row + c * length, length, 1)]
        for r in range(1, groups):
            at = ((rank + r) % groups) * per_device + c * length
            part = lax.dynamic_slice_in_dim(fine_latent, at, length, 1)
            part, _ = lax.optimization_barrier((part, own_block[-1]))
            pieces.append(turn(part, r))
        chunk_pieces.append(pieces)

    table = build_table(low + own_block + high, ordered(w_parent, 0), groups)
    params = (
        jnp.concatenate([ordered(w_fine, 0), ordered(w_node_fine, 0)], axis=1),
        w_edge_out,
        w_node_agg,
        ordered(w_node_out, 1).T,
        jnp.concatenate([edge_bias, node_bias])[None],
        ordered(norm_gain, 0)[:, None],
        ordered(norm_bias, 0)[:, None],
    )
    slots = 2 * lax.dynamic_slice_in_dim(parents, first_row, per_device, 1)
    weights = lax.dynamic_slice_in_dim(interp_weights, first_row, per_device, 1)
    scales = jnp.pad(jnp.repeat(weights, 2, axis=1), ((0, 8 - weights.shape[0]), (0, 0)))
    result = fine_latent
    arrived = []
    for c in range(CHUNKS):
        start = c * length
        outs = update(
            live_rows - first_row - start,
            slots[:, start : start + length],
            chunk_pieces[c],
            table,
            scales[:, 2 * start : 2 * (start + length)],
            params,
        )
        result = lax.dynamic_update_slice_in_dim(result, outs[0], first_row + start, 1)
        for r in range(1, groups):
            arrived.append((turn(outs[r], -r), ((rank + r) % groups) * per_device + start))
    for part, at in arrived:
        result = lax.dynamic_update_slice_in_dim(result, part, at, 1)
    return result


def solution(mesh):
    in_specs = (P("feat", "dom"), P("feat", "dom"), P(None, "dom"), P(None, "dom"), P("dom")) + (P(),) * 10
    return jax.shard_map(shards, mesh=mesh, in_specs=in_specs, out_specs=P("feat", "dom"), check_vma=False)
```

```python
import functools

import jax
import jax.numpy as jnp
from jax import lax
from jax.experimental import pallas as pl
from jax.experimental.pallas import tpu as pltpu
from jax.sharding import PartitionSpec as P

F32 = jnp.float32
BF16 = jnp.bfloat16
PAD = 4
CHUNKS = 2
GROUPS = 16


def dot(a, b, ca, cb):
    return lax.dot_general(a, b, (((ca,), (cb,)), ((), ())), preferred_element_type=F32)


def table_kernel(count, step, *refs):
    pieces, (weight, table, landed, sems) = refs[:-4], refs[-4:]
    blocks = len(pieces) // count
    rows = pieces[0].shape[1]
    steps = rows // step
    flat = table.reshape(2 * table.shape[0], 128)
    flat[pl.ds(0, 2 * PAD), :] = jnp.zeros((2 * PAD, 128), F32)
    flat[pl.ds(2 * (PAD + blocks * rows), 2 * PAD), :] = jnp.zeros((2 * PAD, 128), F32)

    def copies(block, i, slot):
        at = pl.multiple_of(i * step, step)
        features = pieces[0].shape[0]
        return [
            pltpu.make_async_copy(
                pieces[block * count + p].at[:, pl.ds(at, step)],
                landed.at[block % 2, slot, pl.ds(p * features, features), :],
                sems.at[block % 2, slot, p],
            )
            for p in range(count)
        ]

    for copy in copies(0, 0, 0):
        copy.start()
    for block in range(blocks):
        if block + 1 < blocks:
            for copy in copies(block + 1, 0, 0):
                copy.start()

        def one(i, carry, block=block):
            slot = lax.rem(i, 2)

            @pl.when(i + 1 < steps)
            def _():
                for copy in copies(block, i + 1, 1 - slot):
                    copy.start()

            for copy in copies(block, i, slot):
                copy.wait()
            projected = dot(landed[block % 2, slot], weight[...], 0, 0)
            base = pl.multiple_of(2 * (PAD + block * rows + i * step), 8)
            flat[pl.ds(base, step, stride=2), :] = projected[:, :128]
            flat[pl.ds(base + 1, step, stride=2), :] = projected[:, 128:]
            return carry

        lax.fori_loop(0, steps, one, 0)


def update_kernel(count, step, live, slots, *refs):
    pieces = refs[:count]
    table, scales, w_latent, w_edge, w_agg, w_out_t, bias, gain, shift = refs[count : count + 9]
    outs = refs[count + 9 : 2 * count + 9]
    fine, total, spread_out, scale_rows = refs[2 * count + 9 :]
    parents = slots.shape[0]
    nodes = pieces[0].shape[1]
    sublane = lax.broadcasted_iota(jnp.int32, (8, 128), 0)
    owns = [sublane >= 2 * j for j in range(4)]

    def one_step(i, carry):
        at = pl.multiple_of(i * step, step)
        latent = jnp.concatenate([piece[:, pl.ds(at, step)] for piece in pieces], axis=0)
        first = dot(latent, w_latent[...], 0, 0) + bias[...]
        width = first.shape[1] // 2
        scale_rows[...] = scales[:, pl.ds(pl.multiple_of(2 * at, 2 * step), 2 * step)].T
        fine[pl.ds(0, step, stride=2), :] = first[:, :128]
        fine[pl.ds(1, step, stride=2), :] = first[:, 128:width]
        spread_out[...] = first[:, width:]

        def group(g):
            base = pl.multiple_of(g * 8, 8)
            node = at + g * 4
            part = fine[pl.ds(base, 8), :]
            scale = scale_rows[pl.ds(base, 8), :]
            acc = None
            for k in range(parents):
                rows = None
                for j in range(4):
                    loaded = table.at[pl.ds(slots[k, node + j] + (PAD - j), 4)].reshape(8, 128)[...]
                    rows = loaded if rows is None else jnp.where(owns[j], loaded, rows)
                hidden = jnp.maximum(part + rows, 0.0) * scale[:, k : k + 1]
                acc = hidden if acc is None else acc + hidden
            return acc

        def some_groups(b, inner):
            sums = [group(b * GROUPS + u) for u in range(GROUPS)]
            total[pl.ds(pl.multiple_of(b * GROUPS * 8, 8), GROUPS * 8), :] = jnp.concatenate(sums, axis=0)
            return inner

        lax.fori_loop(0, step // (4 * GROUPS), some_groups, 0)
        summed = jnp.concatenate(
            [total[pl.ds(0, step, stride=2), :], total[pl.ds(1, step, stride=2), :]], axis=1
        ).astype(BF16)
        aggregate = dot(summed, w_edge[...], 1, 0).astype(BF16)
        node_hidden = jnp.maximum(spread_out[...] + dot(aggregate, w_agg[...], 1, 0), 0.0).astype(BF16)
        output = dot(w_out_t[...], node_hidden, 1, 1)
        centered = output - jnp.mean(output, axis=0, keepdims=True)
        spread = jnp.mean(centered * centered, axis=0, keepdims=True)
        normed = centered * lax.rsqrt(spread + 1e-05) * gain[...] + shift[...]
        column = at + lax.broadcasted_iota(jnp.int32, (1, step), 1)
        moved = jnp.where(column < live[0], normed, 0.0)
        result = (latent.astype(F32) + moved).astype(BF16)
        part_rows = result.shape[0] // count
        for r in range(count):
            outs[r][:, pl.ds(at, step)] = result[r * part_rows : (r + 1) * part_rows]
        return carry

    lax.fori_loop(0, nodes // step, one_step, 0)


def build_table(pieces, weight, count):
    rows = pieces[0].shape[1] * len(pieces) // count
    step = min(2048, pieces[0].shape[1])
    vmem = pl.BlockSpec(memory_space=pltpu.VMEM)
    return pl.pallas_call(
        functools.partial(table_kernel, count, step),
        out_shape=jax.ShapeDtypeStruct((rows + 2 * PAD, 2, 128), F32),
        in_specs=[pl.BlockSpec(memory_space=pl.ANY)] * len(pieces) + [vmem],
        out_specs=vmem,
        scratch_shapes=[
            pltpu.VMEM((2, 2, weight.shape[0], step), BF16),
            pltpu.SemaphoreType.DMA((2, 2, count)),
        ],
        compiler_params=pltpu.CompilerParams(vmem_limit_bytes=10 << 20),
        cost_estimate=pl.CostEstimate(flops=2 * rows * 65536, bytes_accessed=rows * 1536, transcendentals=0),
    )(*pieces, weight)


def update(live, slots, pieces, table, scales, params):
    count, nodes = len(pieces), pieces[0].shape[1]
    step = min(512, nodes)
    vmem = pl.BlockSpec(memory_space=pltpu.VMEM)
    smem = pl.BlockSpec(memory_space=pltpu.SMEM)
    return pl.pallas_call(
        functools.partial(update_kernel, count, step),
        out_shape=[jax.ShapeDtypeStruct(piece.shape, BF16) for piece in pieces],
        in_specs=[smem] * 2 + [vmem] * (count + 2 + len(params)),
        out_specs=[vmem] * count,
        scratch_shapes=[
            pltpu.VMEM((2 * step, 128), F32),
            pltpu.VMEM((2 * step, 128), F32),
            pltpu.VMEM((step, 256), F32),
            pltpu.VMEM((2 * step, 8), F32),
        ],
        compiler_params=pltpu.CompilerParams(vmem_limit_bytes=10 << 20),
        cost_estimate=pl.CostEstimate(flops=nodes * 700000, bytes_accessed=nodes * 2048, transcendentals=nodes),
    )(live, slots, *pieces, table, scales, *params)


def shards(
    fine_latent,
    coarse_latent,
    parents,
    interp_weights,
    live_rows,
    w_fine,
    w_parent,
    w_edge_out,
    w_node_fine,
    w_node_agg,
    w_node_out,
    edge_bias,
    node_bias,
    norm_gain,
    norm_bias,
):
    groups, domains = lax.axis_size("feat"), lax.axis_size("dom")
    rank = lax.axis_index("feat")
    own_features = fine_latent.shape[0]
    per_device = fine_latent.shape[1] // groups
    length = per_device // CHUNKS
    forward = [(i, i + 1) for i in range(domains - 1)]
    backward = [(i + 1, i) for i in range(domains - 1)]

    def turn(value, r):
        return lax.ppermute(value, "feat", [(i, (i + r) % groups) for i in range(groups)])

    owners = [(rank - r) % groups for r in range(groups)]
    own_block = [coarse_latent] + [turn(coarse_latent, r) for r in range(1, groups)]
    low = [lax.ppermute(piece, "dom", forward) for piece in own_block]
    high = [lax.ppermute(piece, "dom", backward) for piece in own_block]

    def ordered(weight, axis):
        parts = [lax.dynamic_slice_in_dim(weight, o * own_features, own_features, axis) for o in owners]
        return jnp.concatenate(parts, axis=axis)

    first_row = rank * per_device
    chunk_pieces = []
    for c in range(CHUNKS):
        pieces = [lax.dynamic_slice_in_dim(fine_latent, first_row + c * length, length, 1)]
        for r in range(1, groups):
            at = ((rank + r) % groups) * per_device + c * length
            part = lax.dynamic_slice_in_dim(fine_latent, at, length, 1)
            part, _ = lax.optimization_barrier((part, own_block[-1]))
            pieces.append(turn(part, r))
        chunk_pieces.append(pieces)

    table = build_table(low + own_block + high, ordered(w_parent, 0), groups)
    params = (
        jnp.concatenate([ordered(w_fine, 0), ordered(w_node_fine, 0)], axis=1),
        w_edge_out,
        w_node_agg,
        ordered(w_node_out, 1).T,
        jnp.concatenate([edge_bias, node_bias])[None],
        ordered(norm_gain, 0)[:, None],
        ordered(norm_bias, 0)[:, None],
    )
    slots = lax.dynamic_slice_in_dim(parents, first_row, per_device, 1)
    weights = lax.dynamic_slice_in_dim(interp_weights, first_row, per_device, 1)
    scales = jnp.pad(jnp.repeat(weights, 2, axis=1), ((0, 8 - weights.shape[0]), (0, 0)))
    result = fine_latent
    arrived = []
    for c in range(CHUNKS):
        start = c * length
        outs = update(
            live_rows - first_row - start,
            slots[:, start : start + length],
            chunk_pieces[c],
            table,
            scales[:, 2 * start : 2 * (start + length)],
            params,
        )
        result = lax.dynamic_update_slice_in_dim(result, outs[0], first_row + start, 1)
        for r in range(1, groups):
            arrived.append((turn(outs[r], -r), ((rank + r) % groups) * per_device + start))
    for part, at in arrived:
        result = lax.dynamic_update_slice_in_dim(result, part, at, 1)
    return result


def solution(mesh):
    in_specs = (P("feat", "dom"), P("feat", "dom"), P(None, "dom"), P(None, "dom"), P("dom")) + (P(),) * 10
    return jax.shard_map(shards, mesh=mesh, in_specs=in_specs, out_specs=P("feat", "dom"), check_vma=False)
```

```python
import functools

import jax
import jax.numpy as jnp
from jax import lax
from jax.experimental import pallas as pl
from jax.experimental.pallas import tpu as pltpu
from jax.sharding import PartitionSpec as P

F32 = jnp.float32
BF16 = jnp.bfloat16
PAD = 8
CHUNKS = 2
GROUPS = 16


def dot(a, b, ca, cb):
    return lax.dot_general(a, b, (((ca,), (cb,)), ((), ())), preferred_element_type=F32)


def table_kernel(count, step, *refs):
    pieces, (weight, table, landed, sems) = refs[:-4], refs[-4:]
    blocks = len(pieces) // count
    rows = pieces[0].shape[1]
    steps = rows // step
    table[pl.ds(0, PAD), :] = jnp.zeros((PAD, 128), F32)
    table[pl.ds(PAD + 2 * blocks * rows, PAD), :] = jnp.zeros((PAD, 128), F32)

    def copies(block, i, slot):
        at = pl.multiple_of(i * step, step)
        features = pieces[0].shape[0]
        return [
            pltpu.make_async_copy(
                pieces[block * count + p].at[:, pl.ds(at, step)],
                landed.at[block % 2, slot, pl.ds(p * features, features), :],
                sems.at[block % 2, slot, p],
            )
            for p in range(count)
        ]

    for copy in copies(0, 0, 0):
        copy.start()
    for block in range(blocks):
        if block + 1 < blocks:
            for copy in copies(block + 1, 0, 0):
                copy.start()

        def one(i, carry, block=block):
            slot = lax.rem(i, 2)

            @pl.when(i + 1 < steps)
            def _():
                for copy in copies(block, i + 1, 1 - slot):
                    copy.start()

            for copy in copies(block, i, slot):
                copy.wait()
            projected = dot(landed[block % 2, slot], weight[...], 0, 0)
            base = pl.multiple_of(PAD + 2 * (block * rows + i * step), 8)
            table[pl.ds(base, step, stride=2), :] = projected[:, :128]
            table[pl.ds(base + 1, step, stride=2), :] = projected[:, 128:]
            return carry

        lax.fori_loop(0, steps, one, 0)


def update_kernel(count, step, live, slots, *refs):
    pieces = refs[:count]
    table, scales, w_latent, w_edge, w_agg, w_out_t, bias, gain, shift = refs[count : count + 9]
    outs = refs[count + 9 : 2 * count + 9]
    fine, total, spread_out, scale_rows = refs[2 * count + 9 :]
    nodes = pieces[0].shape[1]
    parents = slots.shape[0] // nodes
    sublane = lax.broadcasted_iota(jnp.int32, (8, 128), 0)
    owns = [sublane >= 2 * j for j in range(4)]

    def one_step(i, carry):
        at = pl.multiple_of(i * step, step)
        latent = jnp.concatenate([piece[:, pl.ds(at, step)] for piece in pieces], axis=0)
        first = dot(latent, w_latent[...], 0, 0) + bias[...]
        width = first.shape[1] // 2
        scale_rows[...] = scales[:, pl.ds(pl.multiple_of(2 * at, 2 * step), 2 * step)].T
        fine[pl.ds(0, step, stride=2), :] = first[:, :128]
        fine[pl.ds(1, step, stride=2), :] = first[:, 128:width]
        spread_out[...] = first[:, width:]

        def group(g):
            base = pl.multiple_of(g * 8, 8)
            node = at + g * 4
            part = fine[pl.ds(base, 8), :]
            scale = scale_rows[pl.ds(base, 8), :]
            acc = None
            for k in range(parents):
                rows = None
                for j in range(4):
                    loaded = table[pl.ds(slots[node + (k * nodes + j)] + (PAD - 2 * j), 8), :]
                    rows = loaded if rows is None else jnp.where(owns[j], loaded, rows)
                hidden = jnp.maximum(part + rows, 0.0) * scale[:, k : k + 1]
                acc = hidden if acc is None else acc + hidden
            return acc

        def some_groups(b, inner):
            sums = [group(b * GROUPS + u) for u in range(GROUPS)]
            total[pl.ds(pl.multiple_of(b * GROUPS * 8, 8), GROUPS * 8), :] = jnp.concatenate(sums, axis=0)
            return inner

        lax.fori_loop(0, step // (4 * GROUPS), some_groups, 0)
        summed = jnp.concatenate(
            [total[pl.ds(0, step, stride=2), :], total[pl.ds(1, step, stride=2), :]], axis=1
        ).astype(BF16)
        aggregate = dot(summed, w_edge[...], 1, 0).astype(BF16)
        node_hidden = jnp.maximum(spread_out[...] + dot(aggregate, w_agg[...], 1, 0), 0.0).astype(BF16)
        output = dot(w_out_t[...], node_hidden, 1, 1)
        centered = output - jnp.mean(output, axis=0, keepdims=True)
        spread = jnp.mean(centered * centered, axis=0, keepdims=True)
        normed = centered * lax.rsqrt(spread + 1e-05) * gain[...] + shift[...]
        column = at + lax.broadcasted_iota(jnp.int32, (1, step), 1)
        moved = jnp.where(column < live[0], normed, 0.0)
        result = (latent.astype(F32) + moved).astype(BF16)
        part_rows = result.shape[0] // count
        for r in range(count):
            outs[r][:, pl.ds(at, step)] = result[r * part_rows : (r + 1) * part_rows]
        return carry

    lax.fori_loop(0, nodes // step, one_step, 0)


def build_table(pieces, weight, count):
    rows = pieces[0].shape[1] * len(pieces) // count
    step = min(2048, pieces[0].shape[1])
    vmem = pl.BlockSpec(memory_space=pltpu.VMEM)
    return pl.pallas_call(
        functools.partial(table_kernel, count, step),
        out_shape=jax.ShapeDtypeStruct((2 * rows + 2 * PAD, 128), F32),
        in_specs=[pl.BlockSpec(memory_space=pl.ANY)] * len(pieces) + [vmem],
        out_specs=vmem,
        scratch_shapes=[
            pltpu.VMEM((2, 2, weight.shape[0], step), BF16),
            pltpu.SemaphoreType.DMA((2, 2, count)),
        ],
        compiler_params=pltpu.CompilerParams(vmem_limit_bytes=10 << 20),
        cost_estimate=pl.CostEstimate(flops=2 * rows * 65536, bytes_accessed=rows * 1536, transcendentals=0),
    )(*pieces, weight)


def update(live, slots, pieces, table, scales, params):
    count, nodes = len(pieces), pieces[0].shape[1]
    step = min(512, nodes)
    vmem = pl.BlockSpec(memory_space=pltpu.VMEM)
    smem = pl.BlockSpec(memory_space=pltpu.SMEM)
    return pl.pallas_call(
        functools.partial(update_kernel, count, step),
        out_shape=[jax.ShapeDtypeStruct(piece.shape, BF16) for piece in pieces],
        in_specs=[smem] * 2 + [vmem] * (count + 2 + len(params)),
        out_specs=[vmem] * count,
        scratch_shapes=[
            pltpu.VMEM((2 * step, 128), F32),
            pltpu.VMEM((2 * step, 128), F32),
            pltpu.VMEM((step, 256), F32),
            pltpu.VMEM((2 * step, 8), F32),
        ],
        compiler_params=pltpu.CompilerParams(vmem_limit_bytes=10 << 20),
        cost_estimate=pl.CostEstimate(flops=nodes * 700000, bytes_accessed=nodes * 2048, transcendentals=nodes),
    )(live, slots, *pieces, table, scales, *params)


def shards(
    fine_latent,
    coarse_latent,
    parents,
    interp_weights,
    live_rows,
    w_fine,
    w_parent,
    w_edge_out,
    w_node_fine,
    w_node_agg,
    w_node_out,
    edge_bias,
    node_bias,
    norm_gain,
    norm_bias,
):
    groups, domains = lax.axis_size("feat"), lax.axis_size("dom")
    rank = lax.axis_index("feat")
    own_features = fine_latent.shape[0]
    per_device = fine_latent.shape[1] // groups
    length = per_device // CHUNKS
    forward = [(i, i + 1) for i in range(domains - 1)]
    backward = [(i + 1, i) for i in range(domains - 1)]

    def turn(value, r):
        return lax.ppermute(value, "feat", [(i, (i + r) % groups) for i in range(groups)])

    owners = [(rank - r) % groups for r in range(groups)]
    own_block = [coarse_latent] + [turn(coarse_latent, r) for r in range(1, groups)]
    low = [lax.ppermute(piece, "dom", forward) for piece in own_block]
    high = [lax.ppermute(piece, "dom", backward) for piece in own_block]

    def ordered(weight, axis):
        parts = [lax.dynamic_slice_in_dim(weight, o * own_features, own_features, axis) for o in owners]
        return jnp.concatenate(parts, axis=axis)

    first_row = rank * per_device
    chunk_pieces = []
    for c in range(CHUNKS):
        pieces = [lax.dynamic_slice_in_dim(fine_latent, first_row + c * length, length, 1)]
        for r in range(1, groups):
            at = ((rank + r) % groups) * per_device + c * length
            part = lax.dynamic_slice_in_dim(fine_latent, at, length, 1)
            part, _ = lax.optimization_barrier((part, own_block[-1]))
            pieces.append(turn(part, r))
        chunk_pieces.append(pieces)

    table = build_table(low + own_block + high, ordered(w_parent, 0), groups)
    params = (
        jnp.concatenate([ordered(w_fine, 0), ordered(w_node_fine, 0)], axis=1),
        w_edge_out,
        w_node_agg,
        ordered(w_node_out, 1).T,
        jnp.concatenate([edge_bias, node_bias])[None],
        ordered(norm_gain, 0)[:, None],
        ordered(norm_bias, 0)[:, None],
    )
    slots = 2 * lax.dynamic_slice_in_dim(parents, first_row, per_device, 1)
    weights = lax.dynamic_slice_in_dim(interp_weights, first_row, per_device, 1)
    scales = jnp.pad(jnp.repeat(weights, 2, axis=1), ((0, 8 - weights.shape[0]), (0, 0)))
    result = fine_latent
    arrived = []
    for c in range(CHUNKS):
        start = c * length
        outs = update(
            live_rows - first_row - start,
            slots[:, start : start + length].reshape(-1),
            chunk_pieces[c],
            table,
            scales[:, 2 * start : 2 * (start + length)],
            params,
        )
        result = lax.dynamic_update_slice_in_dim(result, outs[0], first_row + start, 1)
        for r in range(1, groups):
            arrived.append((turn(outs[r], -r), ((rank + r) % groups) * per_device + start))
    for part, at in arrived:
        result = lax.dynamic_update_slice_in_dim(result, part, at, 1)
    return result


def solution(mesh):
    in_specs = (P("feat", "dom"), P("feat", "dom"), P(None, "dom"), P(None, "dom"), P("dom")) + (P(),) * 10
    return jax.shard_map(shards, mesh=mesh, in_specs=in_specs, out_specs=P("feat", "dom"), check_vma=False)
```

```python
import functools

import jax
import jax.numpy as jnp
from jax import lax
from jax.experimental import pallas as pl
from jax.experimental.pallas import tpu as pltpu
from jax.sharding import PartitionSpec as P

F32 = jnp.float32
BF16 = jnp.bfloat16
PAD = 8
CHUNKS = 2
GROUPS = 16
PARTS = 2


def dot(a, b, ca, cb):
    return lax.dot_general(a, b, (((ca,), (cb,)), ((), ())), preferred_element_type=F32)


def table_kernel(segments, step, places, *refs):
    weight, table, landed, sems = refs[-4:]
    rows = (table.shape[0] - 2 * PAD) // 6
    features = landed.shape[2] // sems.shape[2]
    table[pl.ds(0, PAD), :] = jnp.zeros((PAD, 128), F32)
    table[pl.ds(PAD + 6 * rows, PAD), :] = jnp.zeros((PAD, 128), F32)

    def copies(segment, i, slot, which):
        found = []
        for p, (sources, first) in enumerate(segments[segment][3]):
            at = pl.multiple_of(first + i * step, 128)
            found.append(
                pltpu.make_async_copy(
                    refs[sources[min(which, len(sources) - 1)]].at[:, pl.ds(at, step)],
                    landed.at[segment % 2, slot, pl.ds(p * features, features), :],
                    sems.at[segment % 2, slot, p],
                )
            )
        return found

    def start(segment, i, slot):
        if all(len(sources) == 1 for sources, _ in segments[segment][3]):
            for copy in copies(segment, i, slot, 0):
                copy.start()
            return
        for which in range(2):

            @pl.when(places[3] == which)
            def _(which=which):
                for copy in copies(segment, i, slot, which):
                    copy.start()

    start(0, 0, 0)
    for segment, (window, row, length, _) in enumerate(segments):
        steps = length // step
        if segment + 1 < len(segments):
            start(segment + 1, 0, 0)

        def one(i, carry, segment=segment, window=window, row=row, steps=steps):
            slot = lax.rem(i, 2)

            @pl.when(i + 1 < steps)
            def _():
                start(segment, i + 1, 1 - slot)

            for copy in copies(segment, i, slot, 0):
                copy.wait()
            projected = dot(landed[segment % 2, slot], weight[...], 0, 0)
            base = pl.multiple_of(PAD + 2 * (places[window] * rows + row + i * step), 8)
            table[pl.ds(base, step, stride=2), :] = projected[:, :128]
            table[pl.ds(base + 1, step, stride=2), :] = projected[:, 128:]
            return carry

        lax.fori_loop(0, steps, one, 0)


def build_table(places, segments, arrays, weight, rows, table=None):
    pieces = len(segments[0][3])
    step = min(2048, segments[0][2])
    vmem = pl.BlockSpec(memory_space=pltpu.VMEM)
    smem = pl.BlockSpec(memory_space=pltpu.SMEM)
    far = pl.BlockSpec(memory_space=pl.ANY)
    kernel = functools.partial(table_kernel, segments, step)
    operands, specs, aliases = [places, *arrays], [smem] + [far] * len(arrays), {}
    if table is not None:
        aliases = {len(operands): 0}
        operands, specs = operands + [table], specs + [vmem]
    made = sum(segment[2] for segment in segments)
    return pl.pallas_call(
        kernel,
        out_shape=jax.ShapeDtypeStruct((6 * rows + 2 * PAD, 128), F32),
        in_specs=specs + [vmem],
        out_specs=vmem,
        scratch_shapes=[
            pltpu.VMEM((2, 2, weight.shape[0], step), BF16),
            pltpu.SemaphoreType.DMA((2, 2, pieces)),
        ],
        input_output_aliases=aliases,
        compiler_params=pltpu.CompilerParams(vmem_limit_bytes=10 << 20),
        cost_estimate=pl.CostEstimate(flops=2 * made * 65536, bytes_accessed=made * 1536, transcendentals=0),
    )(*operands, weight)


def update_kernel(count, step, start, aux, *refs):
    pieces = refs[:count]
    table, scales, w_latent, w_edge, w_agg, w_out_t, bias, gain, shift = refs[count : count + 9]
    outs = refs[count + 9 : 2 * count + 9]
    fine, total, spread_out, scale_rows, slots, live, sems = refs[2 * count + 9 :]
    nodes = pieces[0].shape[1]
    parents = slots.shape[0] // nodes
    held = aux.shape[0] // (parents + 1)
    fetches = [
        pltpu.make_async_copy(aux.at[pl.ds(k * held + start, nodes)], slots.at[pl.ds(k * nodes, nodes)], sems.at[k])
        for k in range(parents)
    ]
    fetches.append(pltpu.make_async_copy(aux.at[pl.ds(parents * held, 1024)], live, sems.at[parents]))
    for fetch in fetches:
        fetch.start()
    for fetch in fetches:
        fetch.wait()
    sublane = lax.broadcasted_iota(jnp.int32, (8, 128), 0)
    owns = [sublane >= 2 * j for j in range(4)]

    def one_step(i, carry):
        at = pl.multiple_of(i * step, step)
        latent = jnp.concatenate([piece[:, pl.ds(at, step)] for piece in pieces], axis=0)
        first = dot(latent, w_latent[...], 0, 0) + bias[...]
        width = first.shape[1] // 2
        scale_columns = scales[:, pl.ds(pl.multiple_of(start + at, step), step)].T
        scale_rows[pl.ds(0, step, stride=2), :] = scale_columns
        scale_rows[pl.ds(1, step, stride=2), :] = scale_columns
        fine[pl.ds(0, step, stride=2), :] = first[:, :128]
        fine[pl.ds(1, step, stride=2), :] = first[:, 128:width]
        spread_out[...] = first[:, width:]

        def group(g):
            base = pl.multiple_of(g * 8, 8)
            node = at + g * 4
            part = fine[pl.ds(base, 8), :]
            scale = scale_rows[pl.ds(base, 8), :]
            acc = None
            for k in range(parents):
                rows = None
                for j in range(4):
                    loaded = table[pl.ds(slots[node + (k * nodes + j)], 8), :]
                    rows = loaded if rows is None else jnp.where(owns[j], loaded, rows)
                hidden = jnp.maximum(part + rows, 0.0) * scale[:, k : k + 1]
                acc = hidden if acc is None else acc + hidden
            return acc

        def some_groups(b, inner):
            sums = [group(b * GROUPS + u) for u in range(GROUPS)]
            total[pl.ds(pl.multiple_of(b * GROUPS * 8, 8), GROUPS * 8), :] = jnp.concatenate(sums, axis=0)
            return inner

        lax.fori_loop(0, step // (4 * GROUPS), some_groups, 0)
        summed = jnp.concatenate(
            [total[pl.ds(0, step, stride=2), :], total[pl.ds(1, step, stride=2), :]], axis=1
        ).astype(BF16)
        aggregate = dot(summed, w_edge[...], 1, 0).astype(BF16)
        node_hidden = jnp.maximum(spread_out[...] + dot(aggregate, w_agg[...], 1, 0), 0.0).astype(BF16)
        output = dot(w_out_t[...], node_hidden, 1, 1)
        centered = output - jnp.mean(output, axis=0, keepdims=True)
        spread = jnp.mean(centered * centered, axis=0, keepdims=True)
        normed = centered * lax.rsqrt(spread + 1e-05) * gain[...] + shift[...]
        column = start + at + lax.broadcasted_iota(jnp.int32, (1, step), 1)
        moved = jnp.where(column < live[0], normed, 0.0)
        result = (latent.astype(F32) + moved).astype(BF16)
        part_rows = result.shape[0] // count
        for r in range(count):
            outs[r][:, pl.ds(at, step)] = result[r * part_rows : (r + 1) * part_rows]
        return carry

    lax.fori_loop(0, nodes // step, one_step, 0)


def update(start, aux, pieces, table, scales, params):
    count, nodes = len(pieces), pieces[0].shape[1]
    parents = aux.shape[0] - 1
    step = min(512, nodes)
    vmem = pl.BlockSpec(memory_space=pltpu.VMEM)
    far = pl.BlockSpec(memory_space=pl.ANY)
    return pl.pallas_call(
        functools.partial(update_kernel, count, step, start),
        out_shape=[jax.ShapeDtypeStruct(piece.shape, BF16) for piece in pieces],
        in_specs=[far] + [vmem] * (count + 2 + len(params)),
        out_specs=[vmem] * count,
        scratch_shapes=[
            pltpu.VMEM((2 * step, 128), F32),
            pltpu.VMEM((2 * step, 128), F32),
            pltpu.VMEM((step, 256), F32),
            pltpu.VMEM((2 * step, 8), F32),
            pltpu.SMEM((parents * nodes,), jnp.int32),
            pltpu.SMEM((1024,), jnp.int32),
            pltpu.SemaphoreType.DMA((parents + 1,)),
        ],
        compiler_params=pltpu.CompilerParams(vmem_limit_bytes=10 << 20),
        cost_estimate=pl.CostEstimate(flops=nodes * 700000, bytes_accessed=nodes * 2048, transcendentals=nodes),
    )(aux.reshape(-1), *pieces, table, scales, *params)


def after(value, *others):
    return lax.optimization_barrier((value, *others))[0]


def cut(array, at, size):
    return lax.dynamic_slice_in_dim(array, at, size, 1)


def plain(fine_latent, coarse_latent, aux, weights, owners, w_parent, run):
    groups, domains = lax.axis_size("feat"), lax.axis_size("dom")
    rank = lax.axis_index("feat")
    per_device = fine_latent.shape[1] // groups
    length = per_device // CHUNKS
    forward = [(i, i + 1) for i in range(domains - 1)]
    backward = [(i + 1, i) for i in range(domains - 1)]

    def turn(value, r):
        return lax.ppermute(value, "feat", [(i, (i + r) % groups) for i in range(groups)])

    own = [coarse_latent] + [turn(coarse_latent, r) for r in range(1, groups)]
    low = [lax.ppermute(piece, "dom", forward) for piece in own]
    high = [lax.ppermute(piece, "dom", backward) for piece in own]
    first_row = rank * per_device
    rows = coarse_latent.shape[1]
    segments = [
        (w, 0, rows, [((w * groups + p,), 0) for p in range(groups)]) for w in range(3)
    ]
    table = build_table(jnp.arange(4, dtype=jnp.int32), segments, low + own + high, w_parent, rows)
    aux = cut(aux, first_row, per_device)
    aux = jnp.concatenate([aux[:-1], aux[-1:] - first_row])
    weights = cut(weights, first_row, per_device)
    result = fine_latent
    arrived = []
    for c in range(CHUNKS):
        start = c * length
        pieces = [cut(fine_latent, first_row + start, length)]
        for r in range(1, groups):
            part = cut(fine_latent, ((rank + r) % groups) * per_device + start, length)
            pieces.append(turn(after(part, own[-1]), r))
        outs = run(start, aux, pieces, table, weights)
        result = lax.dynamic_update_slice_in_dim(result, outs[0], first_row + start, 1)
        for r in range(1, groups):
            arrived.append((turn(outs[r], -r), ((rank + r) % groups) * per_device + start))
    for part, at in arrived:
        result = lax.dynamic_update_slice_in_dim(result, part, at, 1)
    return result


def paired(fine_latent, coarse_latent, aux, weights, owners, w_parent, run):
    domains = lax.axis_size("dom")
    side, rank = lax.axis_index("dom") % 2, lax.axis_index("feat")
    matched = side == rank
    pairs = range(domains // 2)

    def send(value, moves):
        perm = [((2 * c + a) * 2 + b, (2 * c + x) * 2 + y) for c in pairs for (a, b), (x, y) in moves]
        return lax.ppermute(value, ("dom", "feat"), perm)

    def swap_rank(value):
        return send(value, [((k, f), (k, 1 - f)) for k in range(2) for f in range(2)])

    def swap_side(value):
        return send(value, [((k, f), (1 - k, f)) for k in range(2) for f in range(2)])

    def halo(value):
        perm = [((2 * c - 1) * 2, (2 * c) * 2) for c in pairs if c > 0]
        perm += [((2 * c + 2) * 2 + 1, (2 * c + 1) * 2 + 1) for c in pairs if c + 1 < len(pairs)]
        return lax.ppermute(value, ("dom", "feat"), perm)

    def hand_over(value):
        return send(value, [((0, 0), (1, 0)), ((1, 1), (0, 1))])

    to_first = [((0, 0), (1, 0)), ((1, 1), (0, 1)), ((0, 1), (0, 0)), ((1, 0), (1, 1))]
    from_first = [(b, a) for a, b in to_first]
    to_second = [((0, 1), (1, 0)), ((1, 0), (0, 1))]

    rows = coarse_latent.shape[1]
    part = rows // PARTS
    parts = [lax.slice_in_dim(coarse_latent, i * part, (i + 1) * part, axis=1) for i in range(PARTS)]
    mate = []
    for piece in parts:
        mate.append(swap_rank(after(piece, mate[-1]) if mate else piece))
    halo_own = halo(coarse_latent)
    other = swap_side(coarse_latent)
    halo_mate = [halo(piece) for piece in mate]
    other_mate = [swap_side(piece) for piece in mate]
    passed_own = hand_over(halo_own)
    passed_mate = [hand_over(piece) for piece in halo_mate]

    near = [coarse_latent, other] + mate + other_mate
    near_segments = [
        (w, i * part, part, [((w,), i * part), ((2 + w * PARTS + i,), 0)]) for w in range(2) for i in range(PARTS)
    ]
    far = [halo_own, passed_own] + halo_mate + passed_mate
    far_segments = [
        (2, i * part, part, [((0, 1), i * part), ((2 + i, 2 + PARTS + i), 0)]) for i in range(PARTS)
    ]
    places = jnp.stack([side + 1 - rank, 2 - side - rank, 2 * rank, jnp.where(matched, 0, 1)]).astype(jnp.int32)

    half = fine_latent.shape[1] // 2
    length = half // CHUNKS
    mine = side * half
    chunks = []
    gate = mate[-1]
    for c in range(CHUNKS):
        start = c * length
        local = cut(fine_latent, mine + start, length)
        first = cut(fine_latent, jnp.where(matched, half - mine, mine) + start, length)
        second = cut(fine_latent, half - mine + start, length)
        first, second = send(after(first, gate), to_first), send(after(second, gate), to_second)
        gate = first
        chunks.append([jnp.where(matched, local, first), jnp.where(matched, first, second)])

    aux_local, aux_sent = cut(aux, mine, half), cut(aux, half - mine, half)
    aux = jnp.where(matched, aux_local, hand_over(aux_sent))
    aux = jnp.concatenate([aux[:-1], aux[-1:] - mine])
    weights = jnp.where(matched, cut(weights, mine, half), hand_over(cut(weights, half - mine, half)))

    table = build_table(places, near_segments, near, w_parent, rows)
    far_index = [
        (w, r, n, [(tuple(s), first) for s, first in sources]) for w, r, n, sources in far_segments
    ]
    table = build_table(places, far_index, far, w_parent, rows, table)

    result = jnp.zeros_like(after(fine_latent, gate))
    moved = []
    for c in range(CHUNKS):
        start = c * length
        own, mates = run(start, aux, chunks[c], table, weights)
        first = send(jnp.where(matched, mates, own), from_first)
        second = send(mates, to_second)
        moved.append((start, own, first, second))
    for start, own, first, second in moved:
        result = lax.dynamic_update_slice_in_dim(result, jnp.where(matched, own, first), mine + start, 1)
        result = lax.dynamic_update_slice_in_dim(
            result, jnp.where(matched, first, second), half - mine + start, 1
        )
    return result


def shards(
    fine_latent,
    coarse_latent,
    parents,
    interp_weights,
    live_rows,
    w_fine,
    w_parent,
    w_edge_out,
    w_node_fine,
    w_node_agg,
    w_node_out,
    edge_bias,
    node_bias,
    norm_gain,
    norm_bias,
):
    groups, domains = lax.axis_size("feat"), lax.axis_size("dom")
    rank = lax.axis_index("feat")
    own_features = fine_latent.shape[0]
    owners = [(rank - r) % groups for r in range(groups)]

    def ordered(weight, axis):
        parts = [lax.dynamic_slice_in_dim(weight, o * own_features, own_features, axis) for o in owners]
        return jnp.concatenate(parts, axis=axis)

    params = (
        jnp.concatenate([ordered(w_fine, 0), ordered(w_node_fine, 0)], axis=1),
        w_edge_out,
        w_node_agg,
        ordered(w_node_out, 1).T,
        jnp.concatenate([edge_bias, node_bias])[None],
        ordered(norm_gain, 0)[:, None],
        ordered(norm_bias, 0)[:, None],
    )

    def run(start, aux, pieces, table, weights):
        scales = jnp.pad(weights, ((0, 8 - weights.shape[0]), (0, 0)))
        return update(start, aux, pieces, table, scales, params)

    count = parents.shape[1]
    slots = 2 * parents + (PAD - 2 * (jnp.arange(count, dtype=jnp.int32) % 4))
    aux = jnp.concatenate([slots, jnp.broadcast_to(live_rows[:, None], (1, count))])
    plan = paired if groups == 2 and domains % 2 == 0 else plain
    return plan(fine_latent, coarse_latent, aux, interp_weights, owners, ordered(w_parent, 0), run)


def solution(mesh):
    in_specs = (P("feat", "dom"), P("feat", "dom"), P(None, "dom"), P(None, "dom"), P("dom")) + (P(),) * 10
    return jax.shard_map(shards, mesh=mesh, in_specs=in_specs, out_specs=P("feat", "dom"), check_vma=False)
```

```python
import functools

import jax
import jax.numpy as jnp
from jax import lax
from jax.experimental import pallas as pl
from jax.experimental.pallas import tpu as pltpu
from jax.sharding import PartitionSpec as P

F32 = jnp.float32
BF16 = jnp.bfloat16
PAD = 8
CHUNKS = 2
GROUPS = 16


def dot(a, b, ca, cb):
    return lax.dot_general(a, b, (((ca,), (cb,)), ((), ())), preferred_element_type=F32)


def fill_table(segments, step, places, refs, weight, table, landed, sems):
    rows = (table.shape[0] - 2 * PAD) // 6
    features = landed.shape[2] // sems.shape[2]
    table[pl.ds(0, PAD), :] = jnp.zeros((PAD, 128), F32)
    table[pl.ds(PAD + 6 * rows, PAD), :] = jnp.zeros((PAD, 128), F32)

    def copies(segment, i, slot, which):
        found = []
        for p, (sources, first) in enumerate(segments[segment][3]):
            at = pl.multiple_of(first + i * step, 128)
            found.append(
                pltpu.make_async_copy(
                    refs[sources[min(which, len(sources) - 1)]].at[:, pl.ds(at, step)],
                    landed.at[segment % 2, slot, pl.ds(p * features, features), :],
                    sems.at[segment % 2, slot, p],
                )
            )
        return found

    def start(segment, i, slot):
        if all(len(sources) == 1 for sources, _ in segments[segment][3]):
            for copy in copies(segment, i, slot, 0):
                copy.start()
            return
        for which in range(2):

            @pl.when(places[3] == which)
            def _(which=which):
                for copy in copies(segment, i, slot, which):
                    copy.start()

    start(0, 0, 0)
    for segment, (window, row, length, _) in enumerate(segments):
        steps = length // step
        if segment + 1 < len(segments):
            start(segment + 1, 0, 0)

        def one(i, carry, segment=segment, window=window, row=row, steps=steps):
            slot = lax.rem(i, 2)

            @pl.when(i + 1 < steps)
            def _():
                start(segment, i + 1, 1 - slot)

            for copy in copies(segment, i, slot, 0):
                copy.wait()
            projected = dot(landed[segment % 2, slot], weight[...], 0, 0)
            base = pl.multiple_of(PAD + 2 * (places[window] * rows + row + i * step), 8)
            table[pl.ds(base, step, stride=2), :] = projected[:, :128]
            table[pl.ds(base + 1, step, stride=2), :] = projected[:, 128:]
            return carry

        lax.fori_loop(0, steps, one, 0)


def update_kernel(count, step, start, segments, table_step, aux, *refs):
    pieces, refs = refs[:count], refs[count:]
    scales, w_latent, w_edge, w_agg, w_out_t, bias, gain, shift = refs[:8]
    fine, total, spread_out, scale_rows, slots, live, sems = refs[-7:]
    refs = refs[8:-7]
    if segments is None:
        table, outs = refs[0], refs[1:]
    else:
        places, w_parent, *coarse = refs[: -count - 3]
        *outs, table, landed, landed_sems = refs[-count - 3 :]
    nodes = pieces[0].shape[1]
    parents = slots.shape[0] // nodes
    held = aux.shape[0] // (parents + 1)
    fetches = [
        pltpu.make_async_copy(aux.at[pl.ds(k * held + start, nodes)], slots.at[pl.ds(k * nodes, nodes)], sems.at[k])
        for k in range(parents)
    ]
    fetches.append(pltpu.make_async_copy(aux.at[pl.ds(parents * held, 1024)], live, sems.at[parents]))
    for fetch in fetches:
        fetch.start()
    if segments is not None:
        fill_table(segments, table_step, places, coarse, w_parent, table, landed, landed_sems)
    for fetch in fetches:
        fetch.wait()
    sublane = lax.broadcasted_iota(jnp.int32, (8, 128), 0)
    owns = [sublane >= 2 * j for j in range(4)]

    def one_step(i, carry):
        at = pl.multiple_of(i * step, step)
        latent = jnp.concatenate([piece[:, pl.ds(at, step)] for piece in pieces], axis=0)
        first = dot(latent, w_latent[...], 0, 0) + bias[...]
        width = first.shape[1] // 2
        scale_columns = scales[:, pl.ds(pl.multiple_of(start + at, step), step)].T
        scale_rows[pl.ds(0, step, stride=2), :] = scale_columns
        scale_rows[pl.ds(1, step, stride=2), :] = scale_columns
        fine[pl.ds(0, step, stride=2), :] = first[:, :128]
        fine[pl.ds(1, step, stride=2), :] = first[:, 128:width]
        spread_out[...] = first[:, width:]

        def group(g):
            base = pl.multiple_of(g * 8, 8)
            node = at + g * 4
            part = fine[pl.ds(base, 8), :]
            scale = scale_rows[pl.ds(base, 8), :]
            acc = None
            for k in range(parents):
                rows = None
                for j in range(4):
                    loaded = table[pl.ds(slots[node + (k * nodes + j)], 8), :]
                    rows = loaded if rows is None else jnp.where(owns[j], loaded, rows)
                hidden = jnp.maximum(part + rows, 0.0) * scale[:, k : k + 1]
                acc = hidden if acc is None else acc + hidden
            return acc

        def some_groups(b, inner):
            sums = [group(b * GROUPS + u) for u in range(GROUPS)]
            total[pl.ds(pl.multiple_of(b * GROUPS * 8, 8), GROUPS * 8), :] = jnp.concatenate(sums, axis=0)
            return inner

        lax.fori_loop(0, step // (4 * GROUPS), some_groups, 0)
        summed = jnp.concatenate(
            [total[pl.ds(0, step, stride=2), :], total[pl.ds(1, step, stride=2), :]], axis=1
        ).astype(BF16)
        aggregate = dot(summed, w_edge[...], 1, 0).astype(BF16)
        node_hidden = jnp.maximum(spread_out[...] + dot(aggregate, w_agg[...], 1, 0), 0.0).astype(BF16)
        output = dot(w_out_t[...], node_hidden, 1, 1)
        centered = output - jnp.mean(output, axis=0, keepdims=True)
        spread = jnp.mean(centered * centered, axis=0, keepdims=True)
        normed = centered * lax.rsqrt(spread + 1e-05) * gain[...] + shift[...]
        column = start + at + lax.broadcasted_iota(jnp.int32, (1, step), 1)
        moved = jnp.where(column < live[0], normed, 0.0)
        result = (latent.astype(F32) + moved).astype(BF16)
        part_rows = result.shape[0] // count
        for r in range(count):
            outs[r][:, pl.ds(at, step)] = result[r * part_rows : (r + 1) * part_rows]
        return carry

    lax.fori_loop(0, nodes // step, one_step, 0)


def update(start, aux, pieces, scales, params, table=None, segments=None, places=None, w_parent=None, coarse=()):
    count, nodes = len(pieces), pieces[0].shape[1]
    parents = aux.shape[0] - 1
    step = min(512, nodes)
    vmem = pl.BlockSpec(memory_space=pltpu.VMEM)
    smem = pl.BlockSpec(memory_space=pltpu.SMEM)
    far = pl.BlockSpec(memory_space=pl.ANY)
    out_shape = [jax.ShapeDtypeStruct(piece.shape, BF16) for piece in pieces]
    operands = [aux.reshape(-1), *pieces, scales, *params]
    specs = [far] + [vmem] * (len(operands) - 1)
    scratch, table_step = [], 0
    if segments is None:
        operands, specs = operands + [table], specs + [vmem]
    else:
        operands, specs = operands + [places, w_parent, *coarse], specs + [smem, vmem] + [far] * len(coarse)
        rows = sum(segment[2] for segment in segments)
        table_step = min(2048, segments[0][2])
        out_shape.append(jax.ShapeDtypeStruct((2 * rows + 2 * PAD, 128), F32))
        scratch = [
            pltpu.VMEM((2, 2, w_parent.shape[0], table_step), BF16),
            pltpu.SemaphoreType.DMA((2, 2, len(segments[0][3]))),
        ]
    return pl.pallas_call(
        functools.partial(update_kernel, count, step, start, segments, table_step),
        out_shape=out_shape,
        in_specs=specs,
        out_specs=[vmem] * len(out_shape),
        scratch_shapes=scratch
        + [
            pltpu.VMEM((2 * step, 128), F32),
            pltpu.VMEM((2 * step, 128), F32),
            pltpu.VMEM((step, 256), F32),
            pltpu.VMEM((2 * step, 8), F32),
            pltpu.SMEM((parents * nodes,), jnp.int32),
            pltpu.SMEM((1024,), jnp.int32),
            pltpu.SemaphoreType.DMA((parents + 1,)),
        ],
        compiler_params=pltpu.CompilerParams(vmem_limit_bytes=8 << 20),
        cost_estimate=pl.CostEstimate(flops=nodes * 700000, bytes_accessed=nodes * 2048, transcendentals=nodes),
    )(*operands)


def after(value, *others):
    return lax.optimization_barrier((value, *others))[0]


def cut(array, at, size):
    return lax.dynamic_slice_in_dim(array, at, size, 1)


def plain(fine_latent, coarse_latent, aux, weights, owners, w_parent, run):
    groups, domains = lax.axis_size("feat"), lax.axis_size("dom")
    rank = lax.axis_index("feat")
    per_device = fine_latent.shape[1] // groups
    length = per_device // CHUNKS
    forward = [(i, i + 1) for i in range(domains - 1)]
    backward = [(i + 1, i) for i in range(domains - 1)]

    def turn(value, r):
        return lax.ppermute(value, "feat", [(i, (i + r) % groups) for i in range(groups)])

    own = [coarse_latent] + [turn(coarse_latent, r) for r in range(1, groups)]
    low = [lax.ppermute(piece, "dom", forward) for piece in own]
    high = [lax.ppermute(piece, "dom", backward) for piece in own]
    first_row = rank * per_device
    rows = coarse_latent.shape[1]
    segments = [
        (w, 0, rows, [((w * groups + p,), 0) for p in range(groups)]) for w in range(3)
    ]
    sources = dict(
        segments=segments, places=jnp.arange(4, dtype=jnp.int32), w_parent=w_parent, coarse=low + own + high
    )
    aux = cut(aux, first_row, per_device)
    aux = jnp.concatenate([aux[:-1], aux[-1:] - first_row])
    weights = cut(weights, first_row, per_device)
    result = fine_latent
    arrived = []
    for c in range(CHUNKS):
        start = c * length
        pieces = [cut(fine_latent, first_row + start, length)]
        for r in range(1, groups):
            part = cut(fine_latent, ((rank + r) % groups) * per_device + start, length)
            pieces.append(turn(after(part, own[-1]), r))
        outs = run(start, aux, pieces, weights, **(sources if c == 0 else dict(table=table)))
        table = outs[-1] if c == 0 else table
        result = lax.dynamic_update_slice_in_dim(result, outs[0], first_row + start, 1)
        for r in range(1, groups):
            arrived.append((turn(outs[r], -r), ((rank + r) % groups) * per_device + start))
    for part, at in arrived:
        result = lax.dynamic_update_slice_in_dim(result, part, at, 1)
    return result


def paired(fine_latent, coarse_latent, aux, weights, owners, w_parent, run):
    domains = lax.axis_size("dom")
    side, rank = lax.axis_index("dom") % 2, lax.axis_index("feat")
    matched = side == rank
    pairs = range(domains // 2)

    def send(value, moves):
        perm = [((2 * c + a) * 2 + b, (2 * c + x) * 2 + y) for c in pairs for (a, b), (x, y) in moves]
        return lax.ppermute(value, ("dom", "feat"), perm)

    def swap_rank(value):
        return send(value, [((k, f), (k, 1 - f)) for k in range(2) for f in range(2)])

    def swap_side(value):
        return send(value, [((k, f), (1 - k, f)) for k in range(2) for f in range(2)])

    def halo(value):
        perm = [((2 * c - 1) * 2, (2 * c) * 2) for c in pairs if c > 0]
        perm += [((2 * c + 2) * 2 + 1, (2 * c + 1) * 2 + 1) for c in pairs if c + 1 < len(pairs)]
        return lax.ppermute(value, ("dom", "feat"), perm)

    def hand_over(value):
        return send(value, [((0, 0), (1, 0)), ((1, 1), (0, 1))])

    to_first = [((0, 0), (1, 0)), ((1, 1), (0, 1)), ((0, 1), (0, 0)), ((1, 0), (1, 1))]
    from_first = [(b, a) for a, b in to_first]
    to_second = [((0, 1), (1, 0)), ((1, 0), (0, 1))]

    rows = coarse_latent.shape[1]
    mate = swap_rank(coarse_latent)
    halo_own, other = halo(coarse_latent), swap_side(coarse_latent)
    halo_mate, other_mate = halo(mate), swap_side(mate)
    passed_own, passed_mate = hand_over(halo_own), hand_over(halo_mate)
    coarse = [coarse_latent, mate, other, other_mate, halo_own, passed_own, halo_mate, passed_mate]
    segments = [
        (0, 0, rows, [((0,), 0), ((1,), 0)]),
        (1, 0, rows, [((2,), 0), ((3,), 0)]),
        (2, 0, rows, [((4, 5), 0), ((6, 7), 0)]),
    ]
    places = jnp.stack([side + 1 - rank, 2 - side - rank, 2 * rank, jnp.where(matched, 0, 1)]).astype(jnp.int32)

    half = fine_latent.shape[1] // 2
    length = half // CHUNKS
    mine = side * half
    chunks = []
    for c in range(CHUNKS):
        start = c * length
        local = cut(fine_latent, mine + start, length)
        first = cut(fine_latent, jnp.where(matched, half - mine, mine) + start, length)
        second = cut(fine_latent, half - mine + start, length)
        first, second = send(after(first, mate), to_first), send(after(second, mate), to_second)
        chunks.append([jnp.where(matched, local, first), jnp.where(matched, first, second)])

    aux_local, aux_sent = cut(aux, mine, half), cut(aux, half - mine, half)
    aux = jnp.where(matched, aux_local, hand_over(aux_sent))
    aux = jnp.concatenate([aux[:-1], aux[-1:] - mine])
    weights = jnp.where(matched, cut(weights, mine, half), hand_over(cut(weights, half - mine, half)))

    sources = dict(segments=segments, places=places, w_parent=w_parent, coarse=coarse)
    result = jnp.zeros_like(fine_latent)
    moved = []
    for c in range(CHUNKS):
        start = c * length
        own, mates, *made = run(start, aux, chunks[c], weights, **(sources if c == 0 else dict(table=table)))
        table = made[0] if made else table
        first = send(jnp.where(matched, mates, own), from_first)
        second = send(mates, to_second)
        moved.append((start, own, first, second))
    for start, own, first, second in moved:
        result = lax.dynamic_update_slice_in_dim(result, jnp.where(matched, own, first), mine + start, 1)
        result = lax.dynamic_update_slice_in_dim(
            result, jnp.where(matched, first, second), half - mine + start, 1
        )
    return result


def shards(
    fine_latent,
    coarse_latent,
    parents,
    interp_weights,
    live_rows,
    w_fine,
    w_parent,
    w_edge_out,
    w_node_fine,
    w_node_agg,
    w_node_out,
    edge_bias,
    node_bias,
    norm_gain,
    norm_bias,
):
    groups, domains = lax.axis_size("feat"), lax.axis_size("dom")
    rank = lax.axis_index("feat")
    own_features = fine_latent.shape[0]
    owners = [(rank - r) % groups for r in range(groups)]

    def ordered(weight, axis):
        parts = [lax.dynamic_slice_in_dim(weight, o * own_features, own_features, axis) for o in owners]
        return jnp.concatenate(parts, axis=axis)

    params = (
        jnp.concatenate([ordered(w_fine, 0), ordered(w_node_fine, 0)], axis=1),
        w_edge_out,
        w_node_agg,
        ordered(w_node_out, 1).T,
        jnp.concatenate([edge_bias, node_bias])[None],
        ordered(norm_gain, 0)[:, None],
        ordered(norm_bias, 0)[:, None],
    )

    def run(start, aux, pieces, weights, **table):
        scales = jnp.pad(weights, ((0, 8 - weights.shape[0]), (0, 0)))
        return update(start, aux, pieces, scales, params, **table)

    count = parents.shape[1]
    slots = 2 * parents + (PAD - 2 * (jnp.arange(count, dtype=jnp.int32) % 4))
    aux = jnp.concatenate([slots, jnp.broadcast_to(live_rows[:, None], (1, count))])
    plan = paired if groups == 2 and domains % 2 == 0 else plain
    return plan(fine_latent, coarse_latent, aux, interp_weights, owners, ordered(w_parent, 0), run)


def solution(mesh):
    in_specs = (P("feat", "dom"), P("feat", "dom"), P(None, "dom"), P(None, "dom"), P("dom")) + (P(),) * 10
    return jax.shard_map(shards, mesh=mesh, in_specs=in_specs, out_specs=P("feat", "dom"), check_vma=False)
```

```python
import functools

import jax
import jax.numpy as jnp
from jax import lax
from jax.experimental import pallas as pl
from jax.experimental.pallas import tpu as pltpu
from jax.sharding import PartitionSpec as P

F32 = jnp.float32
BF16 = jnp.bfloat16
PAD = 8
CHUNKS = 2
GROUPS = 16


def dot(a, b, ca, cb):
    return lax.dot_general(a, b, (((ca,), (cb,)), ((), ())), preferred_element_type=F32)


def fill_table(segments, step, places, refs, weight, table, landed, sems):
    rows = (table.shape[0] - 2 * PAD) // 6
    features = landed.shape[2] // sems.shape[2]
    table[pl.ds(0, PAD), :] = jnp.zeros((PAD, 128), F32)
    table[pl.ds(PAD + 6 * rows, PAD), :] = jnp.zeros((PAD, 128), F32)

    def copies(segment, i, slot, which):
        found = []
        for p, (sources, first) in enumerate(segments[segment][3]):
            at = pl.multiple_of(first + i * step, 128)
            found.append(
                pltpu.make_async_copy(
                    refs[sources[min(which, len(sources) - 1)]].at[:, pl.ds(at, step)],
                    landed.at[segment % 2, slot, pl.ds(p * features, features), :],
                    sems.at[segment % 2, slot, p],
                )
            )
        return found

    def start(segment, i, slot):
        if all(len(sources) == 1 for sources, _ in segments[segment][3]):
            for copy in copies(segment, i, slot, 0):
                copy.start()
            return
        for which in range(2):

            @pl.when(places[3] == which)
            def _(which=which):
                for copy in copies(segment, i, slot, which):
                    copy.start()

    start(0, 0, 0)
    for segment, (window, row, length, _) in enumerate(segments):
        steps = length // step
        if segment + 1 < len(segments):
            start(segment + 1, 0, 0)

        def one(i, carry, segment=segment, window=window, row=row, steps=steps):
            slot = lax.rem(i, 2)

            @pl.when(i + 1 < steps)
            def _():
                start(segment, i + 1, 1 - slot)

            for copy in copies(segment, i, slot, 0):
                copy.wait()
            projected = dot(landed[segment % 2, slot], weight[...], 0, 0)
            base = pl.multiple_of(PAD + 2 * (places[window] * rows + row + i * step), 8)
            table[pl.ds(base, step, stride=2), :] = projected[:, :128]
            table[pl.ds(base + 1, step, stride=2), :] = projected[:, 128:]
            return carry

        lax.fori_loop(0, steps, one, 0)


def update_kernel(sources, step, start, segments, table_step, places, aux, *refs):
    count = len(sources)
    given = 1 + max(at for source in sources for at, _ in source)
    arrays, refs = refs[:given], refs[given:]
    scales, w_latent, w_edge, w_agg, w_out_t, bias, gain, shift = refs[:8]
    table, latents, fine, total, spread_out, scale_rows, slots, live, sems = refs[-9:]
    refs = refs[8:-9]
    features, nodes = latents.shape[0] // count, latents.shape[1]
    parents = slots.shape[0] // nodes
    if segments is None:
        kept, outs = refs[0], refs[1:]
        move = pltpu.make_async_copy(kept, table, sems.at[parents + 1 + count])
        move.start()
    else:
        w_parent, *coarse = refs[: -count - 3]
        *outs, kept, landed, landed_sems = refs[-count - 3 :]
        move = pltpu.make_async_copy(table, kept, sems.at[parents + 1 + count])
    held = aux.shape[0] // (parents + 1)
    fetches = [
        pltpu.make_async_copy(aux.at[pl.ds(k * held + start, nodes)], slots.at[pl.ds(k * nodes, nodes)], sems.at[k])
        for k in range(parents)
    ]
    fetches.append(pltpu.make_async_copy(aux.at[pl.ds(parents * held, 1024)], live, sems.at[parents]))
    for fetch in fetches:
        fetch.start()

    def bring(p, which):
        at, shifted = sources[p][min(which, len(sources[p]) - 1)]
        column = pl.multiple_of(places[4] + start, 128) if shifted else 0
        return pltpu.make_async_copy(
            arrays[at].at[:, pl.ds(column, nodes)],
            latents.at[pl.ds(p * features, features), :],
            sems.at[parents + 1 + p],
        )

    for p, source in enumerate(sources):
        for which in range(len(source)):

            @pl.when((places[3] == which) | (len(source) == 1))
            def _(p=p, which=which):
                bring(p, which).start()

    if segments is not None:
        fill_table(segments, table_step, places, coarse, w_parent, table, landed, landed_sems)
        move.start()
    for fetch in fetches:
        fetch.wait()
    for p in range(count):
        bring(p, 0).wait()
    if segments is None:
        move.wait()
    sublane = lax.broadcasted_iota(jnp.int32, (8, 128), 0)
    owns = [sublane >= 2 * j for j in range(4)]

    def one_step(i, carry):
        at = pl.multiple_of(i * step, step)
        latent = latents[:, pl.ds(at, step)]
        first = dot(latent, w_latent[...], 0, 0) + bias[...]
        width = first.shape[1] // 2
        scale_columns = scales[:, pl.ds(pl.multiple_of(start + at, step), step)].T
        scale_rows[pl.ds(0, step, stride=2), :] = scale_columns
        scale_rows[pl.ds(1, step, stride=2), :] = scale_columns
        fine[pl.ds(0, step, stride=2), :] = first[:, :128]
        fine[pl.ds(1, step, stride=2), :] = first[:, 128:width]
        spread_out[...] = first[:, width:]

        def group(g):
            base = pl.multiple_of(g * 8, 8)
            node = at + g * 4
            part = fine[pl.ds(base, 8), :]
            scale = scale_rows[pl.ds(base, 8), :]
            acc = None
            for k in range(parents):
                rows = None
                for j in range(4):
                    loaded = table[pl.ds(slots[node + (k * nodes + j)], 8), :]
                    rows = loaded if rows is None else jnp.where(owns[j], loaded, rows)
                hidden = jnp.maximum(part + rows, 0.0) * scale[:, k : k + 1]
                acc = hidden if acc is None else acc + hidden
            return acc

        def some_groups(b, inner):
            sums = [group(b * GROUPS + u) for u in range(GROUPS)]
            total[pl.ds(pl.multiple_of(b * GROUPS * 8, 8), GROUPS * 8), :] = jnp.concatenate(sums, axis=0)
            return inner

        lax.fori_loop(0, step // (4 * GROUPS), some_groups, 0)
        summed = jnp.concatenate(
            [total[pl.ds(0, step, stride=2), :], total[pl.ds(1, step, stride=2), :]], axis=1
        ).astype(BF16)
        aggregate = dot(summed, w_edge[...], 1, 0).astype(BF16)
        node_hidden = jnp.maximum(spread_out[...] + dot(aggregate, w_agg[...], 1, 0), 0.0).astype(BF16)
        output = dot(w_out_t[...], node_hidden, 1, 1)
        centered = output - jnp.mean(output, axis=0, keepdims=True)
        spread = jnp.mean(centered * centered, axis=0, keepdims=True)
        normed = centered * lax.rsqrt(spread + 1e-05) * gain[...] + shift[...]
        column = start + at + lax.broadcasted_iota(jnp.int32, (1, step), 1)
        moved = jnp.where(column < live[0], normed, 0.0)
        result = (latent.astype(F32) + moved).astype(BF16)
        for r in range(count):
            outs[r][:, pl.ds(at, step)] = result[r * features : (r + 1) * features]
        return carry

    lax.fori_loop(0, nodes // step, one_step, 0)
    if segments is not None:
        move.wait()


def update(
    start, nodes, aux, arrays, sources, scales, params, places, table=None, segments=None, w_parent=None, coarse=()
):
    count, features = len(sources), arrays[0].shape[0]
    parents = aux.shape[0] - 1
    step = min(512, nodes)
    vmem = pl.BlockSpec(memory_space=pltpu.VMEM)
    smem = pl.BlockSpec(memory_space=pltpu.SMEM)
    far = pl.BlockSpec(memory_space=pltpu.HBM)
    out_shape = [jax.ShapeDtypeStruct((features, nodes), BF16)] * count
    operands = [places, aux.reshape(-1), *arrays, scales, *params]
    specs = [smem, far] + [far] * len(arrays) + [vmem] * (1 + len(params))
    scratch, table_step = [], 0
    if segments is None:
        operands, specs = operands + [table], specs + [far]
    else:
        operands, specs = operands + [w_parent, *coarse], specs + [vmem] + [far] * len(coarse)
        table_step = min(2048, segments[0][2])
        table = jax.ShapeDtypeStruct((2 * sum(segment[2] for segment in segments) + 2 * PAD, 128), F32)
        out_shape.append(table)
        scratch = [
            pltpu.VMEM((2, 2, w_parent.shape[0], table_step), BF16),
            pltpu.SemaphoreType.DMA((2, 2, len(segments[0][3]))),
        ]
    return pl.pallas_call(
        functools.partial(update_kernel, sources, step, start, segments, table_step),
        out_shape=out_shape,
        in_specs=specs,
        out_specs=[vmem] * count + [far] * (len(out_shape) - count),
        scratch_shapes=scratch
        + [
            pltpu.VMEM(table.shape, F32),
            pltpu.VMEM((count * features, nodes), BF16),
            pltpu.VMEM((2 * step, 128), F32),
            pltpu.VMEM((2 * step, 128), F32),
            pltpu.VMEM((step, 256), F32),
            pltpu.VMEM((2 * step, 8), F32),
            pltpu.SMEM((parents * nodes,), jnp.int32),
            pltpu.SMEM((1024,), jnp.int32),
            pltpu.SemaphoreType.DMA((parents + 2 + count,)),
        ],
        compiler_params=pltpu.CompilerParams(vmem_limit_bytes=40 << 20),
        cost_estimate=pl.CostEstimate(flops=nodes * 700000, bytes_accessed=nodes * 2048, transcendentals=nodes),
    )(*operands)


def after(value, *others):
    return lax.optimization_barrier((value, *others))[0]


def cut(array, at, size):
    return lax.dynamic_slice_in_dim(array, at, size, 1)


def plain(fine_latent, coarse_latent, aux, weights, w_parent, run):
    groups, domains = lax.axis_size("feat"), lax.axis_size("dom")
    rank = lax.axis_index("feat")
    per_device = fine_latent.shape[1] // groups
    length = per_device // CHUNKS
    forward = [(i, i + 1) for i in range(domains - 1)]
    backward = [(i + 1, i) for i in range(domains - 1)]

    def turn(value, r):
        return lax.ppermute(value, "feat", [(i, (i + r) % groups) for i in range(groups)])

    own = [coarse_latent] + [turn(coarse_latent, r) for r in range(1, groups)]
    low = [lax.ppermute(piece, "dom", forward) for piece in own]
    high = [lax.ppermute(piece, "dom", backward) for piece in own]
    first_row = rank * per_device
    rows = coarse_latent.shape[1]
    segments = [
        (w, 0, rows, [((w * groups + p,), 0) for p in range(groups)]) for w in range(3)
    ]
    making = dict(segments=segments, w_parent=w_parent, coarse=low + own + high)
    places = jnp.stack([0, 1, 2, 0, first_row]).astype(jnp.int32)
    sources = [((0, True),)] + [((r, False),) for r in range(1, groups)]
    aux = cut(aux, first_row, per_device)
    aux = jnp.concatenate([aux[:-1], aux[-1:] - first_row])
    weights = cut(weights, first_row, per_device)
    result = fine_latent
    arrived = []
    for c in range(CHUNKS):
        start = c * length
        pieces = [fine_latent]
        for r in range(1, groups):
            part = cut(fine_latent, ((rank + r) % groups) * per_device + start, length)
            pieces.append(turn(after(part, own[-1]), r))
        outs = run(start, length, aux, pieces, sources, weights, places, **(making if c == 0 else dict(table=table)))
        table = outs[-1] if c == 0 else table
        result = lax.dynamic_update_slice_in_dim(result, outs[0], first_row + start, 1)
        for r in range(1, groups):
            arrived.append((turn(outs[r], -r), ((rank + r) % groups) * per_device + start))
    for part, at in arrived:
        result = lax.dynamic_update_slice_in_dim(result, part, at, 1)
    return result


def paired(fine_latent, coarse_latent, aux, weights, w_parent, run):
    domains = lax.axis_size("dom")
    side, rank = lax.axis_index("dom") % 2, lax.axis_index("feat")
    matched = side == rank
    pairs = range(domains // 2)

    def send(value, moves):
        perm = [((2 * c + a) * 2 + b, (2 * c + x) * 2 + y) for c in pairs for (a, b), (x, y) in moves]
        return lax.ppermute(value, ("dom", "feat"), perm)

    def swap_rank(value):
        return send(value, [((k, f), (k, 1 - f)) for k in range(2) for f in range(2)])

    def swap_side(value):
        return send(value, [((k, f), (1 - k, f)) for k in range(2) for f in range(2)])

    def halo(value):
        perm = [((2 * c - 1) * 2, (2 * c) * 2) for c in pairs if c > 0]
        perm += [((2 * c + 2) * 2 + 1, (2 * c + 1) * 2 + 1) for c in pairs if c + 1 < len(pairs)]
        return lax.ppermute(value, ("dom", "feat"), perm)

    def hand_over(value):
        return send(value, [((0, 0), (1, 0)), ((1, 1), (0, 1))])

    to_first = [((0, 0), (1, 0)), ((1, 1), (0, 1)), ((0, 1), (0, 0)), ((1, 0), (1, 1))]
    from_first = [(b, a) for a, b in to_first]
    to_second = [((0, 1), (1, 0)), ((1, 0), (0, 1))]

    half = fine_latent.shape[1] // 2
    mine = side * half
    rows = coarse_latent.shape[1]
    mate = swap_rank(coarse_latent)
    halo_own, other = halo(coarse_latent), swap_side(after(coarse_latent, mate))
    halo_mate, other_mate = halo(mate), swap_side(mate)
    passed_own, passed_mate = hand_over(halo_own), hand_over(halo_mate)
    coarse = [coarse_latent, mate, other, other_mate, halo_own, passed_own, halo_mate, passed_mate]
    segments = [
        (0, 0, rows, [((0,), 0), ((1,), 0)]),
        (1, 0, rows, [((2,), 0), ((3,), 0)]),
        (2, 0, rows, [((4, 5), 0), ((6, 7), 0)]),
    ]
    places = jnp.stack([side + 1 - rank, 2 - side - rank, 2 * rank, jnp.where(matched, 0, 1), mine])
    places = places.astype(jnp.int32)

    length = half // CHUNKS
    chunks = []
    for c in range(CHUNKS):
        start = c * length
        first = cut(fine_latent, jnp.where(matched, half - mine, mine) + start, length)
        second = cut(fine_latent, half - mine + start, length)
        first, second = send(after(first, mate), to_first), send(after(second, mate), to_second)
        chunks.append([first, fine_latent, second])

    aux_local, aux_sent = cut(aux, mine, half), cut(aux, half - mine, half)
    aux = jnp.where(matched, aux_local, hand_over(aux_sent))
    aux = jnp.concatenate([aux[:-1], aux[-1:] - mine])
    weights = jnp.where(matched, cut(weights, mine, half), hand_over(cut(weights, half - mine, half)))

    making = dict(segments=segments, w_parent=w_parent, coarse=coarse)
    sources = [((0, False),), ((1, True), (2, False))]
    result = jnp.zeros_like(fine_latent)
    moved = []
    for c in range(CHUNKS):
        start = c * length
        out, kept, *made = run(
            start, length, aux, chunks[c], sources, weights, places, **(making if c == 0 else dict(table=table))
        )
        table = made[0] if made else table
        moved.append((start, kept, send(out, from_first), send(kept, to_second)))
    for start, kept, first, second in moved:
        result = lax.dynamic_update_slice_in_dim(result, jnp.where(matched, kept, first), mine + start, 1)
        result = lax.dynamic_update_slice_in_dim(
            result, jnp.where(matched, first, second), half - mine + start, 1
        )
    return result


def shards(
    fine_latent,
    coarse_latent,
    parents,
    interp_weights,
    live_rows,
    w_fine,
    w_parent,
    w_edge_out,
    w_node_fine,
    w_node_agg,
    w_node_out,
    edge_bias,
    node_bias,
    norm_gain,
    norm_bias,
):
    groups, domains = lax.axis_size("feat"), lax.axis_size("dom")
    rank = lax.axis_index("feat")
    own_features = fine_latent.shape[0]
    owners = [(rank - r) % groups for r in range(groups)]
    pairing = groups == 2 and domains % 2 == 0
    flip = jnp.where(lax.axis_index("dom") % 2 == rank, 1, 0) if pairing else 0

    def ordered(weight, axis, flip=flip):
        parts = [lax.dynamic_slice_in_dim(weight, o * own_features, own_features, axis) for o in owners]
        if pairing:
            parts = [jnp.where(flip == 1, parts[1], parts[0]), jnp.where(flip == 1, parts[0], parts[1])]
        return jnp.concatenate(parts, axis=axis)

    params = (
        jnp.concatenate([ordered(w_fine, 0), ordered(w_node_fine, 0)], axis=1),
        w_edge_out,
        w_node_agg,
        ordered(w_node_out, 1).T,
        jnp.concatenate([edge_bias, node_bias])[None],
        ordered(norm_gain, 0)[:, None],
        ordered(norm_bias, 0)[:, None],
    )

    def run(start, nodes, aux, arrays, sources, weights, places, **table):
        scales = jnp.pad(weights, ((0, 8 - weights.shape[0]), (0, 0)))
        return update(start, nodes, aux, arrays, sources, scales, params, places, **table)

    count = parents.shape[1]
    slots = 2 * parents + (PAD - 2 * (jnp.arange(count, dtype=jnp.int32) % 4))
    aux = jnp.concatenate([slots, jnp.broadcast_to(live_rows[:, None], (1, count))])
    plan = paired if pairing else plain
    return plan(fine_latent, coarse_latent, aux, interp_weights, ordered(w_parent, 0, 0), run)


def solution(mesh):
    in_specs = (P("feat", "dom"), P("feat", "dom"), P(None, "dom"), P(None, "dom"), P("dom")) + (P(),) * 10
    return jax.shard_map(shards, mesh=mesh, in_specs=in_specs, out_specs=P("feat", "dom"), check_vma=False)
```

```python
import functools

import jax
import jax.numpy as jnp
from jax import lax
from jax.experimental import pallas as pl
from jax.experimental.pallas import tpu as pltpu
from jax.sharding import PartitionSpec as P

F32 = jnp.float32
BF16 = jnp.bfloat16
PAD = 8
CHUNKS = 2
STEP = 128


def dot(a, b, ca, cb):
    return lax.dot_general(a, b, (((ca,), (cb,)), ((), ())), preferred_element_type=F32)


def fill_table(segments, step, places, refs, weight, table, landed, sems):
    rows = (table.shape[0] - 2 * PAD) // 6
    features = landed.shape[2] // sems.shape[2]
    table[pl.ds(0, PAD), :] = jnp.zeros((PAD, 128), F32)
    table[pl.ds(PAD + 6 * rows, PAD), :] = jnp.zeros((PAD, 128), F32)

    def copies(segment, i, slot, which):
        found = []
        for p, (sources, first) in enumerate(segments[segment][3]):
            at = pl.multiple_of(first + i * step, 128)
            found.append(
                pltpu.make_async_copy(
                    refs[sources[min(which, len(sources) - 1)]].at[:, pl.ds(at, step)],
                    landed.at[segment % 2, slot, pl.ds(p * features, features), :],
                    sems.at[segment % 2, slot, p],
                )
            )
        return found

    def start(segment, i, slot):
        if all(len(sources) == 1 for sources, _ in segments[segment][3]):
            for copy in copies(segment, i, slot, 0):
                copy.start()
            return
        for which in range(2):

            @pl.when(places[3] == which)
            def _(which=which):
                for copy in copies(segment, i, slot, which):
                    copy.start()

    start(0, 0, 0)
    for segment, (window, row, length, _) in enumerate(segments):
        steps = length // step
        if segment + 1 < len(segments):
            start(segment + 1, 0, 0)

        def one(i, carry, segment=segment, window=window, row=row, steps=steps):
            slot = lax.rem(i, 2)

            @pl.when(i + 1 < steps)
            def _():
                start(segment, i + 1, 1 - slot)

            for copy in copies(segment, i, slot, 0):
                copy.wait()
            projected = dot(landed[segment % 2, slot], weight[...], 0, 0)
            base = pl.multiple_of(PAD + 2 * (places[window] * rows + row + i * step), 8)
            table[pl.ds(base, step, stride=2), :] = projected[:, :128]
            table[pl.ds(base + 1, step, stride=2), :] = projected[:, 128:]
            return carry

        lax.fori_loop(0, steps, one, 0)


def update_kernel(sources, step, start, segments, table_step, places, aux, *refs):
    count = len(sources)
    given = 1 + max(at for source in sources for at, _ in source)
    arrays, refs = refs[:given], refs[given:]
    scales, w_latent, w_edge, w_agg, w_out_t, bias, gain, shift = refs[:8]
    table, latents, fine, total, earlier, later, scale_rows, slots, live, sems = refs[-10:]
    refs = refs[8:-10]
    features, nodes = latents.shape[0] // count, latents.shape[1]
    parents = slots.shape[0] // nodes
    if segments is None:
        kept, outs = refs[0], refs[1:]
        move = pltpu.make_async_copy(kept, table, sems.at[parents + 1 + count])
        move.start()
    else:
        w_parent, *coarse = refs[: -count - 3]
        *outs, kept, landed, landed_sems = refs[-count - 3 :]
        move = pltpu.make_async_copy(table, kept, sems.at[parents + 1 + count])
    held = aux.shape[0] // (parents + 1)
    fetches = [
        pltpu.make_async_copy(aux.at[pl.ds(k * held + start, nodes)], slots.at[pl.ds(k * nodes, nodes)], sems.at[k])
        for k in range(parents)
    ]
    fetches.append(pltpu.make_async_copy(aux.at[pl.ds(parents * held, 1024)], live, sems.at[parents]))
    for fetch in fetches:
        fetch.start()

    def bring(p, which):
        at, shifted = sources[p][min(which, len(sources[p]) - 1)]
        column = pl.multiple_of(places[4] + start, 128) if shifted else 0
        return pltpu.make_async_copy(
            arrays[at].at[:, pl.ds(column, nodes)],
            latents.at[pl.ds(p * features, features), :],
            sems.at[parents + 1 + p],
        )

    for p, source in enumerate(sources):
        for which in range(len(source)):

            @pl.when((places[3] == which) | (len(source) == 1))
            def _(p=p, which=which):
                bring(p, which).start()

    if segments is not None:
        fill_table(segments, table_step, places, coarse, w_parent, table, landed, landed_sems)
        move.start()
    for fetch in fetches:
        fetch.wait()
    for p in range(count):
        bring(p, 0).wait()
    if segments is None:
        move.wait()
    sublane = lax.broadcasted_iota(jnp.int32, (8, 128), 0)
    owns = [sublane >= 2 * j for j in range(4)]

    def begin(i):
        columns = pl.ds(pl.multiple_of(i * step, step), step)
        first = dot(latents[:, columns], w_latent[...], 0, 0) + bias[...]
        return first, scales[:, pl.ds(pl.multiple_of(start + i * step, step), step)].T

    def keep(first, scale_columns):
        width = first.shape[1] // 2
        fine[pl.ds(0, step, stride=2), :] = first[:, :128]
        fine[pl.ds(1, step, stride=2), :] = first[:, 128:width]
        later[...] = first[:, width:]
        scale_rows[pl.ds(0, step, stride=2), :] = scale_columns
        scale_rows[pl.ds(1, step, stride=2), :] = scale_columns

    def group(at, g):
        part = fine[pl.ds(g * 8, 8), :]
        scale = scale_rows[pl.ds(g * 8, 8), :]
        acc = None
        for k in range(parents):
            rows = None
            for j in range(4):
                loaded = table[pl.ds(slots[at + (k * nodes + g * 4 + j)], 8), :]
                rows = loaded if rows is None else jnp.where(owns[j], loaded, rows)
            hidden = jnp.maximum(part + rows, 0.0) * scale[:, k : k + 1]
            acc = hidden if acc is None else acc + hidden
        return acc

    def finish(i, summed, own_part):
        at = pl.multiple_of(i * step, step)
        aggregate = dot(summed.astype(BF16), w_edge[...], 1, 0).astype(BF16)
        node_hidden = jnp.maximum(own_part + dot(aggregate, w_agg[...], 1, 0), 0.0).astype(BF16)
        output = dot(w_out_t[...], node_hidden, 1, 1)
        centered = output - jnp.mean(output, axis=0, keepdims=True)
        spread = jnp.mean(centered * centered, axis=0, keepdims=True)
        normed = centered * lax.rsqrt(spread + 1e-05) * gain[...] + shift[...]
        column = start + at + lax.broadcasted_iota(jnp.int32, (1, step), 1)
        moved = jnp.where(column < live[0], normed, 0.0)
        return (latents[:, pl.ds(at, step)].astype(F32) + moved).astype(BF16)

    def write(i, result):
        for r in range(count):
            outs[r][:, pl.ds(pl.multiple_of(i * step, step), step)] = result[r * features : (r + 1) * features]

    def gathered():
        return jnp.concatenate([total[pl.ds(0, step, stride=2), :], total[pl.ds(1, step, stride=2), :]], axis=1)

    steps = nodes // step
    keep(*begin(0))

    def one_step(i, carry):
        before, after = jnp.maximum(i - 1, 0), jnp.minimum(i + 1, steps - 1)
        summed, own_part, current = gathered(), earlier[...], later[...]
        sums = [group(pl.multiple_of(i * step, step), g) for g in range(step // 4)]
        result = finish(before, summed, own_part)
        begun = begin(after)
        write(before, result)
        total[...] = jnp.concatenate(sums, axis=0)
        earlier[...] = current
        keep(*begun)
        return carry

    lax.fori_loop(0, steps, one_step, 0)
    write(steps - 1, finish(steps - 1, gathered(), earlier[...]))
    if segments is not None:
        move.wait()


def update(
    start, nodes, aux, arrays, sources, scales, params, places, table=None, segments=None, w_parent=None, coarse=()
):
    count, features = len(sources), arrays[0].shape[0]
    parents = aux.shape[0] - 1
    step = min(STEP, nodes)
    vmem = pl.BlockSpec(memory_space=pltpu.VMEM)
    smem = pl.BlockSpec(memory_space=pltpu.SMEM)
    far = pl.BlockSpec(memory_space=pltpu.HBM)
    out_shape = [jax.ShapeDtypeStruct((features, nodes), BF16)] * count
    operands = [places, aux.reshape(-1), *arrays, scales, *params]
    specs = [smem, far] + [far] * len(arrays) + [vmem] * (1 + len(params))
    scratch, table_step = [], 0
    if segments is None:
        operands, specs = operands + [table], specs + [far]
    else:
        operands, specs = operands + [w_parent, *coarse], specs + [vmem] + [far] * len(coarse)
        table_step = min(2048, segments[0][2])
        table = jax.ShapeDtypeStruct((2 * sum(segment[2] for segment in segments) + 2 * PAD, 128), F32)
        out_shape.append(table)
        scratch = [
            pltpu.VMEM((2, 2, w_parent.shape[0], table_step), BF16),
            pltpu.SemaphoreType.DMA((2, 2, len(segments[0][3]))),
        ]
    return pl.pallas_call(
        functools.partial(update_kernel, sources, step, start, segments, table_step),
        out_shape=out_shape,
        in_specs=specs,
        out_specs=[vmem] * count + [far] * (len(out_shape) - count),
        scratch_shapes=scratch
        + [
            pltpu.VMEM(table.shape, F32),
            pltpu.VMEM((count * features, nodes), BF16),
            pltpu.VMEM((2 * step, 128), F32),
            pltpu.VMEM((2 * step, 128), F32),
            pltpu.VMEM((step, 256), F32),
            pltpu.VMEM((step, 256), F32),
            pltpu.VMEM((2 * step, 8), F32),
            pltpu.SMEM((parents * nodes,), jnp.int32),
            pltpu.SMEM((1024,), jnp.int32),
            pltpu.SemaphoreType.DMA((parents + 2 + count,)),
        ],
        compiler_params=pltpu.CompilerParams(vmem_limit_bytes=40 << 20),
        cost_estimate=pl.CostEstimate(flops=nodes * 700000, bytes_accessed=nodes * 2048, transcendentals=nodes),
    )(*operands)


def after(value, *others):
    return lax.optimization_barrier((value, *others))[0]


def cut(array, at, size):
    return lax.dynamic_slice_in_dim(array, at, size, 1)


def plain(fine_latent, coarse_latent, aux, weights, w_parent, run):
    groups, domains = lax.axis_size("feat"), lax.axis_size("dom")
    rank = lax.axis_index("feat")
    per_device = fine_latent.shape[1] // groups
    length = per_device // CHUNKS
    forward = [(i, i + 1) for i in range(domains - 1)]
    backward = [(i + 1, i) for i in range(domains - 1)]

    def turn(value, r):
        return lax.ppermute(value, "feat", [(i, (i + r) % groups) for i in range(groups)])

    own = [coarse_latent] + [turn(coarse_latent, r) for r in range(1, groups)]
    low = [lax.ppermute(piece, "dom", forward) for piece in own]
    high = [lax.ppermute(piece, "dom", backward) for piece in own]
    first_row = rank * per_device
    rows = coarse_latent.shape[1]
    segments = [
        (w, 0, rows, [((w * groups + p,), 0) for p in range(groups)]) for w in range(3)
    ]
    making = dict(segments=segments, w_parent=w_parent, coarse=low + own + high)
    places = jnp.stack([0, 1, 2, 0, first_row]).astype(jnp.int32)
    sources = [((0, True),)] + [((r, False),) for r in range(1, groups)]
    aux = cut(aux, first_row, per_device)
    aux = jnp.concatenate([aux[:-1], aux[-1:] - first_row])
    weights = cut(weights, first_row, per_device)
    result = fine_latent
    arrived = []
    for c in range(CHUNKS):
        start = c * length
        pieces = [fine_latent]
        for r in range(1, groups):
            part = cut(fine_latent, ((rank + r) % groups) * per_device + start, length)
            pieces.append(turn(after(part, own[-1]), r))
        outs = run(start, length, aux, pieces, sources, weights, places, **(making if c == 0 else dict(table=table)))
        table = outs[-1] if c == 0 else table
        result = lax.dynamic_update_slice_in_dim(result, outs[0], first_row + start, 1)
        for r in range(1, groups):
            arrived.append((turn(outs[r], -r), ((rank + r) % groups) * per_device + start))
    for part, at in arrived:
        result = lax.dynamic_update_slice_in_dim(result, part, at, 1)
    return result


def paired(fine_latent, coarse_latent, aux, weights, w_parent, run):
    domains = lax.axis_size("dom")
    side, rank = lax.axis_index("dom") % 2, lax.axis_index("feat")
    matched = side == rank
    pairs = range(domains // 2)

    def send(value, moves):
        perm = [((2 * c + a) * 2 + b, (2 * c + x) * 2 + y) for c in pairs for (a, b), (x, y) in moves]
        return lax.ppermute(value, ("dom", "feat"), perm)

    def swap_rank(value):
        return send(value, [((k, f), (k, 1 - f)) for k in range(2) for f in range(2)])

    def swap_side(value):
        return send(value, [((k, f), (1 - k, f)) for k in range(2) for f in range(2)])

    def halo(value):
        perm = [((2 * c - 1) * 2, (2 * c) * 2) for c in pairs if c > 0]
        perm += [((2 * c + 2) * 2 + 1, (2 * c + 1) * 2 + 1) for c in pairs if c + 1 < len(pairs)]
        return lax.ppermute(value, ("dom", "feat"), perm)

    def hand_over(value):
        return send(value, [((0, 0), (1, 0)), ((1, 1), (0, 1))])

    to_first = [((0, 0), (1, 0)), ((1, 1), (0, 1)), ((0, 1), (0, 0)), ((1, 0), (1, 1))]
    from_first = [(b, a) for a, b in to_first]
    to_second = [((0, 1), (1, 0)), ((1, 0), (0, 1))]

    half = fine_latent.shape[1] // 2
    mine = side * half
    rows = coarse_latent.shape[1]
    mate = swap_rank(coarse_latent)
    halo_own, other = halo(coarse_latent), swap_side(after(coarse_latent, mate))
    halo_mate, other_mate = halo(mate), swap_side(mate)
    passed_own, passed_mate = hand_over(halo_own), hand_over(halo_mate)
    coarse = [coarse_latent, mate, other, other_mate, halo_own, passed_own, halo_mate, passed_mate]
    segments = [
        (0, 0, rows, [((0,), 0), ((1,), 0)]),
        (1, 0, rows, [((2,), 0), ((3,), 0)]),
        (2, 0, rows, [((4, 5), 0), ((6, 7), 0)]),
    ]
    places = jnp.stack([side + 1 - rank, 2 - side - rank, 2 * rank, jnp.where(matched, 0, 1), mine])
    places = places.astype(jnp.int32)

    length = half // CHUNKS
    chunks = []
    for c in range(CHUNKS):
        start = c * length
        first = cut(fine_latent, jnp.where(matched, half - mine, mine) + start, length)
        second = cut(fine_latent, half - mine + start, length)
        first, second = send(after(first, mate), to_first), send(after(second, mate), to_second)
        chunks.append([first, fine_latent, second])

    aux_local, aux_sent = cut(aux, mine, half), cut(aux, half - mine, half)
    aux = jnp.where(matched, aux_local, hand_over(aux_sent))
    aux = jnp.concatenate([aux[:-1], aux[-1:] - mine])
    weights = jnp.where(matched, cut(weights, mine, half), hand_over(cut(weights, half - mine, half)))

    making = dict(segments=segments, w_parent=w_parent, coarse=coarse)
    sources = [((0, False),), ((1, True), (2, False))]
    result = jnp.zeros_like(fine_latent)
    moved = []
    for c in range(CHUNKS):
        start = c * length
        out, kept, *made = run(
            start, length, aux, chunks[c], sources, weights, places, **(making if c == 0 else dict(table=table))
        )
        table = made[0] if made else table
        moved.append((start, kept, send(out, from_first), send(kept, to_second)))
    for start, kept, first, second in moved:
        result = lax.dynamic_update_slice_in_dim(result, jnp.where(matched, kept, first), mine + start, 1)
        result = lax.dynamic_update_slice_in_dim(
            result, jnp.where(matched, first, second), half - mine + start, 1
        )
    return result


def shards(
    fine_latent,
    coarse_latent,
    parents,
    interp_weights,
    live_rows,
    w_fine,
    w_parent,
    w_edge_out,
    w_node_fine,
    w_node_agg,
    w_node_out,
    edge_bias,
    node_bias,
    norm_gain,
    norm_bias,
):
    groups, domains = lax.axis_size("feat"), lax.axis_size("dom")
    rank = lax.axis_index("feat")
    own_features = fine_latent.shape[0]
    owners = [(rank - r) % groups for r in range(groups)]
    pairing = groups == 2 and domains % 2 == 0
    flip = jnp.where(lax.axis_index("dom") % 2 == rank, 1, 0) if pairing else 0

    def ordered(weight, axis, flip=flip):
        parts = [lax.dynamic_slice_in_dim(weight, o * own_features, own_features, axis) for o in owners]
        if pairing:
            parts = [jnp.where(flip == 1, parts[1], parts[0]), jnp.where(flip == 1, parts[0], parts[1])]
        return jnp.concatenate(parts, axis=axis)

    params = (
        jnp.concatenate([ordered(w_fine, 0), ordered(w_node_fine, 0)], axis=1),
        w_edge_out,
        w_node_agg,
        ordered(w_node_out, 1).T,
        jnp.concatenate([edge_bias, node_bias])[None],
        jnp.broadcast_to(ordered(norm_gain, 0)[:, None], (norm_gain.shape[0], STEP)),
        jnp.broadcast_to(ordered(norm_bias, 0)[:, None], (norm_bias.shape[0], STEP)),
    )

    def run(start, nodes, aux, arrays, sources, weights, places, **table):
        scales = jnp.pad(weights, ((0, 8 - weights.shape[0]), (0, 0)))
        return update(start, nodes, aux, arrays, sources, scales, params, places, **table)

    count = parents.shape[1]
    slots = 2 * parents + (PAD - 2 * (jnp.arange(count, dtype=jnp.int32) % 4))
    aux = jnp.concatenate([slots, jnp.broadcast_to(live_rows[:, None], (1, count))])
    plan = paired if pairing else plain
    return plan(fine_latent, coarse_latent, aux, interp_weights, ordered(w_parent, 0, 0), run)


def solution(mesh):
    in_specs = (P("feat", "dom"), P("feat", "dom"), P(None, "dom"), P(None, "dom"), P("dom")) + (P(),) * 10
    return jax.shard_map(shards, mesh=mesh, in_specs=in_specs, out_specs=P("feat", "dom"), check_vma=False)
```

```python
import functools

import jax
import jax.numpy as jnp
from jax import lax
from jax.experimental import pallas as pl
from jax.experimental.pallas import tpu as pltpu
from jax.sharding import PartitionSpec as P

F32 = jnp.float32
BF16 = jnp.bfloat16
PAD = 8
CHUNKS = 2
STEP = 128


def dot(a, b, ca, cb):
    return lax.dot_general(a, b, (((ca,), (cb,)), ((), ())), preferred_element_type=F32)


def fill_table(segments, step, places, refs, weight, table, landed, sems):
    rows = (table.shape[0] - 2 * PAD) // 6
    features = landed.shape[2] // sems.shape[2]
    table[pl.ds(0, PAD), :] = jnp.zeros((PAD, 128), F32)
    table[pl.ds(PAD + 6 * rows, PAD), :] = jnp.zeros((PAD, 128), F32)

    def copies(segment, i, slot, which):
        found = []
        for p, (sources, first) in enumerate(segments[segment][3]):
            at = pl.multiple_of(first + i * step, 128)
            found.append(
                pltpu.make_async_copy(
                    refs[sources[min(which, len(sources) - 1)]].at[:, pl.ds(at, step)],
                    landed.at[segment % 2, slot, pl.ds(p * features, features), :],
                    sems.at[segment % 2, slot, p],
                )
            )
        return found

    def start(segment, i, slot):
        if all(len(sources) == 1 for sources, _ in segments[segment][3]):
            for copy in copies(segment, i, slot, 0):
                copy.start()
            return
        for which in range(2):

            @pl.when(places[3] == which)
            def _(which=which):
                for copy in copies(segment, i, slot, which):
                    copy.start()

    start(0, 0, 0)
    for segment, (window, row, length, _) in enumerate(segments):
        steps = length // step
        if segment + 1 < len(segments):
            start(segment + 1, 0, 0)

        def one(i, carry, segment=segment, window=window, row=row, steps=steps):
            slot = lax.rem(i, 2)

            @pl.when(i + 1 < steps)
            def _():
                start(segment, i + 1, 1 - slot)

            for copy in copies(segment, i, slot, 0):
                copy.wait()
            projected = dot(landed[segment % 2, slot], weight[...], 0, 0)
            base = pl.multiple_of(PAD + 2 * (places[window] * rows + row + i * step), 8)
            table[pl.ds(base, step, stride=2), :] = projected[:, :128]
            table[pl.ds(base + 1, step, stride=2), :] = projected[:, 128:]
            return carry

        lax.fori_loop(0, steps, one, 0)


def update_kernel(sources, step, start, segments, table_step, places, aux, *refs):
    count = len(sources)
    given = 1 + max(at for source in sources for at, _ in source)
    arrays, refs = refs[:given], refs[given:]
    scales, lanes, w_latent, w_edge, w_agg, w_out_t, bias, gain, shift = refs[:9]
    table, latents, fine, total, earlier, later, scale_rows, slots, live, sems = refs[-10:]
    refs = refs[9:-10]
    features, nodes = latents.shape[0] // count, latents.shape[1]
    parents = slots.shape[0] // nodes
    if segments is None:
        kept, outs = refs[0], refs[1:]
        move = pltpu.make_async_copy(kept, table, sems.at[parents + 1 + count])
        move.start()
    else:
        w_parent, *coarse = refs[: -count - 3]
        *outs, kept, landed, landed_sems = refs[-count - 3 :]
        move = pltpu.make_async_copy(table, kept, sems.at[parents + 1 + count])
    held = aux.shape[0] // (parents + 1)
    fetches = [
        pltpu.make_async_copy(aux.at[pl.ds(k * held + start, nodes)], slots.at[pl.ds(k * nodes, nodes)], sems.at[k])
        for k in range(parents)
    ]
    fetches.append(pltpu.make_async_copy(aux.at[pl.ds(parents * held, 1024)], live, sems.at[parents]))
    for fetch in fetches:
        fetch.start()

    def bring(p, which):
        at, shifted = sources[p][min(which, len(sources[p]) - 1)]
        column = pl.multiple_of(places[4] + start, 128) if shifted else 0
        return pltpu.make_async_copy(
            arrays[at].at[:, pl.ds(column, nodes)],
            latents.at[pl.ds(p * features, features), :],
            sems.at[parents + 1 + p],
        )

    for p, source in enumerate(sources):
        for which in range(len(source)):

            @pl.when((places[3] == which) | (len(source) == 1))
            def _(p=p, which=which):
                bring(p, which).start()

    if segments is not None:
        fill_table(segments, table_step, places, coarse, w_parent, table, landed, landed_sems)
        move.start()
    for fetch in fetches:
        fetch.wait()
    for p in range(count):
        bring(p, 0).wait()
    if segments is None:
        move.wait()
    sublane = lax.broadcasted_iota(jnp.int32, (8, 128), 0)
    owns = [sublane >= 2 * j for j in range(4)]

    def begin(i):
        columns = pl.ds(pl.multiple_of(i * step, step), step)
        first = dot(latents[:, columns], w_latent[...], 0, 0) + bias[...]
        weights = dot(scales[:, pl.ds(pl.multiple_of(start + i * step, step), step)], lanes[...], 0, 0)
        return first, weights

    def keep(first, weights):
        width = first.shape[1] // 2
        fine[pl.ds(0, step, stride=2), :] = first[:, :128]
        fine[pl.ds(1, step, stride=2), :] = first[:, 128:width]
        later[...] = first[:, width:]
        for k in range(parents):
            spread_over_lanes = weights[:, k * 128 : (k + 1) * 128]
            scale_rows[k, pl.ds(0, step, stride=2), :] = spread_over_lanes
            scale_rows[k, pl.ds(1, step, stride=2), :] = spread_over_lanes

    def group(at, g):
        part = fine[pl.ds(g * 8, 8), :]
        acc = None
        for k in range(parents):
            rows = None
            for j in range(4):
                loaded = table[pl.ds(slots[at + (k * nodes + g * 4 + j)], 8), :]
                rows = loaded if rows is None else jnp.where(owns[j], loaded, rows)
            hidden = jnp.maximum(part + rows, 0.0) * scale_rows[k, pl.ds(g * 8, 8), :]
            acc = hidden if acc is None else acc + hidden
        return acc

    def finish(i, summed, own_part):
        at = pl.multiple_of(i * step, step)
        aggregate = dot(summed.astype(BF16), w_edge[...], 1, 0).astype(BF16)
        node_hidden = jnp.maximum(own_part + dot(aggregate, w_agg[...], 1, 0), 0.0).astype(BF16)
        output = dot(w_out_t[...], node_hidden, 1, 1)
        centered = output - jnp.mean(output, axis=0, keepdims=True)
        spread = jnp.mean(centered * centered, axis=0, keepdims=True)
        normed = centered * lax.rsqrt(spread + 1e-05) * gain[...] + shift[...]
        column = start + at + lax.broadcasted_iota(jnp.int32, (1, step), 1)
        moved = jnp.where(column < live[0], normed, 0.0)
        return (latents[:, pl.ds(at, step)].astype(F32) + moved).astype(BF16)

    def write(i, result):
        for r in range(count):
            outs[r][:, pl.ds(pl.multiple_of(i * step, step), step)] = result[r * features : (r + 1) * features]

    def gathered():
        return jnp.concatenate([total[pl.ds(0, step, stride=2), :], total[pl.ds(1, step, stride=2), :]], axis=1)

    steps = nodes // step
    keep(*begin(0))

    def one_step(i, carry):
        before, after = jnp.maximum(i - 1, 0), jnp.minimum(i + 1, steps - 1)
        summed, own_part, current = gathered(), earlier[...], later[...]
        sums = [group(pl.multiple_of(i * step, step), g) for g in range(step // 4)]
        result = finish(before, summed, own_part)
        begun = begin(after)
        write(before, result)
        total[...] = jnp.concatenate(sums, axis=0)
        earlier[...] = current
        keep(*begun)
        return carry

    lax.fori_loop(0, steps, one_step, 0)
    write(steps - 1, finish(steps - 1, gathered(), earlier[...]))
    if segments is not None:
        move.wait()


def update(
    start, nodes, aux, arrays, sources, scales, params, places, table=None, segments=None, w_parent=None, coarse=()
):
    count, features = len(sources), arrays[0].shape[0]
    parents = aux.shape[0] - 1
    step = min(STEP, nodes)
    vmem = pl.BlockSpec(memory_space=pltpu.VMEM)
    smem = pl.BlockSpec(memory_space=pltpu.SMEM)
    far = pl.BlockSpec(memory_space=pltpu.HBM)
    out_shape = [jax.ShapeDtypeStruct((features, nodes), BF16)] * count
    operands = [places, aux.reshape(-1), *arrays, scales, *params]
    specs = [smem, far] + [far] * len(arrays) + [vmem] * (1 + len(params))
    scratch, table_step = [], 0
    if segments is None:
        operands, specs = operands + [table], specs + [far]
    else:
        operands, specs = operands + [w_parent, *coarse], specs + [vmem] + [far] * len(coarse)
        table_step = min(2048, segments[0][2])
        table = jax.ShapeDtypeStruct((2 * sum(segment[2] for segment in segments) + 2 * PAD, 128), F32)
        out_shape.append(table)
        scratch = [
            pltpu.VMEM((2, 2, w_parent.shape[0], table_step), BF16),
            pltpu.SemaphoreType.DMA((2, 2, len(segments[0][3]))),
        ]
    return pl.pallas_call(
        functools.partial(update_kernel, sources, step, start, segments, table_step),
        out_shape=out_shape,
        in_specs=specs,
        out_specs=[vmem] * count + [far] * (len(out_shape) - count),
        scratch_shapes=scratch
        + [
            pltpu.VMEM(table.shape, F32),
            pltpu.VMEM((count * features, nodes), BF16),
            pltpu.VMEM((2 * step, 128), F32),
            pltpu.VMEM((2 * step, 128), F32),
            pltpu.VMEM((step, 256), F32),
            pltpu.VMEM((step, 256), F32),
            pltpu.VMEM((parents, 2 * step, 128), F32),
            pltpu.SMEM((parents * nodes,), jnp.int32),
            pltpu.SMEM((1024,), jnp.int32),
            pltpu.SemaphoreType.DMA((parents + 2 + count,)),
        ],
        compiler_params=pltpu.CompilerParams(vmem_limit_bytes=40 << 20),
        cost_estimate=pl.CostEstimate(flops=nodes * 700000, bytes_accessed=nodes * 2048, transcendentals=nodes),
    )(*operands)


def after(value, *others):
    return lax.optimization_barrier((value, *others))[0]


def cut(array, at, size):
    return lax.dynamic_slice_in_dim(array, at, size, 1)


def plain(fine_latent, coarse_latent, aux, weights, w_parent, run):
    groups, domains = lax.axis_size("feat"), lax.axis_size("dom")
    rank = lax.axis_index("feat")
    per_device = fine_latent.shape[1] // groups
    length = per_device // CHUNKS
    forward = [(i, i + 1) for i in range(domains - 1)]
    backward = [(i + 1, i) for i in range(domains - 1)]

    def turn(value, r):
        return lax.ppermute(value, "feat", [(i, (i + r) % groups) for i in range(groups)])

    own = [coarse_latent] + [turn(coarse_latent, r) for r in range(1, groups)]
    low = [lax.ppermute(piece, "dom", forward) for piece in own]
    high = [lax.ppermute(piece, "dom", backward) for piece in own]
    first_row = rank * per_device
    rows = coarse_latent.shape[1]
    segments = [
        (w, 0, rows, [((w * groups + p,), 0) for p in range(groups)]) for w in range(3)
    ]
    making = dict(segments=segments, w_parent=w_parent, coarse=low + own + high)
    places = jnp.stack([0, 1, 2, 0, first_row]).astype(jnp.int32)
    sources = [((0, True),)] + [((r, False),) for r in range(1, groups)]
    aux = cut(aux, first_row, per_device)
    aux = jnp.concatenate([aux[:-1], aux[-1:] - first_row])
    weights = cut(weights, first_row, per_device)
    result = fine_latent
    arrived = []
    for c in range(CHUNKS):
        start = c * length
        pieces = [fine_latent]
        for r in range(1, groups):
            part = cut(fine_latent, ((rank + r) % groups) * per_device + start, length)
            pieces.append(turn(after(part, own[-1]), r))
        outs = run(start, length, aux, pieces, sources, weights, places, **(making if c == 0 else dict(table=table)))
        table = outs[-1] if c == 0 else table
        result = lax.dynamic_update_slice_in_dim(result, outs[0], first_row + start, 1)
        for r in range(1, groups):
            arrived.append((turn(outs[r], -r), ((rank + r) % groups) * per_device + start))
    for part, at in arrived:
        result = lax.dynamic_update_slice_in_dim(result, part, at, 1)
    return result


def paired(fine_latent, coarse_latent, aux, weights, w_parent, run):
    domains = lax.axis_size("dom")
    side, rank = lax.axis_index("dom") % 2, lax.axis_index("feat")
    matched = side == rank
    pairs = range(domains // 2)

    def send(value, moves):
        perm = [((2 * c + a) * 2 + b, (2 * c + x) * 2 + y) for c in pairs for (a, b), (x, y) in moves]
        return lax.ppermute(value, ("dom", "feat"), perm)

    def swap_rank(value):
        return send(value, [((k, f), (k, 1 - f)) for k in range(2) for f in range(2)])

    def swap_side(value):
        return send(value, [((k, f), (1 - k, f)) for k in range(2) for f in range(2)])

    def halo(value):
        perm = [((2 * c - 1) * 2, (2 * c) * 2) for c in pairs if c > 0]
        perm += [((2 * c + 2) * 2 + 1, (2 * c + 1) * 2 + 1) for c in pairs if c + 1 < len(pairs)]
        return lax.ppermute(value, ("dom", "feat"), perm)

    def hand_over(value):
        return send(value, [((0, 0), (1, 0)), ((1, 1), (0, 1))])

    to_first = [((0, 0), (1, 0)), ((1, 1), (0, 1)), ((0, 1), (0, 0)), ((1, 0), (1, 1))]
    from_first = [(b, a) for a, b in to_first]
    to_second = [((0, 1), (1, 0)), ((1, 0), (0, 1))]

    half = fine_latent.shape[1] // 2
    mine = side * half
    rows = coarse_latent.shape[1]
    mate = swap_rank(coarse_latent)
    halo_own, other = halo(coarse_latent), swap_side(after(coarse_latent, mate))
    halo_mate, other_mate = halo(mate), swap_side(mate)
    passed_own, passed_mate = hand_over(halo_own), hand_over(halo_mate)
    coarse = [coarse_latent, mate, other, other_mate, halo_own, passed_own, halo_mate, passed_mate]
    segments = [
        (0, 0, rows, [((0,), 0), ((1,), 0)]),
        (1, 0, rows, [((2,), 0), ((3,), 0)]),
        (2, 0, rows, [((4, 5), 0), ((6, 7), 0)]),
    ]
    places = jnp.stack([side + 1 - rank, 2 - side - rank, 2 * rank, jnp.where(matched, 0, 1), mine])
    places = places.astype(jnp.int32)

    length = half // CHUNKS
    chunks = []
    for c in range(CHUNKS):
        start = c * length
        first = cut(fine_latent, jnp.where(matched, half - mine, mine) + start, length)
        second = cut(fine_latent, half - mine + start, length)
        first, second = send(after(first, mate), to_first), send(after(second, mate), to_second)
        chunks.append([first, fine_latent, second])

    aux_local, aux_sent = cut(aux, mine, half), cut(aux, half - mine, half)
    aux = jnp.where(matched, aux_local, hand_over(aux_sent))
    aux = jnp.concatenate([aux[:-1], aux[-1:] - mine])
    weights = jnp.where(matched, cut(weights, mine, half), hand_over(cut(weights, half - mine, half)))

    making = dict(segments=segments, w_parent=w_parent, coarse=coarse)
    sources = [((0, False),), ((1, True), (2, False))]
    result = jnp.zeros_like(fine_latent)
    moved = []
    for c in range(CHUNKS):
        start = c * length
        out, kept, *made = run(
            start, length, aux, chunks[c], sources, weights, places, **(making if c == 0 else dict(table=table))
        )
        table = made[0] if made else table
        moved.append((start, kept, send(out, from_first), send(kept, to_second)))
    for start, kept, first, second in moved:
        result = lax.dynamic_update_slice_in_dim(result, jnp.where(matched, kept, first), mine + start, 1)
        result = lax.dynamic_update_slice_in_dim(
            result, jnp.where(matched, first, second), half - mine + start, 1
        )
    return result


def shards(
    fine_latent,
    coarse_latent,
    parents,
    interp_weights,
    live_rows,
    w_fine,
    w_parent,
    w_edge_out,
    w_node_fine,
    w_node_agg,
    w_node_out,
    edge_bias,
    node_bias,
    norm_gain,
    norm_bias,
):
    groups, domains = lax.axis_size("feat"), lax.axis_size("dom")
    rank = lax.axis_index("feat")
    own_features = fine_latent.shape[0]
    owners = [(rank - r) % groups for r in range(groups)]
    pairing = groups == 2 and domains % 2 == 0
    flip = jnp.where(lax.axis_index("dom") % 2 == rank, 1, 0) if pairing else 0

    def ordered(weight, axis, flip=flip):
        parts = [lax.dynamic_slice_in_dim(weight, o * own_features, own_features, axis) for o in owners]
        if pairing:
            parts = [jnp.where(flip == 1, parts[1], parts[0]), jnp.where(flip == 1, parts[0], parts[1])]
        return jnp.concatenate(parts, axis=axis)

    params = (
        jnp.concatenate([ordered(w_fine, 0), ordered(w_node_fine, 0)], axis=1),
        w_edge_out,
        w_node_agg,
        ordered(w_node_out, 1).T,
        jnp.concatenate([edge_bias, node_bias])[None],
        jnp.broadcast_to(ordered(norm_gain, 0)[:, None], (norm_gain.shape[0], STEP)),
        jnp.broadcast_to(ordered(norm_bias, 0)[:, None], (norm_bias.shape[0], STEP)),
    )

    ways = interp_weights.shape[0]
    row, column = jnp.arange(4 * ways)[:, None], jnp.arange(128 * ways)[None]
    lanes = ((row % ways == column // 128) & (row < 3 * ways)).astype(BF16)

    def run(start, nodes, aux, arrays, sources, weights, places, **table):
        high = lax.reduce_precision(weights, 8, 7)
        middle = lax.reduce_precision(weights - high, 8, 7)
        scales = jnp.concatenate([high, middle, weights - high - middle, jnp.zeros_like(high)]).astype(BF16)
        return update(start, nodes, aux, arrays, sources, scales, (lanes, *params), places, **table)

    count = parents.shape[1]
    slots = 2 * parents + (PAD - 2 * (jnp.arange(count, dtype=jnp.int32) % 4))
    aux = jnp.concatenate([slots, jnp.broadcast_to(live_rows[:, None], (1, count))])
    plan = paired if pairing else plain
    return plan(fine_latent, coarse_latent, aux, interp_weights, ordered(w_parent, 0, 0), run)


def solution(mesh):
    in_specs = (P("feat", "dom"), P("feat", "dom"), P(None, "dom"), P(None, "dom"), P("dom")) + (P(),) * 10
    return jax.shard_map(shards, mesh=mesh, in_specs=in_specs, out_specs=P("feat", "dom"), check_vma=False)
```

```python
import functools

import jax
import jax.numpy as jnp
from jax import lax
from jax.experimental import pallas as pl
from jax.experimental.pallas import tpu as pltpu
from jax.sharding import PartitionSpec as P

F32 = jnp.float32
BF16 = jnp.bfloat16
PAD = 8
CHUNKS = 2
STEP = 256
GROUPS = 16


def dot(a, b, ca, cb):
    return lax.dot_general(a, b, (((ca,), (cb,)), ((), ())), preferred_element_type=F32)


def fill_table(segments, step, places, refs, weight, table, landed, sems):
    rows = (table.shape[0] - 2 * PAD) // 6
    features = landed.shape[2] // sems.shape[2]
    table[pl.ds(0, PAD), :] = jnp.zeros((PAD, 128), F32)
    table[pl.ds(PAD + 6 * rows, PAD), :] = jnp.zeros((PAD, 128), F32)

    def copies(segment, i, slot, which):
        found = []
        for p, (sources, first) in enumerate(segments[segment][3]):
            at = pl.multiple_of(first + i * step, 128)
            found.append(
                pltpu.make_async_copy(
                    refs[sources[min(which, len(sources) - 1)]].at[:, pl.ds(at, step)],
                    landed.at[segment % 2, slot, pl.ds(p * features, features), :],
                    sems.at[segment % 2, slot, p],
                )
            )
        return found

    def start(segment, i, slot):
        if all(len(sources) == 1 for sources, _ in segments[segment][3]):
            for copy in copies(segment, i, slot, 0):
                copy.start()
            return
        for which in range(2):

            @pl.when(places[3] == which)
            def _(which=which):
                for copy in copies(segment, i, slot, which):
                    copy.start()

    start(0, 0, 0)
    for segment, (window, row, length, _) in enumerate(segments):
        steps = length // step
        if segment + 1 < len(segments):
            start(segment + 1, 0, 0)

        def one(i, carry, segment=segment, window=window, row=row, steps=steps):
            slot = lax.rem(i, 2)

            @pl.when(i + 1 < steps)
            def _():
                start(segment, i + 1, 1 - slot)

            for copy in copies(segment, i, slot, 0):
                copy.wait()
            projected = dot(landed[segment % 2, slot], weight[...], 0, 0)
            base = pl.multiple_of(PAD + 2 * (places[window] * rows + row + i * step), 8)
            table[pl.ds(base, step, stride=2), :] = projected[:, :128]
            table[pl.ds(base + 1, step, stride=2), :] = projected[:, 128:]
            return carry

        lax.fori_loop(0, steps, one, 0)


def update_kernel(sources, step, start, segments, table_step, places, aux, *refs):
    count = len(sources)
    given = 1 + max(at for source in sources for at, _ in source)
    arrays, refs = refs[:given], refs[given:]
    scales, w_latent, w_edge, w_agg, w_out_t, bias, gain, shift = refs[:8]
    table, latents, fine, total, earlier, later, scale_rows, slots, live, sems = refs[-10:]
    refs = refs[8:-10]
    features, nodes = latents.shape[0] // count, latents.shape[1]
    parents = slots.shape[0] // nodes
    if segments is None:
        kept, outs = refs[0], refs[1:]
        move = pltpu.make_async_copy(kept, table, sems.at[parents + 1 + count])
        move.start()
    else:
        w_parent, *coarse = refs[: -count - 3]
        *outs, kept, landed, landed_sems = refs[-count - 3 :]
        move = pltpu.make_async_copy(table, kept, sems.at[parents + 1 + count])
    held = aux.shape[0] // (parents + 1)
    fetches = [
        pltpu.make_async_copy(aux.at[pl.ds(k * held + start, nodes)], slots.at[pl.ds(k * nodes, nodes)], sems.at[k])
        for k in range(parents)
    ]
    fetches.append(pltpu.make_async_copy(aux.at[pl.ds(parents * held, 1024)], live, sems.at[parents]))
    for fetch in fetches:
        fetch.start()

    def bring(p, which):
        at, shifted = sources[p][min(which, len(sources[p]) - 1)]
        column = pl.multiple_of(places[4] + start, 128) if shifted else 0
        return pltpu.make_async_copy(
            arrays[at].at[:, pl.ds(column, nodes)],
            latents.at[pl.ds(p * features, features), :],
            sems.at[parents + 1 + p],
        )

    for p, source in enumerate(sources):
        for which in range(len(source)):

            @pl.when((places[3] == which) | (len(source) == 1))
            def _(p=p, which=which):
                bring(p, which).start()

    if segments is not None:
        fill_table(segments, table_step, places, coarse, w_parent, table, landed, landed_sems)
        move.start()
    for fetch in fetches:
        fetch.wait()
    for p in range(count):
        bring(p, 0).wait()
    if segments is None:
        move.wait()
    sublane = lax.broadcasted_iota(jnp.int32, (8, 128), 0)
    owns = [sublane >= 2 * j for j in range(4)]

    def begin(i):
        columns = pl.ds(pl.multiple_of(i * step, step), step)
        first = dot(latents[:, columns], w_latent[...], 0, 0) + bias[...]
        return first, scales[:, pl.ds(pl.multiple_of(start + i * step, step), step)].T

    def keep(first, scale_columns):
        width = first.shape[1] // 2
        fine[pl.ds(0, step, stride=2), :] = first[:, :128]
        fine[pl.ds(1, step, stride=2), :] = first[:, 128:width]
        later[...] = first[:, width:]
        scale_rows[pl.ds(0, step, stride=2), :] = scale_columns
        scale_rows[pl.ds(1, step, stride=2), :] = scale_columns

    def group(at, g):
        part = fine[pl.ds(g * 8, 8), :]
        scale = scale_rows[pl.ds(g * 8, 8), :]
        acc = None
        for k in range(parents):
            rows = None
            for j in range(4):
                loaded = table[pl.ds(slots[at + (k * nodes + g * 4 + j)], 8), :]
                rows = loaded if rows is None else jnp.where(owns[j], loaded, rows)
            hidden = jnp.maximum(part + rows, 0.0) * scale[:, k : k + 1]
            acc = hidden if acc is None else acc + hidden
        return acc

    def finish(i, summed, own_part):
        at = pl.multiple_of(i * step, step)
        aggregate = dot(summed.astype(BF16), w_edge[...], 1, 0).astype(BF16)
        node_hidden = jnp.maximum(own_part + dot(aggregate, w_agg[...], 1, 0), 0.0).astype(BF16)
        output = dot(w_out_t[...], node_hidden, 1, 1)
        centered = output - jnp.mean(output, axis=0, keepdims=True)
        spread = jnp.mean(centered * centered, axis=0, keepdims=True)
        normed = centered * lax.rsqrt(spread + 1e-05) * gain[...] + shift[...]
        column = start + at + lax.broadcasted_iota(jnp.int32, (1, step), 1)
        moved = jnp.where(column < live[0], normed, 0.0)
        return (latents[:, pl.ds(at, step)].astype(F32) + moved).astype(BF16)

    def write(i, result):
        for r in range(count):
            outs[r][:, pl.ds(pl.multiple_of(i * step, step), step)] = result[r * features : (r + 1) * features]

    def gathered():
        return jnp.concatenate([total[pl.ds(0, step, stride=2), :], total[pl.ds(1, step, stride=2), :]], axis=1)

    steps = nodes // step
    keep(*begin(0))

    def one_step(i, carry):
        before, after = jnp.maximum(i - 1, 0), jnp.minimum(i + 1, steps - 1)
        summed, own_part, current = gathered(), earlier[...], later[...]
        result = finish(before, summed, own_part)
        begun = begin(after)
        for first in range(0, step // 4, GROUPS):
            sums = [group(pl.multiple_of(i * step, step), first + g) for g in range(GROUPS)]
            total[pl.ds(first * 8, GROUPS * 8), :] = jnp.concatenate(sums, axis=0)
        write(before, result)
        earlier[...] = current
        keep(*begun)
        return carry

    lax.fori_loop(0, steps, one_step, 0)
    write(steps - 1, finish(steps - 1, gathered(), earlier[...]))
    if segments is not None:
        move.wait()


def update(
    start, nodes, aux, arrays, sources, scales, params, places, table=None, segments=None, w_parent=None, coarse=()
):
    count, features = len(sources), arrays[0].shape[0]
    parents = aux.shape[0] - 1
    step = min(STEP, nodes)
    vmem = pl.BlockSpec(memory_space=pltpu.VMEM)
    smem = pl.BlockSpec(memory_space=pltpu.SMEM)
    far = pl.BlockSpec(memory_space=pltpu.HBM)
    out_shape = [jax.ShapeDtypeStruct((features, nodes), BF16)] * count
    operands = [places, aux.reshape(-1), *arrays, scales, *params]
    specs = [smem, far] + [far] * len(arrays) + [vmem] * (1 + len(params))
    scratch, table_step = [], 0
    if segments is None:
        operands, specs = operands + [table], specs + [far]
    else:
        operands, specs = operands + [w_parent, *coarse], specs + [vmem] + [far] * len(coarse)
        table_step = min(2048, segments[0][2])
        table = jax.ShapeDtypeStruct((2 * sum(segment[2] for segment in segments) + 2 * PAD, 128), F32)
        out_shape.append(table)
        scratch = [
            pltpu.VMEM((2, 2, w_parent.shape[0], table_step), BF16),
            pltpu.SemaphoreType.DMA((2, 2, len(segments[0][3]))),
        ]
    return pl.pallas_call(
        functools.partial(update_kernel, sources, step, start, segments, table_step),
        out_shape=out_shape,
        in_specs=specs,
        out_specs=[vmem] * count + [far] * (len(out_shape) - count),
        scratch_shapes=scratch
        + [
            pltpu.VMEM(table.shape, F32),
            pltpu.VMEM((count * features, nodes), BF16),
            pltpu.VMEM((2 * step, 128), F32),
            pltpu.VMEM((2 * step, 128), F32),
            pltpu.VMEM((step, 256), F32),
            pltpu.VMEM((step, 256), F32),
            pltpu.VMEM((2 * step, 8), F32),
            pltpu.SMEM((parents * nodes,), jnp.int32),
            pltpu.SMEM((1024,), jnp.int32),
            pltpu.SemaphoreType.DMA((parents + 2 + count,)),
        ],
        compiler_params=pltpu.CompilerParams(vmem_limit_bytes=40 << 20),
        cost_estimate=pl.CostEstimate(flops=nodes * 700000, bytes_accessed=nodes * 2048, transcendentals=nodes),
    )(*operands)


def after(value, *others):
    return lax.optimization_barrier((value, *others))[0]


def cut(array, at, size):
    return lax.dynamic_slice_in_dim(array, at, size, 1)


def plain(fine_latent, coarse_latent, aux, weights, w_parent, run):
    groups, domains = lax.axis_size("feat"), lax.axis_size("dom")
    rank = lax.axis_index("feat")
    per_device = fine_latent.shape[1] // groups
    length = per_device // CHUNKS
    forward = [(i, i + 1) for i in range(domains - 1)]
    backward = [(i + 1, i) for i in range(domains - 1)]

    def turn(value, r):
        return lax.ppermute(value, "feat", [(i, (i + r) % groups) for i in range(groups)])

    own = [coarse_latent] + [turn(coarse_latent, r) for r in range(1, groups)]
    low = [lax.ppermute(piece, "dom", forward) for piece in own]
    high = [lax.ppermute(piece, "dom", backward) for piece in own]
    first_row = rank * per_device
    rows = coarse_latent.shape[1]
    segments = [
        (w, 0, rows, [((w * groups + p,), 0) for p in range(groups)]) for w in range(3)
    ]
    making = dict(segments=segments, w_parent=w_parent, coarse=low + own + high)
    places = jnp.stack([0, 1, 2, 0, first_row]).astype(jnp.int32)
    sources = [((0, True),)] + [((r, False),) for r in range(1, groups)]
    aux = cut(aux, first_row, per_device)
    aux = jnp.concatenate([aux[:-1], aux[-1:] - first_row])
    weights = cut(weights, first_row, per_device)
    result = fine_latent
    arrived = []
    for c in range(CHUNKS):
        start = c * length
        pieces = [fine_latent]
        for r in range(1, groups):
            part = cut(fine_latent, ((rank + r) % groups) * per_device + start, length)
            pieces.append(turn(after(part, own[-1]), r))
        outs = run(start, length, aux, pieces, sources, weights, places, **(making if c == 0 else dict(table=table)))
        table = outs[-1] if c == 0 else table
        result = lax.dynamic_update_slice_in_dim(result, outs[0], first_row + start, 1)
        for r in range(1, groups):
            arrived.append((turn(outs[r], -r), ((rank + r) % groups) * per_device + start))
    for part, at in arrived:
        result = lax.dynamic_update_slice_in_dim(result, part, at, 1)
    return result


def paired(fine_latent, coarse_latent, aux, weights, w_parent, run):
    domains = lax.axis_size("dom")
    side, rank = lax.axis_index("dom") % 2, lax.axis_index("feat")
    matched = side == rank
    pairs = range(domains // 2)

    def send(value, moves):
        perm = [((2 * c + a) * 2 + b, (2 * c + x) * 2 + y) for c in pairs for (a, b), (x, y) in moves]
        return lax.ppermute(value, ("dom", "feat"), perm)

    def swap_rank(value):
        return send(value, [((k, f), (k, 1 - f)) for k in range(2) for f in range(2)])

    def swap_side(value):
        return send(value, [((k, f), (1 - k, f)) for k in range(2) for f in range(2)])

    def halo(value):
        perm = [((2 * c - 1) * 2, (2 * c) * 2) for c in pairs if c > 0]
        perm += [((2 * c + 2) * 2 + 1, (2 * c + 1) * 2 + 1) for c in pairs if c + 1 < len(pairs)]
        return lax.ppermute(value, ("dom", "feat"), perm)

    def hand_over(value):
        return send(value, [((0, 0), (1, 0)), ((1, 1), (0, 1))])

    to_first = [((0, 0), (1, 0)), ((1, 1), (0, 1)), ((0, 1), (0, 0)), ((1, 0), (1, 1))]
    from_first = [(b, a) for a, b in to_first]
    to_second = [((0, 1), (1, 0)), ((1, 0), (0, 1))]

    half = fine_latent.shape[1] // 2
    mine = side * half
    rows = coarse_latent.shape[1]
    mate = swap_rank(coarse_latent)
    halo_own, other = halo(coarse_latent), swap_side(after(coarse_latent, mate))
    halo_mate, other_mate = halo(mate), swap_side(mate)
    passed_own, passed_mate = hand_over(halo_own), hand_over(halo_mate)
    coarse = [coarse_latent, mate, other, other_mate, halo_own, passed_own, halo_mate, passed_mate]
    segments = [
        (0, 0, rows, [((0,), 0), ((1,), 0)]),
        (1, 0, rows, [((2,), 0), ((3,), 0)]),
        (2, 0, rows, [((4, 5), 0), ((6, 7), 0)]),
    ]
    places = jnp.stack([side + 1 - rank, 2 - side - rank, 2 * rank, jnp.where(matched, 0, 1), mine])
    places = places.astype(jnp.int32)

    length = half // CHUNKS
    chunks = []
    for c in range(CHUNKS):
        start = c * length
        first = cut(fine_latent, jnp.where(matched, half - mine, mine) + start, length)
        second = cut(fine_latent, half - mine + start, length)
        first, second = send(after(first, mate), to_first), send(after(second, mate), to_second)
        chunks.append([first, fine_latent, second])

    aux_local, aux_sent = cut(aux, mine, half), cut(aux, half - mine, half)
    aux = jnp.where(matched, aux_local, hand_over(aux_sent))
    aux = jnp.concatenate([aux[:-1], aux[-1:] - mine])
    weights = jnp.where(matched, cut(weights, mine, half), hand_over(cut(weights, half - mine, half)))

    making = dict(segments=segments, w_parent=w_parent, coarse=coarse)
    sources = [((0, False),), ((1, True), (2, False))]
    result = jnp.zeros_like(fine_latent)
    moved = []
    for c in range(CHUNKS):
        start = c * length
        out, kept, *made = run(
            start, length, aux, chunks[c], sources, weights, places, **(making if c == 0 else dict(table=table))
        )
        table = made[0] if made else table
        moved.append((start, kept, send(out, from_first), send(kept, to_second)))
    for start, kept, first, second in moved:
        result = lax.dynamic_update_slice_in_dim(result, jnp.where(matched, kept, first), mine + start, 1)
        result = lax.dynamic_update_slice_in_dim(
            result, jnp.where(matched, first, second), half - mine + start, 1
        )
    return result


def shards(
    fine_latent,
    coarse_latent,
    parents,
    interp_weights,
    live_rows,
    w_fine,
    w_parent,
    w_edge_out,
    w_node_fine,
    w_node_agg,
    w_node_out,
    edge_bias,
    node_bias,
    norm_gain,
    norm_bias,
):
    groups, domains = lax.axis_size("feat"), lax.axis_size("dom")
    rank = lax.axis_index("feat")
    own_features = fine_latent.shape[0]
    owners = [(rank - r) % groups for r in range(groups)]
    pairing = groups == 2 and domains % 2 == 0
    flip = jnp.where(lax.axis_index("dom") % 2 == rank, 1, 0) if pairing else 0

    def ordered(weight, axis, flip=flip):
        parts = [lax.dynamic_slice_in_dim(weight, o * own_features, own_features, axis) for o in owners]
        if pairing:
            parts = [jnp.where(flip == 1, parts[1], parts[0]), jnp.where(flip == 1, parts[0], parts[1])]
        return jnp.concatenate(parts, axis=axis)

    params = (
        jnp.concatenate([ordered(w_fine, 0), ordered(w_node_fine, 0)], axis=1),
        w_edge_out,
        w_node_agg,
        ordered(w_node_out, 1).T,
        jnp.concatenate([edge_bias, node_bias])[None],
        jnp.broadcast_to(ordered(norm_gain, 0)[:, None], (norm_gain.shape[0], STEP)),
        jnp.broadcast_to(ordered(norm_bias, 0)[:, None], (norm_bias.shape[0], STEP)),
    )

    def run(start, nodes, aux, arrays, sources, weights, places, **table):
        scales = jnp.pad(weights, ((0, 8 - weights.shape[0]), (0, 0)))
        return update(start, nodes, aux, arrays, sources, scales, params, places, **table)

    count = parents.shape[1]
    slots = 2 * parents + (PAD - 2 * (jnp.arange(count, dtype=jnp.int32) % 4))
    aux = jnp.concatenate([slots, jnp.broadcast_to(live_rows[:, None], (1, count))])
    plan = paired if pairing else plain
    return plan(fine_latent, coarse_latent, aux, interp_weights, ordered(w_parent, 0, 0), run)


def solution(mesh):
    in_specs = (P("feat", "dom"), P("feat", "dom"), P(None, "dom"), P(None, "dom"), P("dom")) + (P(),) * 10
    return jax.shard_map(shards, mesh=mesh, in_specs=in_specs, out_specs=P("feat", "dom"), check_vma=False)
```

```python
import functools

import jax
import jax.numpy as jnp
from jax import lax
from jax.experimental import pallas as pl
from jax.experimental.pallas import tpu as pltpu
from jax.sharding import PartitionSpec as P

F32 = jnp.float32
BF16 = jnp.bfloat16
PAD = 8
CHUNKS = 2
STEP = 256
GROUPS = 13


def dot(a, b, ca, cb):
    return lax.dot_general(a, b, (((ca,), (cb,)), ((), ())), preferred_element_type=F32)


def fill_table(segments, step, places, refs, weight, table, landed, sems):
    rows = (table.shape[0] - 2 * PAD) // 6
    features = landed.shape[2] // sems.shape[2]
    table[pl.ds(0, PAD), :] = jnp.zeros((PAD, 128), F32)
    table[pl.ds(PAD + 6 * rows, PAD), :] = jnp.zeros((PAD, 128), F32)

    def copies(segment, i, slot, which):
        found = []
        for p, (sources, first) in enumerate(segments[segment][3]):
            at = pl.multiple_of(first + i * step, 128)
            found.append(
                pltpu.make_async_copy(
                    refs[sources[min(which, len(sources) - 1)]].at[:, pl.ds(at, step)],
                    landed.at[segment % 2, slot, pl.ds(p * features, features), :],
                    sems.at[segment % 2, slot, p],
                )
            )
        return found

    def start(segment, i, slot):
        if all(len(sources) == 1 for sources, _ in segments[segment][3]):
            for copy in copies(segment, i, slot, 0):
                copy.start()
            return
        for which in range(2):

            @pl.when(places[3] == which)
            def _(which=which):
                for copy in copies(segment, i, slot, which):
                    copy.start()

    start(0, 0, 0)
    for segment, (window, row, length, _) in enumerate(segments):
        steps = length // step
        if segment + 1 < len(segments):
            start(segment + 1, 0, 0)

        def one(i, carry, segment=segment, window=window, row=row, steps=steps):
            slot = lax.rem(i, 2)

            @pl.when(i + 1 < steps)
            def _():
                start(segment, i + 1, 1 - slot)

            for copy in copies(segment, i, slot, 0):
                copy.wait()
            projected = dot(landed[segment % 2, slot], weight[...], 0, 0)
            base = pl.multiple_of(PAD + 2 * (places[window] * rows + row + i * step), 8)
            table[pl.ds(base, step, stride=2), :] = projected[:, :128]
            table[pl.ds(base + 1, step, stride=2), :] = projected[:, 128:]
            return carry

        lax.fori_loop(0, steps, one, 0)


def update_kernel(sources, step, start, segments, table_step, places, aux, *refs):
    count = len(sources)
    given = 1 + max(at for source in sources for at, _ in source)
    arrays, refs = refs[:given], refs[given:]
    scales, w_latent, w_edge, w_agg, w_out_t, bias, gain, shift = refs[:8]
    table, latents, fine, total, earlier, later, scale_rows, slots, live, sems = refs[-10:]
    refs = refs[8:-10]
    features, nodes = latents.shape[0] // count, latents.shape[1]
    parents = slots.shape[0] // nodes
    if segments is None:
        kept, outs = refs[0], refs[1:]
        move = pltpu.make_async_copy(kept, table, sems.at[parents + 1 + count])
        move.start()
    else:
        w_parent, *coarse = refs[: -count - 3]
        *outs, kept, landed, landed_sems = refs[-count - 3 :]
        move = pltpu.make_async_copy(table, kept, sems.at[parents + 1 + count])
    held = aux.shape[0] // (parents + 1)
    fetches = [
        pltpu.make_async_copy(aux.at[pl.ds(parents * start, parents * nodes)], slots, sems.at[0]),
    ]
    fetches.append(pltpu.make_async_copy(aux.at[pl.ds(parents * held, 1024)], live, sems.at[parents]))
    for fetch in fetches:
        fetch.start()

    def bring(p, which):
        at, shifted = sources[p][min(which, len(sources[p]) - 1)]
        column = pl.multiple_of(places[4] + start, 128) if shifted else 0
        return pltpu.make_async_copy(
            arrays[at].at[:, pl.ds(column, nodes)],
            latents.at[pl.ds(p * features, features), :],
            sems.at[parents + 1 + p],
        )

    for p, source in enumerate(sources):
        for which in range(len(source)):

            @pl.when((places[3] == which) | (len(source) == 1))
            def _(p=p, which=which):
                bring(p, which).start()

    if segments is not None:
        fill_table(segments, table_step, places, coarse, w_parent, table, landed, landed_sems)
        move.start()
    for fetch in fetches:
        fetch.wait()
    for p in range(count):
        bring(p, 0).wait()
    if segments is None:
        move.wait()
    sublane = lax.broadcasted_iota(jnp.int32, (8, 128), 0)
    owns = [sublane >= 2 * j for j in range(4)]

    def begin(i):
        columns = pl.ds(pl.multiple_of(i * step, step), step)
        first = dot(latents[:, columns], w_latent[...], 0, 0) + bias[...]
        return first, scales[:, pl.ds(pl.multiple_of(start + i * step, step), step)].T

    def keep(first, scale_columns):
        width = first.shape[1] // 2
        fine[pl.ds(0, step, stride=2), :] = first[:, :128]
        fine[pl.ds(1, step, stride=2), :] = first[:, 128:width]
        later[...] = first[:, width:]
        scale_rows[pl.ds(0, step, stride=2), :] = scale_columns
        scale_rows[pl.ds(1, step, stride=2), :] = scale_columns

    def group(at, g):
        part = fine[pl.ds(g * 8, 8), :]
        scale = scale_rows[pl.ds(g * 8, 8), :]
        acc = None
        for k in range(parents):
            rows = None
            for j in range(4):
                loaded = table[pl.ds(slots[at + (k * step + g * 4 + j)], 8), :]
                rows = loaded if rows is None else jnp.where(owns[j], loaded, rows)
            hidden = jnp.maximum(part + rows, 0.0) * scale[:, k : k + 1]
            acc = hidden if acc is None else acc + hidden
        return acc

    def finish(i, summed, own_part):
        at = pl.multiple_of(i * step, step)
        aggregate = dot(summed.astype(BF16), w_edge[...], 1, 0).astype(BF16)
        yield
        node_hidden = jnp.maximum(own_part + dot(aggregate, w_agg[...], 1, 0), 0.0).astype(BF16)
        yield
        output = dot(w_out_t[...], node_hidden, 1, 1)
        yield
        centered = output - jnp.mean(output, axis=0, keepdims=True)
        spread = jnp.mean(centered * centered, axis=0, keepdims=True)
        yield
        normed = centered * lax.rsqrt(spread + 1e-05) * gain[...] + shift[...]
        column = start + at + lax.broadcasted_iota(jnp.int32, (1, step), 1)
        moved = jnp.where(column < live[0], normed, 0.0)
        yield (latents[:, pl.ds(at, step)].astype(F32) + moved).astype(BF16)

    def last(parts):
        for value in parts:
            pass
        return value

    def write(i, result):
        for r in range(count):
            outs[r][:, pl.ds(pl.multiple_of(i * step, step), step)] = result[r * features : (r + 1) * features]

    def gathered():
        return jnp.concatenate([total[pl.ds(0, step, stride=2), :], total[pl.ds(1, step, stride=2), :]], axis=1)

    steps = nodes // step
    keep(*begin(0))

    def one_step(i, carry):
        before, after = jnp.maximum(i - 1, 0), jnp.minimum(i + 1, steps - 1)
        summed, own_part, current = gathered(), earlier[...], later[...]
        parts = finish(before, summed, own_part)
        base = pl.multiple_of(i * (parents * step), parents * step)
        begun = begin(after)
        for first in range(0, step // 4, GROUPS):
            result = next(parts, None) if first < 4 * GROUPS else last(parts)
            sums = [group(base, g) for g in range(first, min(first + GROUPS, step // 4))]
            total[pl.ds(first * 8, len(sums) * 8), :] = jnp.concatenate(sums, axis=0)
        write(before, result)
        earlier[...] = current
        keep(*begun)
        return carry

    lax.fori_loop(0, steps, one_step, 0)
    write(steps - 1, last(finish(steps - 1, gathered(), earlier[...])))
    if segments is not None:
        move.wait()


def by_step(aux, step):
    slots = aux[:-1].reshape(aux.shape[0] - 1, -1, step).transpose(1, 0, 2)
    return jnp.concatenate([slots.reshape(-1), aux[-1]])


def update(
    start, nodes, aux, arrays, sources, scales, params, places, table=None, segments=None, w_parent=None, coarse=()
):
    count, features = len(sources), arrays[0].shape[0]
    parents = aux.shape[0] - 1
    step = min(STEP, nodes)
    vmem = pl.BlockSpec(memory_space=pltpu.VMEM)
    smem = pl.BlockSpec(memory_space=pltpu.SMEM)
    far = pl.BlockSpec(memory_space=pltpu.HBM)
    out_shape = [jax.ShapeDtypeStruct((features, nodes), BF16)] * count
    operands = [places, by_step(aux, step), *arrays, scales, *params]
    specs = [smem, far] + [far] * len(arrays) + [vmem] * (1 + len(params))
    scratch, table_step = [], 0
    if segments is None:
        operands, specs = operands + [table], specs + [far]
    else:
        operands, specs = operands + [w_parent, *coarse], specs + [vmem] + [far] * len(coarse)
        table_step = min(2048, segments[0][2])
        table = jax.ShapeDtypeStruct((2 * sum(segment[2] for segment in segments) + 2 * PAD, 128), F32)
        out_shape.append(table)
        scratch = [
            pltpu.VMEM((2, 2, w_parent.shape[0], table_step), BF16),
            pltpu.SemaphoreType.DMA((2, 2, len(segments[0][3]))),
        ]
    return pl.pallas_call(
        functools.partial(update_kernel, sources, step, start, segments, table_step),
        out_shape=out_shape,
        in_specs=specs,
        out_specs=[vmem] * count + [far] * (len(out_shape) - count),
        scratch_shapes=scratch
        + [
            pltpu.VMEM(table.shape, F32),
            pltpu.VMEM((count * features, nodes), BF16),
            pltpu.VMEM((2 * step, 128), F32),
            pltpu.VMEM((2 * step, 128), F32),
            pltpu.VMEM((step, 256), F32),
            pltpu.VMEM((step, 256), F32),
            pltpu.VMEM((2 * step, 8), F32),
            pltpu.SMEM((parents * nodes,), jnp.int32),
            pltpu.SMEM((1024,), jnp.int32),
            pltpu.SemaphoreType.DMA((parents + 2 + count,)),
        ],
        compiler_params=pltpu.CompilerParams(vmem_limit_bytes=40 << 20),
        cost_estimate=pl.CostEstimate(flops=nodes * 700000, bytes_accessed=nodes * 2048, transcendentals=nodes),
    )(*operands)


def after(value, *others):
    return lax.optimization_barrier((value, *others))[0]


def cut(array, at, size):
    return lax.dynamic_slice_in_dim(array, at, size, 1)


def plain(fine_latent, coarse_latent, aux, weights, w_parent, run):
    groups, domains = lax.axis_size("feat"), lax.axis_size("dom")
    rank = lax.axis_index("feat")
    per_device = fine_latent.shape[1] // groups
    length = per_device // CHUNKS
    forward = [(i, i + 1) for i in range(domains - 1)]
    backward = [(i + 1, i) for i in range(domains - 1)]

    def turn(value, r):
        return lax.ppermute(value, "feat", [(i, (i + r) % groups) for i in range(groups)])

    own = [coarse_latent] + [turn(coarse_latent, r) for r in range(1, groups)]
    low = [lax.ppermute(piece, "dom", forward) for piece in own]
    high = [lax.ppermute(piece, "dom", backward) for piece in own]
    first_row = rank * per_device
    rows = coarse_latent.shape[1]
    segments = [
        (w, 0, rows, [((w * groups + p,), 0) for p in range(groups)]) for w in range(3)
    ]
    making = dict(segments=segments, w_parent=w_parent, coarse=low + own + high)
    places = jnp.stack([0, 1, 2, 0, first_row]).astype(jnp.int32)
    sources = [((0, True),)] + [((r, False),) for r in range(1, groups)]
    aux = cut(aux, first_row, per_device)
    aux = jnp.concatenate([aux[:-1], aux[-1:] - first_row])
    weights = cut(weights, first_row, per_device)
    result = fine_latent
    arrived = []
    for c in range(CHUNKS):
        start = c * length
        pieces = [fine_latent]
        for r in range(1, groups):
            part = cut(fine_latent, ((rank + r) % groups) * per_device + start, length)
            pieces.append(turn(after(part, own[-1]), r))
        outs = run(start, length, aux, pieces, sources, weights, places, **(making if c == 0 else dict(table=table)))
        table = outs[-1] if c == 0 else table
        result = lax.dynamic_update_slice_in_dim(result, outs[0], first_row + start, 1)
        for r in range(1, groups):
            arrived.append((turn(outs[r], -r), ((rank + r) % groups) * per_device + start))
    for part, at in arrived:
        result = lax.dynamic_update_slice_in_dim(result, part, at, 1)
    return result


def paired(fine_latent, coarse_latent, aux, weights, w_parent, run):
    domains = lax.axis_size("dom")
    side, rank = lax.axis_index("dom") % 2, lax.axis_index("feat")
    matched = side == rank
    pairs = range(domains // 2)

    def send(value, moves):
        perm = [((2 * c + a) * 2 + b, (2 * c + x) * 2 + y) for c in pairs for (a, b), (x, y) in moves]
        return lax.ppermute(value, ("dom", "feat"), perm)

    def swap_rank(value):
        return send(value, [((k, f), (k, 1 - f)) for k in range(2) for f in range(2)])

    def swap_side(value):
        return send(value, [((k, f), (1 - k, f)) for k in range(2) for f in range(2)])

    def halo(value):
        perm = [((2 * c - 1) * 2, (2 * c) * 2) for c in pairs if c > 0]
        perm += [((2 * c + 2) * 2 + 1, (2 * c + 1) * 2 + 1) for c in pairs if c + 1 < len(pairs)]
        return lax.ppermute(value, ("dom", "feat"), perm)

    def hand_over(value):
        return send(value, [((0, 0), (1, 0)), ((1, 1), (0, 1))])

    to_first = [((0, 0), (1, 0)), ((1, 1), (0, 1)), ((0, 1), (0, 0)), ((1, 0), (1, 1))]
    from_first = [(b, a) for a, b in to_first]
    to_second = [((0, 1), (1, 0)), ((1, 0), (0, 1))]

    half = fine_latent.shape[1] // 2
    mine = side * half
    rows = coarse_latent.shape[1]
    mate = swap_rank(coarse_latent)
    halo_own, other = halo(coarse_latent), swap_side(after(coarse_latent, mate))
    halo_mate, other_mate = halo(mate), swap_side(mate)
    passed_own, passed_mate = hand_over(halo_own), hand_over(halo_mate)
    coarse = [coarse_latent, mate, other, other_mate, halo_own, passed_own, halo_mate, passed_mate]
    segments = [
        (0, 0, rows, [((0,), 0), ((1,), 0)]),
        (1, 0, rows, [((2,), 0), ((3,), 0)]),
        (2, 0, rows, [((4, 5), 0), ((6, 7), 0)]),
    ]
    places = jnp.stack([side + 1 - rank, 2 - side - rank, 2 * rank, jnp.where(matched, 0, 1), mine])
    places = places.astype(jnp.int32)

    length = half // CHUNKS
    chunks = []
    for c in range(CHUNKS):
        start = c * length
        first = cut(fine_latent, jnp.where(matched, half - mine, mine) + start, length)
        second = cut(fine_latent, half - mine + start, length)
        first, second = send(after(first, mate), to_first), send(after(second, mate), to_second)
        chunks.append([first, fine_latent, second])

    aux_local, aux_sent = cut(aux, mine, half), cut(aux, half - mine, half)
    aux = jnp.where(matched, aux_local, hand_over(aux_sent))
    aux = jnp.concatenate([aux[:-1], aux[-1:] - mine])
    weights = jnp.where(matched, cut(weights, mine, half), hand_over(cut(weights, half - mine, half)))

    making = dict(segments=segments, w_parent=w_parent, coarse=coarse)
    sources = [((0, False),), ((1, True), (2, False))]
    result = jnp.zeros_like(fine_latent)
    moved = []
    for c in range(CHUNKS):
        start = c * length
        out, kept, *made = run(
            start, length, aux, chunks[c], sources, weights, places, **(making if c == 0 else dict(table=table))
        )
        table = made[0] if made else table
        moved.append((start, kept, send(out, from_first), send(kept, to_second)))
    for start, kept, first, second in moved:
        result = lax.dynamic_update_slice_in_dim(result, jnp.where(matched, kept, first), mine + start, 1)
        result = lax.dynamic_update_slice_in_dim(
            result, jnp.where(matched, first, second), half - mine + start, 1
        )
    return result


def shards(
    fine_latent,
    coarse_latent,
    parents,
    interp_weights,
    live_rows,
    w_fine,
    w_parent,
    w_edge_out,
    w_node_fine,
    w_node_agg,
    w_node_out,
    edge_bias,
    node_bias,
    norm_gain,
    norm_bias,
):
    groups, domains = lax.axis_size("feat"), lax.axis_size("dom")
    rank = lax.axis_index("feat")
    own_features = fine_latent.shape[0]
    owners = [(rank - r) % groups for r in range(groups)]
    pairing = groups == 2 and domains % 2 == 0
    flip = jnp.where(lax.axis_index("dom") % 2 == rank, 1, 0) if pairing else 0

    def ordered(weight, axis, flip=flip):
        parts = [lax.dynamic_slice_in_dim(weight, o * own_features, own_features, axis) for o in owners]
        if pairing:
            parts = [jnp.where(flip == 1, parts[1], parts[0]), jnp.where(flip == 1, parts[0], parts[1])]
        return jnp.concatenate(parts, axis=axis)

    params = (
        jnp.concatenate([ordered(w_fine, 0), ordered(w_node_fine, 0)], axis=1),
        w_edge_out,
        w_node_agg,
        ordered(w_node_out, 1).T,
        jnp.concatenate([edge_bias, node_bias])[None],
        jnp.broadcast_to(ordered(norm_gain, 0)[:, None], (norm_gain.shape[0], STEP)),
        jnp.broadcast_to(ordered(norm_bias, 0)[:, None], (norm_bias.shape[0], STEP)),
    )

    def run(start, nodes, aux, arrays, sources, weights, places, **table):
        scales = jnp.pad(weights, ((0, 8 - weights.shape[0]), (0, 0)))
        return update(start, nodes, aux, arrays, sources, scales, params, places, **table)

    count = parents.shape[1]
    slots = 2 * parents + (PAD - 2 * (jnp.arange(count, dtype=jnp.int32) % 4))
    aux = jnp.concatenate([slots, jnp.broadcast_to(live_rows[:, None], (1, count))])
    plan = paired if pairing else plain
    return plan(fine_latent, coarse_latent, aux, interp_weights, ordered(w_parent, 0, 0), run)


def solution(mesh):
    in_specs = (P("feat", "dom"), P("feat", "dom"), P(None, "dom"), P(None, "dom"), P("dom")) + (P(),) * 10
    return jax.shard_map(shards, mesh=mesh, in_specs=in_specs, out_specs=P("feat", "dom"), check_vma=False)
```

```python
import functools

import jax
import jax.numpy as jnp
from jax import lax
from jax.experimental import pallas as pl
from jax.experimental.pallas import tpu as pltpu
from jax.sharding import PartitionSpec as P

F32 = jnp.float32
BF16 = jnp.bfloat16
PAD = 8
SHARE = 4
PARTS = 2
STEP = 256
GROUPS = 13


def dot(a, b, ca, cb):
    return lax.dot_general(a, b, (((ca,), (cb,)), ((), ())), preferred_element_type=F32)


def fill_table(segments, step, places, refs, weight, table, landed, sems):
    rows = (table.shape[0] - 2 * PAD) // 6
    features = landed.shape[2] // sems.shape[2]
    table[pl.ds(0, PAD), :] = jnp.zeros((PAD, 128), F32)
    table[pl.ds(PAD + 6 * rows, PAD), :] = jnp.zeros((PAD, 128), F32)

    def copies(segment, i, slot, which):
        found = []
        for p, (sources, first) in enumerate(segments[segment][3]):
            at = pl.multiple_of(first + i * step, 128)
            found.append(
                pltpu.make_async_copy(
                    refs[sources[min(which, len(sources) - 1)]].at[:, pl.ds(at, step)],
                    landed.at[segment % 2, slot, pl.ds(p * features, features), :],
                    sems.at[segment % 2, slot, p],
                )
            )
        return found

    def start(segment, i, slot):
        if all(len(sources) == 1 for sources, _ in segments[segment][3]):
            for copy in copies(segment, i, slot, 0):
                copy.start()
            return
        for which in range(2):

            @pl.when(places[3] == which)
            def _(which=which):
                for copy in copies(segment, i, slot, which):
                    copy.start()

    start(0, 0, 0)
    for segment, (window, row, length, _) in enumerate(segments):
        steps = length // step
        if segment + 1 < len(segments):
            start(segment + 1, 0, 0)

        def one(i, carry, segment=segment, window=window, row=row, steps=steps):
            slot = lax.rem(i, 2)

            @pl.when(i + 1 < steps)
            def _():
                start(segment, i + 1, 1 - slot)

            for copy in copies(segment, i, slot, 0):
                copy.wait()
            projected = dot(landed[segment % 2, slot], weight[...], 0, 0)
            base = pl.multiple_of(PAD + 2 * (places[window] * rows + row + i * step), 8)
            table[pl.ds(base, step, stride=2), :] = projected[:, :128]
            table[pl.ds(base + 1, step, stride=2), :] = projected[:, 128:]
            return carry

        lax.fori_loop(0, steps, one, 0)


def update_kernel(sources, step, start, segments, table_step, places, aux, *refs):
    count = len(sources)
    given = 1 + max(at for source in sources for at, _ in source)
    arrays, refs = refs[:given], refs[given:]
    given, refs = refs[:8], refs[8:]
    held_here, refs = refs[-8:], refs[:-8]
    scales, w_latent, w_edge, w_agg, w_out_t, bias, gain, shift = held_here
    table, latents, fine, total, earlier, later, scale_rows, slots, live, sems, given_sems = refs[-11:]
    refs = refs[:-11]
    fetches = [
        pltpu.make_async_copy(far if at else far.at[:, pl.ds(start, near.shape[1])], near, given_sems.at[at])
        for at, (far, near) in enumerate(zip(given, held_here))
    ]
    features, nodes = latents.shape[0] // count, latents.shape[1]
    parents = slots.shape[0] // nodes
    if segments is None:
        kept, outs = refs[0], refs[1:]
        move = pltpu.make_async_copy(kept, table, sems.at[parents + 1 + count])
        move.start()
    else:
        w_parent, *coarse = refs[: -count - 3]
        *outs, kept, landed, landed_sems = refs[-count - 3 :]
        move = pltpu.make_async_copy(table, kept, sems.at[parents + 1 + count])
    held = aux.shape[0] // (parents + 1)
    fetches.append(pltpu.make_async_copy(aux.at[pl.ds(parents * start, parents * nodes)], slots, sems.at[0]))
    fetches.append(pltpu.make_async_copy(aux.at[pl.ds(parents * held, 1024)], live, sems.at[parents]))
    for fetch in fetches:
        fetch.start()

    def bring(p, which):
        at, shifted = sources[p][min(which, len(sources[p]) - 1)]
        column = pl.multiple_of(places[4] + start, 128) if shifted else 0
        return pltpu.make_async_copy(
            arrays[at].at[:, pl.ds(column, nodes)],
            latents.at[pl.ds(p * features, features), :],
            sems.at[parents + 1 + p],
        )

    for p, source in enumerate(sources):
        for which in range(len(source)):

            @pl.when((places[3] == which) | (len(source) == 1))
            def _(p=p, which=which):
                bring(p, which).start()

    if segments is not None:
        fill_table(segments, table_step, places, coarse, w_parent, table, landed, landed_sems)
        move.start()
    for fetch in fetches:
        fetch.wait()
    for p in range(count):
        bring(p, 0).wait()
    if segments is None:
        move.wait()
    sublane = lax.broadcasted_iota(jnp.int32, (8, 128), 0)
    owns = [sublane >= 2 * j for j in range(4)]

    def begin(i):
        columns = pl.ds(pl.multiple_of(i * step, step), step)
        first = dot(latents[:, columns], w_latent[...], 0, 0) + bias[...]
        return first, scales[:, pl.ds(pl.multiple_of(i * step, step), step)].T

    def keep(first, scale_columns):
        width = first.shape[1] // 2
        fine[pl.ds(0, step, stride=2), :] = first[:, :128]
        fine[pl.ds(1, step, stride=2), :] = first[:, 128:width]
        later[...] = first[:, width:]
        scale_rows[pl.ds(0, step, stride=2), :] = scale_columns
        scale_rows[pl.ds(1, step, stride=2), :] = scale_columns

    def group(at, g):
        part = fine[pl.ds(g * 8, 8), :]
        scale = scale_rows[pl.ds(g * 8, 8), :]
        acc = None
        for k in range(parents):
            rows = None
            for j in range(4):
                loaded = table[pl.ds(slots[at + (k * step + g * 4 + j)], 8), :]
                rows = loaded if rows is None else jnp.where(owns[j], loaded, rows)
            hidden = jnp.maximum(part + rows, 0.0) * scale[:, k : k + 1]
            acc = hidden if acc is None else acc + hidden
        return acc

    def widened(ref):
        return jnp.concatenate([ref[...]] * (step // 128), axis=1)

    def finish(i, summed, own_part):
        at = pl.multiple_of(i * step, step)
        aggregate = dot(summed.astype(BF16), w_edge[...], 1, 0).astype(BF16)
        yield
        node_hidden = jnp.maximum(own_part + dot(aggregate, w_agg[...], 1, 0), 0.0).astype(BF16)
        yield
        output = dot(w_out_t[...], node_hidden, 1, 1)
        yield
        centered = output - jnp.mean(output, axis=0, keepdims=True)
        spread = jnp.mean(centered * centered, axis=0, keepdims=True)
        yield
        normed = centered * lax.rsqrt(spread + 1e-05) * widened(gain) + widened(shift)
        column = start + at + lax.broadcasted_iota(jnp.int32, (1, step), 1)
        moved = jnp.where(column < live[0], normed, 0.0)
        yield (latents[:, pl.ds(at, step)].astype(F32) + moved).astype(BF16)

    def last(parts):
        for value in parts:
            pass
        return value

    def write(i, result):
        for r in range(count):
            outs[r][:, pl.ds(pl.multiple_of(i * step, step), step)] = result[r * features : (r + 1) * features]

    def gathered():
        return jnp.concatenate([total[pl.ds(0, step, stride=2), :], total[pl.ds(1, step, stride=2), :]], axis=1)

    steps = nodes // step
    keep(*begin(0))

    def one_step(i, carry):
        before, after = jnp.maximum(i - 1, 0), jnp.minimum(i + 1, steps - 1)
        summed, own_part, current = gathered(), earlier[...], later[...]
        parts = finish(before, summed, own_part)
        base = pl.multiple_of(i * (parents * step), parents * step)
        begun = begin(after)
        for first in range(0, step // 4, GROUPS):
            result = next(parts, None) if first < 4 * GROUPS else last(parts)
            sums = [group(base, g) for g in range(first, min(first + GROUPS, step // 4))]
            total[pl.ds(first * 8, len(sums) * 8), :] = jnp.concatenate(sums, axis=0)
        write(before, result)
        earlier[...] = current
        keep(*begun)
        return carry

    lax.fori_loop(0, steps, one_step, 0)
    write(steps - 1, last(finish(steps - 1, gathered(), earlier[...])))
    if segments is not None:
        move.wait()


def by_step(aux, step):
    slots = aux[:-1].reshape(aux.shape[0] - 1, -1, step).transpose(1, 0, 2)
    return jnp.concatenate([slots.reshape(-1), aux[-1]])


def update(
    start, nodes, aux, arrays, sources, scales, params, places, table=None, segments=None, w_parent=None, coarse=()
):
    count, features = len(sources), arrays[0].shape[0]
    parents = aux.shape[0] - 1
    step = min(STEP, nodes)
    vmem = pl.BlockSpec(memory_space=pltpu.VMEM)
    smem = pl.BlockSpec(memory_space=pltpu.SMEM)
    far = pl.BlockSpec(memory_space=pltpu.HBM)
    out_shape = [jax.ShapeDtypeStruct((features, nodes), BF16)] * count
    operands = [places, by_step(aux, step), *arrays, scales, *params]
    specs = [smem, far] + [far] * (len(arrays) + 1 + len(params))
    scratch, table_step = [], 0
    if segments is None:
        operands, specs = operands + [table], specs + [far]
    else:
        operands, specs = operands + [w_parent, *coarse], specs + [vmem] + [far] * len(coarse)
        table_step = min(2048, segments[0][2])
        table = jax.ShapeDtypeStruct((2 * sum(segment[2] for segment in segments) + 2 * PAD, 128), F32)
        out_shape.append(table)
        scratch = [
            pltpu.VMEM((2, 2, w_parent.shape[0], table_step), BF16),
            pltpu.SemaphoreType.DMA((2, 2, len(segments[0][3]))),
        ]
    return pl.pallas_call(
        functools.partial(update_kernel, sources, step, start, segments, table_step),
        out_shape=out_shape,
        in_specs=specs,
        out_specs=[vmem] * count + [far] * (len(out_shape) - count),
        scratch_shapes=scratch
        + [
            pltpu.VMEM(table.shape, F32),
            pltpu.VMEM((count * features, nodes), BF16),
            pltpu.VMEM((2 * step, 128), F32),
            pltpu.VMEM((2 * step, 128), F32),
            pltpu.VMEM((step, 256), F32),
            pltpu.VMEM((step, 256), F32),
            pltpu.VMEM((2 * step, 8), F32),
            pltpu.SMEM((parents * nodes,), jnp.int32),
            pltpu.SMEM((1024,), jnp.int32),
            pltpu.SemaphoreType.DMA((parents + 2 + count,)),
            pltpu.SemaphoreType.DMA((1 + len(params),)),
            pltpu.VMEM((scales.shape[0], nodes), F32),
        ]
        + [pltpu.VMEM(param.shape, param.dtype) for param in params],
        compiler_params=pltpu.CompilerParams(vmem_limit_bytes=40 << 20),
        cost_estimate=pl.CostEstimate(flops=nodes * 700000, bytes_accessed=nodes * 2048, transcendentals=nodes),
    )(*operands)


def after(value, *others):
    return lax.optimization_barrier((value, *others))[0]


def shares(nodes):
    first = nodes * SHARE // 8 // STEP * STEP
    return [(0, first), (first, nodes - first)]


def cut(array, at, size):
    return lax.dynamic_slice_in_dim(array, at, size, 1)


def plain(fine_latent, coarse_latent, aux, weights, w_parent, run):
    groups, domains = lax.axis_size("feat"), lax.axis_size("dom")
    rank = lax.axis_index("feat")
    per_device = fine_latent.shape[1] // groups
    forward = [(i, i + 1) for i in range(domains - 1)]
    backward = [(i + 1, i) for i in range(domains - 1)]

    def turn(value, r):
        return lax.ppermute(value, "feat", [(i, (i + r) % groups) for i in range(groups)])

    own = [coarse_latent] + [turn(coarse_latent, r) for r in range(1, groups)]
    low = [lax.ppermute(piece, "dom", forward) for piece in own]
    high = [lax.ppermute(piece, "dom", backward) for piece in own]
    first_row = rank * per_device
    rows = coarse_latent.shape[1]
    segments = [
        (w, 0, rows, [((w * groups + p,), 0) for p in range(groups)]) for w in range(3)
    ]
    making = dict(segments=segments, w_parent=w_parent, coarse=low + own + high)
    places = jnp.stack([0, 1, 2, 0, first_row]).astype(jnp.int32)
    sources = [((0, True),)] + [((r, False),) for r in range(1, groups)]
    aux = cut(aux, first_row, per_device)
    aux = jnp.concatenate([aux[:-1], aux[-1:] - first_row])
    weights = cut(weights, first_row, per_device)
    result = fine_latent
    arrived = []
    for c, (start, length) in enumerate(shares(per_device)):
        pieces = [fine_latent]
        for r in range(1, groups):
            part = cut(fine_latent, ((rank + r) % groups) * per_device + start, length)
            pieces.append(turn(after(part, own[-1]), r))
        outs = run(start, length, aux, pieces, sources, weights, places, **(making if c == 0 else dict(table=table)))
        table = outs[-1] if c == 0 else table
        result = lax.dynamic_update_slice_in_dim(result, outs[0], first_row + start, 1)
        for r in range(1, groups):
            arrived.append((turn(outs[r], -r), ((rank + r) % groups) * per_device + start))
    for part, at in arrived:
        result = lax.dynamic_update_slice_in_dim(result, part, at, 1)
    return result


def paired(fine_latent, coarse_latent, aux, weights, w_parent, run):
    domains = lax.axis_size("dom")
    side, rank = lax.axis_index("dom") % 2, lax.axis_index("feat")
    matched = side == rank
    pairs = range(domains // 2)

    def send(value, moves):
        perm = [((2 * c + a) * 2 + b, (2 * c + x) * 2 + y) for c in pairs for (a, b), (x, y) in moves]
        return lax.ppermute(value, ("dom", "feat"), perm)

    def swap_rank(value):
        return send(value, [((k, f), (k, 1 - f)) for k in range(2) for f in range(2)])

    def swap_side(value):
        return send(value, [((k, f), (1 - k, f)) for k in range(2) for f in range(2)])

    def halo(value):
        perm = [((2 * c - 1) * 2, (2 * c) * 2) for c in pairs if c > 0]
        perm += [((2 * c + 2) * 2 + 1, (2 * c + 1) * 2 + 1) for c in pairs if c + 1 < len(pairs)]
        return lax.ppermute(value, ("dom", "feat"), perm)

    def hand_over(value):
        return send(value, [((0, 0), (1, 0)), ((1, 1), (0, 1))])

    to_first = [((0, 0), (1, 0)), ((1, 1), (0, 1)), ((0, 1), (0, 0)), ((1, 0), (1, 1))]
    from_first = [(b, a) for a, b in to_first]
    to_second = [((0, 1), (1, 0)), ((1, 0), (0, 1))]

    half = fine_latent.shape[1] // 2
    mine = side * half
    rows = coarse_latent.shape[1]
    part = rows // PARTS
    mate = []
    for i in range(PARTS):
        piece = lax.slice_in_dim(coarse_latent, i * part, (i + 1) * part, axis=1)
        mate.append(swap_rank(after(piece, mate[-1]) if mate else piece))
    halo_own, other = halo(coarse_latent), swap_side(after(coarse_latent, mate[-1]))
    halo_mate, other_mate = [halo(piece) for piece in mate], [swap_side(piece) for piece in mate]
    passed_own, passed_mate = hand_over(halo_own), [hand_over(piece) for piece in halo_mate]
    coarse = [coarse_latent, other, halo_own, passed_own, *mate, *other_mate, *halo_mate, *passed_mate]
    segments = []
    for window, own in enumerate([(0,), (1,), (2, 3)]):
        for i in range(PARTS):
            came = tuple(4 + (w + window) * PARTS + i for w in range(len(own)))
            segments.append((window, i * part, part, [(own, i * part), (came, 0)]))
    places = jnp.stack([side + 1 - rank, 2 - side - rank, 2 * rank, jnp.where(matched, 0, 1), mine])
    places = places.astype(jnp.int32)

    chunks = []
    for c, (start, length) in enumerate(shares(half)):
        first = cut(fine_latent, jnp.where(matched, half - mine, mine) + start, length)
        second = cut(fine_latent, half - mine + start, length)
        first, second = send(after(first, mate[-1]), to_first), send(after(second, mate[-1]), to_second)
        chunks.append([first, fine_latent, second])

    both = jnp.concatenate([aux.astype(F32), weights])
    both = jnp.where(matched, cut(both, mine, half), hand_over(cut(both, half - mine, half)))
    aux, weights = both[: aux.shape[0]].astype(jnp.int32), both[aux.shape[0] :]
    aux = jnp.concatenate([aux[:-1], aux[-1:] - mine])

    making = dict(segments=segments, w_parent=w_parent, coarse=coarse)
    sources = [((0, False),), ((1, True), (2, False))]
    result = jnp.zeros_like(fine_latent)
    moved = []
    for c, (start, length) in enumerate(shares(half)):
        out, kept, *made = run(
            start, length, aux, chunks[c], sources, weights, places, **(making if c == 0 else dict(table=table))
        )
        table = made[0] if made else table
        moved.append((start, kept, send(out, from_first), send(kept, to_second)))
    for start, kept, first, second in moved:
        result = lax.dynamic_update_slice_in_dim(result, jnp.where(matched, kept, first), mine + start, 1)
        result = lax.dynamic_update_slice_in_dim(
            result, jnp.where(matched, first, second), half - mine + start, 1
        )
    return result


def shards(
    fine_latent,
    coarse_latent,
    parents,
    interp_weights,
    live_rows,
    w_fine,
    w_parent,
    w_edge_out,
    w_node_fine,
    w_node_agg,
    w_node_out,
    edge_bias,
    node_bias,
    norm_gain,
    norm_bias,
):
    groups, domains = lax.axis_size("feat"), lax.axis_size("dom")
    rank = lax.axis_index("feat")
    own_features = fine_latent.shape[0]
    owners = [(rank - r) % groups for r in range(groups)]
    pairing = groups == 2 and domains % 2 == 0
    flip = jnp.where(lax.axis_index("dom") % 2 == rank, 1, 0) if pairing else 0

    def ordered(weight, axis, flip=flip):
        parts = [lax.dynamic_slice_in_dim(weight, o * own_features, own_features, axis) for o in owners]
        if pairing:
            parts = [jnp.where(flip == 1, parts[1], parts[0]), jnp.where(flip == 1, parts[0], parts[1])]
        return jnp.concatenate(parts, axis=axis)

    params = (
        jnp.concatenate([ordered(w_fine, 0), ordered(w_node_fine, 0)], axis=1),
        w_edge_out,
        w_node_agg,
        ordered(w_node_out, 1).T,
        jnp.concatenate([edge_bias, node_bias])[None],
        jnp.broadcast_to(ordered(norm_gain, 0)[:, None], (norm_gain.shape[0], 128)),
        jnp.broadcast_to(ordered(norm_bias, 0)[:, None], (norm_bias.shape[0], 128)),
    )

    def run(start, nodes, aux, arrays, sources, weights, places, **table):
        scales = jnp.pad(weights, ((0, 8 - weights.shape[0]), (0, 0)))
        return update(start, nodes, aux, arrays, sources, scales, params, places, **table)

    count = parents.shape[1]
    slots = 2 * parents + (PAD - 2 * (jnp.arange(count, dtype=jnp.int32) % 4))
    aux = jnp.concatenate([slots, jnp.broadcast_to(live_rows[:, None], (1, count))])
    plan = paired if pairing else plain
    return plan(fine_latent, coarse_latent, aux, interp_weights, ordered(w_parent, 0, 0), run)


def solution(mesh):
    in_specs = (P("feat", "dom"), P("feat", "dom"), P(None, "dom"), P(None, "dom"), P("dom")) + (P(),) * 10
    return jax.shard_map(shards, mesh=mesh, in_specs=in_specs, out_specs=P("feat", "dom"), check_vma=False)
```

```python
import functools

import jax
import jax.numpy as jnp
from jax import lax
from jax.experimental import pallas as pl
from jax.experimental.pallas import tpu as pltpu
from jax.sharding import PartitionSpec as P

F32 = jnp.float32
BF16 = jnp.bfloat16
PAD = 8
SHARE = 4
PARTS = 1
STEP = 256
GROUPS = 13


def dot(a, b, ca, cb):
    return lax.dot_general(a, b, (((ca,), (cb,)), ((), ())), preferred_element_type=F32)


def fill_table(segments, step, places, refs, weight, table, landed, sems):
    rows = (table.shape[0] - 2 * PAD) // 6
    features = landed.shape[2] // sems.shape[2]
    table[pl.ds(0, PAD), :] = jnp.zeros((PAD, 128), F32)
    table[pl.ds(PAD + 6 * rows, PAD), :] = jnp.zeros((PAD, 128), F32)

    def copies(segment, i, slot, which):
        found = []
        for p, (sources, first) in enumerate(segments[segment][3]):
            at = pl.multiple_of(first + i * step, 128)
            found.append(
                pltpu.make_async_copy(
                    refs[sources[min(which, len(sources) - 1)]].at[:, pl.ds(at, step)],
                    landed.at[segment % 2, slot, pl.ds(p * features, features), :],
                    sems.at[segment % 2, slot, p],
                )
            )
        return found

    def start(segment, i, slot):
        if all(len(sources) == 1 for sources, _ in segments[segment][3]):
            for copy in copies(segment, i, slot, 0):
                copy.start()
            return
        for which in range(2):

            @pl.when(places[3] == which)
            def _(which=which):
                for copy in copies(segment, i, slot, which):
                    copy.start()

    start(0, 0, 0)
    for segment, (window, row, length, _) in enumerate(segments):
        steps = length // step
        if segment + 1 < len(segments):
            start(segment + 1, 0, 0)

        def one(i, carry, segment=segment, window=window, row=row, steps=steps):
            slot = lax.rem(i, 2)

            @pl.when(i + 1 < steps)
            def _():
                start(segment, i + 1, 1 - slot)

            for copy in copies(segment, i, slot, 0):
                copy.wait()
            projected = dot(landed[segment % 2, slot], weight[...], 0, 0)
            base = pl.multiple_of(PAD + 2 * (places[window] * rows + row + i * step), 8)
            table[pl.ds(base, step, stride=2), :] = projected[:, :128]
            table[pl.ds(base + 1, step, stride=2), :] = projected[:, 128:]
            return carry

        lax.fori_loop(0, steps, one, 0)


def update_kernel(sources, step, start, segments, table_step, places, aux, *refs):
    count = len(sources)
    given = 1 + max(at for source in sources for at, _ in source)
    arrays, refs = refs[:given], refs[given:]
    given, refs = refs[:8], refs[8:]
    held_here, refs = refs[-8:], refs[:-8]
    scales, w_latent, w_edge, w_agg, w_out_t, bias, gain, shift = held_here
    table, latents, fine, total, earlier, later, scale_rows, slots, live, sems, given_sems = refs[-11:]
    refs = refs[:-11]
    fetches = [
        pltpu.make_async_copy(far if at else far.at[:, pl.ds(start, near.shape[1])], near, given_sems.at[at])
        for at, (far, near) in enumerate(zip(given, held_here))
    ]
    features, nodes = latents.shape[0] // count, latents.shape[1]
    parents = slots.shape[0] // nodes
    if segments is None:
        kept, outs = refs[0], refs[1:]
        move = pltpu.make_async_copy(kept, table, sems.at[parents + 1 + count])
        move.start()
    else:
        w_parent, *coarse = refs[: -count - 3]
        *outs, kept, landed, landed_sems = refs[-count - 3 :]
        move = pltpu.make_async_copy(table, kept, sems.at[parents + 1 + count])
    held = aux.shape[0] // (parents + 1)
    fetches.append(pltpu.make_async_copy(aux.at[pl.ds(parents * start, parents * nodes)], slots, sems.at[0]))
    fetches.append(pltpu.make_async_copy(aux.at[pl.ds(parents * held, 1024)], live, sems.at[parents]))
    for fetch in fetches:
        fetch.start()

    def bring(p, which):
        at, shifted = sources[p][min(which, len(sources[p]) - 1)]
        column = arrays[at].shape[1] - nodes if shifted is None else pl.multiple_of(places[4] + start, 128)
        return pltpu.make_async_copy(
            arrays[at].at[:, pl.ds(column, nodes)],
            latents.at[pl.ds(p * features, features), :],
            sems.at[parents + 1 + p],
        )

    for p, source in enumerate(sources):
        for which in range(len(source)):

            @pl.when((places[3] == which) | (len(source) == 1))
            def _(p=p, which=which):
                bring(p, which).start()

    if segments is not None:
        fill_table(segments, table_step, places, coarse, w_parent, table, landed, landed_sems)
        move.start()
    for fetch in fetches:
        fetch.wait()
    for p in range(count):
        bring(p, 0).wait()
    if segments is None:
        move.wait()
    sublane = lax.broadcasted_iota(jnp.int32, (8, 128), 0)
    owns = [sublane >= 2 * j for j in range(4)]

    def begin(i):
        columns = pl.ds(pl.multiple_of(i * step, step), step)
        first = dot(latents[:, columns], w_latent[...], 0, 0) + bias[...]
        return first, scales[:, pl.ds(pl.multiple_of(i * step, step), step)].T

    def keep(first, scale_columns):
        width = first.shape[1] // 2
        fine[pl.ds(0, step, stride=2), :] = first[:, :128]
        fine[pl.ds(1, step, stride=2), :] = first[:, 128:width]
        later[...] = first[:, width:]
        scale_rows[pl.ds(0, step, stride=2), :] = scale_columns
        scale_rows[pl.ds(1, step, stride=2), :] = scale_columns

    def group(at, g):
        part = fine[pl.ds(g * 8, 8), :]
        scale = scale_rows[pl.ds(g * 8, 8), :]
        acc = None
        for k in range(parents):
            rows = None
            for j in range(4):
                loaded = table[pl.ds(slots[at + (k * step + g * 4 + j)], 8), :]
                rows = loaded if rows is None else jnp.where(owns[j], loaded, rows)
            hidden = jnp.maximum(part + rows, 0.0) * scale[:, k : k + 1]
            acc = hidden if acc is None else acc + hidden
        return acc

    def widened(ref):
        return jnp.concatenate([ref[...]] * (step // 128), axis=1)

    def finish(i, summed, own_part):
        at = pl.multiple_of(i * step, step)
        aggregate = dot(summed.astype(BF16), w_edge[...], 1, 0).astype(BF16)
        yield
        node_hidden = jnp.maximum(own_part + dot(aggregate, w_agg[...], 1, 0), 0.0).astype(BF16)
        yield
        output = dot(w_out_t[...], node_hidden, 1, 1)
        yield
        centered = output - jnp.mean(output, axis=0, keepdims=True)
        spread = jnp.mean(centered * centered, axis=0, keepdims=True)
        yield
        normed = centered * lax.rsqrt(spread + 1e-05) * widened(gain) + widened(shift)
        column = start + at + lax.broadcasted_iota(jnp.int32, (1, step), 1)
        moved = jnp.where(column < live[0], normed, 0.0)
        yield (latents[:, pl.ds(at, step)].astype(F32) + moved).astype(BF16)

    def last(parts):
        for value in parts:
            pass
        return value

    def write(i, result):
        for r in range(count):
            outs[r][:, pl.ds(pl.multiple_of(i * step, step), step)] = result[r * features : (r + 1) * features]

    def gathered():
        return jnp.concatenate([total[pl.ds(0, step, stride=2), :], total[pl.ds(1, step, stride=2), :]], axis=1)

    steps = nodes // step
    keep(*begin(0))

    def one_step(i, carry):
        before, after = jnp.maximum(i - 1, 0), jnp.minimum(i + 1, steps - 1)
        summed, own_part, current = gathered(), earlier[...], later[...]
        parts = finish(before, summed, own_part)
        base = pl.multiple_of(i * (parents * step), parents * step)
        begun = begin(after)
        for first in range(0, step // 4, GROUPS):
            result = next(parts, None) if first < 4 * GROUPS else last(parts)
            sums = [group(base, g) for g in range(first, min(first + GROUPS, step // 4))]
            total[pl.ds(first * 8, len(sums) * 8), :] = jnp.concatenate(sums, axis=0)
        write(before, result)
        earlier[...] = current
        keep(*begun)
        return carry

    lax.fori_loop(0, steps, one_step, 0)
    write(steps - 1, last(finish(steps - 1, gathered(), earlier[...])))
    if segments is not None:
        move.wait()


def by_step(aux, step):
    slots = aux[:-1].reshape(aux.shape[0] - 1, -1, step).transpose(1, 0, 2)
    return jnp.concatenate([slots.reshape(-1), aux[-1]])


def update(
    start, nodes, aux, arrays, sources, scales, params, places, table=None, segments=None, w_parent=None, coarse=()
):
    count, features = len(sources), arrays[0].shape[0]
    parents = aux.shape[0] - 1
    step = min(STEP, nodes)
    vmem = pl.BlockSpec(memory_space=pltpu.VMEM)
    smem = pl.BlockSpec(memory_space=pltpu.SMEM)
    far = pl.BlockSpec(memory_space=pltpu.HBM)
    out_shape = [jax.ShapeDtypeStruct((features, nodes), BF16)] * count
    operands = [places, by_step(aux, step), *arrays, scales, *params]
    specs = [smem, far] + [far] * (len(arrays) + 1 + len(params))
    scratch, table_step = [], 0
    if segments is None:
        operands, specs = operands + [table], specs + [far]
    else:
        operands, specs = operands + [w_parent, *coarse], specs + [vmem] + [far] * len(coarse)
        table_step = min(2048, segments[0][2])
        table = jax.ShapeDtypeStruct((2 * sum(segment[2] for segment in segments) + 2 * PAD, 128), F32)
        out_shape.append(table)
        scratch = [
            pltpu.VMEM((2, 2, w_parent.shape[0], table_step), BF16),
            pltpu.SemaphoreType.DMA((2, 2, len(segments[0][3]))),
        ]
    return pl.pallas_call(
        functools.partial(update_kernel, sources, step, start, segments, table_step),
        out_shape=out_shape,
        in_specs=specs,
        out_specs=[vmem] * count + [far] * (len(out_shape) - count),
        scratch_shapes=scratch
        + [
            pltpu.VMEM(table.shape, F32),
            pltpu.VMEM((count * features, nodes), BF16),
            pltpu.VMEM((2 * step, 128), F32),
            pltpu.VMEM((2 * step, 128), F32),
            pltpu.VMEM((step, 256), F32),
            pltpu.VMEM((step, 256), F32),
            pltpu.VMEM((2 * step, 8), F32),
            pltpu.SMEM((parents * nodes,), jnp.int32),
            pltpu.SMEM((1024,), jnp.int32),
            pltpu.SemaphoreType.DMA((parents + 2 + count,)),
            pltpu.SemaphoreType.DMA((1 + len(params),)),
            pltpu.VMEM((scales.shape[0], nodes), F32),
        ]
        + [pltpu.VMEM(param.shape, param.dtype) for param in params],
        compiler_params=pltpu.CompilerParams(vmem_limit_bytes=40 << 20),
        cost_estimate=pl.CostEstimate(flops=nodes * 700000, bytes_accessed=nodes * 2048, transcendentals=nodes),
    )(*operands)


def after(value, *others):
    return lax.optimization_barrier((value, *others))[0]


def shares(nodes):
    first = nodes * SHARE // 8 // STEP * STEP
    return [(0, first), (first, nodes - first)]


def cut(array, at, size):
    return lax.dynamic_slice_in_dim(array, at, size, 1)


def plain(fine_latent, coarse_latent, aux, weights, w_parent, run):
    groups, domains = lax.axis_size("feat"), lax.axis_size("dom")
    rank = lax.axis_index("feat")
    per_device = fine_latent.shape[1] // groups
    forward = [(i, i + 1) for i in range(domains - 1)]
    backward = [(i + 1, i) for i in range(domains - 1)]

    def turn(value, r):
        return lax.ppermute(value, "feat", [(i, (i + r) % groups) for i in range(groups)])

    own = [coarse_latent] + [turn(coarse_latent, r) for r in range(1, groups)]
    low = [lax.ppermute(piece, "dom", forward) for piece in own]
    high = [lax.ppermute(piece, "dom", backward) for piece in own]
    first_row = rank * per_device
    rows = coarse_latent.shape[1]
    segments = [
        (w, 0, rows, [((w * groups + p,), 0) for p in range(groups)]) for w in range(3)
    ]
    making = dict(segments=segments, w_parent=w_parent, coarse=low + own + high)
    places = jnp.stack([0, 1, 2, 0, first_row]).astype(jnp.int32)
    sources = [((0, 0),)] + [((r, None),) for r in range(1, groups)]
    aux = cut(aux, first_row, per_device)
    aux = jnp.concatenate([aux[:-1], aux[-1:] - first_row])
    weights = cut(weights, first_row, per_device)
    result = fine_latent
    arrived = []
    for c, (start, length) in enumerate(shares(per_device)):
        pieces = [fine_latent]
        for r in range(1, groups):
            part = cut(fine_latent, ((rank + r) % groups) * per_device + start, length)
            pieces.append(turn(after(part, own[-1]), r))
        outs = run(start, length, aux, pieces, sources, weights, places, **(making if c == 0 else dict(table=table)))
        table = outs[-1] if c == 0 else table
        result = lax.dynamic_update_slice_in_dim(result, outs[0], first_row + start, 1)
        for r in range(1, groups):
            arrived.append((turn(outs[r], -r), ((rank + r) % groups) * per_device + start))
    for part, at in arrived:
        result = lax.dynamic_update_slice_in_dim(result, part, at, 1)
    return result


def paired(fine_latent, coarse_latent, aux, weights, w_parent, run):
    domains = lax.axis_size("dom")
    side, rank = lax.axis_index("dom") % 2, lax.axis_index("feat")
    matched = side == rank
    pairs = range(domains // 2)

    def send(value, moves):
        perm = [((2 * c + a) * 2 + b, (2 * c + x) * 2 + y) for c in pairs for (a, b), (x, y) in moves]
        return lax.ppermute(value, ("dom", "feat"), perm)

    def swap_rank(value):
        return send(value, [((k, f), (k, 1 - f)) for k in range(2) for f in range(2)])

    def swap_side(value):
        return send(value, [((k, f), (1 - k, f)) for k in range(2) for f in range(2)])

    def halo(value):
        perm = [((2 * c - 1) * 2, (2 * c) * 2) for c in pairs if c > 0]
        perm += [((2 * c + 2) * 2 + 1, (2 * c + 1) * 2 + 1) for c in pairs if c + 1 < len(pairs)]
        return lax.ppermute(value, ("dom", "feat"), perm)

    def hand_over(value):
        return send(value, [((0, 0), (1, 0)), ((1, 1), (0, 1))])

    to_first = [((0, 0), (1, 0)), ((1, 1), (0, 1)), ((0, 1), (0, 0)), ((1, 0), (1, 1))]
    from_first = [(b, a) for a, b in to_first]
    to_second = [((0, 1), (1, 0)), ((1, 0), (0, 1))]

    half = fine_latent.shape[1] // 2
    mine = side * half
    rows = coarse_latent.shape[1]
    part = rows // PARTS
    mate = []
    for i in range(PARTS):
        piece = lax.slice_in_dim(coarse_latent, i * part, (i + 1) * part, axis=1)
        mate.append(swap_rank(after(piece, mate[-1]) if mate else piece))
    halo_own, other = halo(coarse_latent), swap_side(after(coarse_latent, mate[-1]))
    halo_mate, other_mate = [halo(piece) for piece in mate], [swap_side(piece) for piece in mate]
    passed_own, passed_mate = hand_over(halo_own), [hand_over(piece) for piece in halo_mate]
    coarse = [coarse_latent, other, halo_own, passed_own, *mate, *other_mate, *halo_mate, *passed_mate]
    segments = []
    for window, own in enumerate([(0,), (1,), (2, 3)]):
        for i in range(PARTS):
            came = tuple(4 + (w + window) * PARTS + i for w in range(len(own)))
            segments.append((window, i * part, part, [(own, i * part), (came, 0)]))
    places = jnp.stack([side + 1 - rank, 2 - side - rank, 2 * rank, jnp.where(matched, 0, 1), mine])
    places = places.astype(jnp.int32)

    chunks = []
    for start, length in shares(half):
        extra = max(half // 2 - length, 0)
        first = cut(fine_latent, jnp.where(matched, half - mine, mine) + start - extra, length + extra)
        second = cut(fine_latent, half - mine + start - extra, length + extra)
        first, second = send(after(first, mate[-1]), to_first), send(after(second, mate[-1]), to_second)
        chunks.append([first, fine_latent, second])

    both = jnp.concatenate([aux.astype(F32), weights])
    both = jnp.where(matched, cut(both, mine, half), hand_over(cut(both, half - mine, half)))
    aux, weights = both[: aux.shape[0]].astype(jnp.int32), both[aux.shape[0] :]
    aux = jnp.concatenate([aux[:-1], aux[-1:] - mine])

    making = dict(segments=segments, w_parent=w_parent, coarse=coarse)
    sources = [((0, None),), ((1, 0), (2, None))]
    result = jnp.zeros_like(fine_latent)
    moved = []
    for c, (start, length) in enumerate(shares(half)):
        out, kept, *made = run(
            start, length, aux, chunks[c], sources, weights, places, **(making if c == 0 else dict(table=table))
        )
        table = made[0] if made else table
        moved.append((start, kept, send(out, from_first), send(kept, to_second)))
    for start, kept, first, second in moved:
        result = lax.dynamic_update_slice_in_dim(result, jnp.where(matched, kept, first), mine + start, 1)
        result = lax.dynamic_update_slice_in_dim(
            result, jnp.where(matched, first, second), half - mine + start, 1
        )
    return result


def shards(
    fine_latent,
    coarse_latent,
    parents,
    interp_weights,
    live_rows,
    w_fine,
    w_parent,
    w_edge_out,
    w_node_fine,
    w_node_agg,
    w_node_out,
    edge_bias,
    node_bias,
    norm_gain,
    norm_bias,
):
    groups, domains = lax.axis_size("feat"), lax.axis_size("dom")
    rank = lax.axis_index("feat")
    own_features = fine_latent.shape[0]
    owners = [(rank - r) % groups for r in range(groups)]
    pairing = groups == 2 and domains % 2 == 0
    flip = jnp.where(lax.axis_index("dom") % 2 == rank, 1, 0) if pairing else 0

    def ordered(weight, axis, flip=flip):
        parts = [lax.dynamic_slice_in_dim(weight, o * own_features, own_features, axis) for o in owners]
        if pairing:
            parts = [jnp.where(flip == 1, parts[1], parts[0]), jnp.where(flip == 1, parts[0], parts[1])]
        return jnp.concatenate(parts, axis=axis)

    params = (
        jnp.concatenate([ordered(w_fine, 0), ordered(w_node_fine, 0)], axis=1),
        w_edge_out,
        w_node_agg,
        ordered(w_node_out, 1).T,
        jnp.concatenate([edge_bias, node_bias])[None],
        jnp.broadcast_to(ordered(norm_gain, 0)[:, None], (norm_gain.shape[0], 128)),
        jnp.broadcast_to(ordered(norm_bias, 0)[:, None], (norm_bias.shape[0], 128)),
    )

    def run(start, nodes, aux, arrays, sources, weights, places, **table):
        scales = jnp.pad(weights, ((0, 8 - weights.shape[0]), (0, 0)))
        return update(start, nodes, aux, arrays, sources, scales, params, places, **table)

    count = parents.shape[1]
    slots = 2 * parents + (PAD - 2 * (jnp.arange(count, dtype=jnp.int32) % 4))
    aux = jnp.concatenate([slots, jnp.broadcast_to(live_rows[:, None], (1, count))])
    plan = paired if pairing else plain
    return plan(fine_latent, coarse_latent, aux, interp_weights, ordered(w_parent, 0, 0), run)


def solution(mesh):
    in_specs = (P("feat", "dom"), P("feat", "dom"), P(None, "dom"), P(None, "dom"), P("dom")) + (P(),) * 10
    return jax.shard_map(shards, mesh=mesh, in_specs=in_specs, out_specs=P("feat", "dom"), check_vma=False)
```

```python
import functools

import jax
import jax.numpy as jnp
from jax import lax
from jax.experimental import pallas as pl
from jax.experimental.pallas import tpu as pltpu
from jax.sharding import PartitionSpec as P

F32 = jnp.float32
BF16 = jnp.bfloat16
PAD = 8
SHARE = 4
PARTS = 1
STEP = 512
GROUPS = 13


def dot(a, b, ca, cb):
    return lax.dot_general(a, b, (((ca,), (cb,)), ((), ())), preferred_element_type=F32)


def fill_table(segments, step, places, refs, weight, table, landed, sems):
    rows = (table.shape[0] - 2 * PAD) // 6
    features = landed.shape[2] // sems.shape[2]
    table[pl.ds(0, PAD), :] = jnp.zeros((PAD, 128), F32)
    table[pl.ds(PAD + 6 * rows, PAD), :] = jnp.zeros((PAD, 128), F32)

    def copies(segment, i, slot, which):
        found = []
        for p, (sources, first) in enumerate(segments[segment][3]):
            at = pl.multiple_of(first + i * step, 128)
            found.append(
                pltpu.make_async_copy(
                    refs[sources[min(which, len(sources) - 1)]].at[:, pl.ds(at, step)],
                    landed.at[segment % 2, slot, pl.ds(p * features, features), :],
                    sems.at[segment % 2, slot, p],
                )
            )
        return found

    def start(segment, i, slot):
        if all(len(sources) == 1 for sources, _ in segments[segment][3]):
            for copy in copies(segment, i, slot, 0):
                copy.start()
            return
        for which in range(2):

            @pl.when(places[3] == which)
            def _(which=which):
                for copy in copies(segment, i, slot, which):
                    copy.start()

    start(0, 0, 0)
    for segment, (window, row, length, _) in enumerate(segments):
        steps = length // step
        if segment + 1 < len(segments):
            start(segment + 1, 0, 0)

        def one(i, carry, segment=segment, window=window, row=row, steps=steps):
            slot = lax.rem(i, 2)

            @pl.when(i + 1 < steps)
            def _():
                start(segment, i + 1, 1 - slot)

            for copy in copies(segment, i, slot, 0):
                copy.wait()
            projected = dot(landed[segment % 2, slot], weight[...], 0, 0)
            base = pl.multiple_of(PAD + 2 * (places[window] * rows + row + i * step), 8)
            table[pl.ds(base, step, stride=2), :] = projected[:, :128]
            table[pl.ds(base + 1, step, stride=2), :] = projected[:, 128:]
            return carry

        lax.fori_loop(0, steps, one, 0)


def update_kernel(sources, step, start, segments, table_step, places, aux, *refs):
    count = len(sources)
    given = 1 + max(at for source in sources for at, _ in source)
    arrays, refs = refs[:given], refs[given:]
    given, refs = refs[:8], refs[8:]
    held_here, refs = refs[-8:], refs[:-8]
    scales, w_latent, w_edge, w_agg, w_out_t, bias, gain, shift = held_here
    table, latents, fine, total, earlier, later, scale_rows, slots, live, sems, given_sems = refs[-11:]
    refs = refs[:-11]
    fetches = [
        pltpu.make_async_copy(far if at else far.at[:, pl.ds(start, near.shape[1])], near, given_sems.at[at])
        for at, (far, near) in enumerate(zip(given, held_here))
    ]
    features, nodes = latents.shape[0] // count, latents.shape[1]
    parents = slots.shape[0] // nodes
    if segments is None:
        kept, outs = refs[0], refs[1:]
        move = pltpu.make_async_copy(kept, table, sems.at[parents + 1 + count])
        move.start()
    else:
        w_parent, *coarse = refs[: -count - 3]
        *outs, kept, landed, landed_sems = refs[-count - 3 :]
        move = pltpu.make_async_copy(table, kept, sems.at[parents + 1 + count])
    held = aux.shape[0] // (parents + 1)
    fetches.append(pltpu.make_async_copy(aux.at[pl.ds(parents * start, parents * nodes)], slots, sems.at[0]))
    fetches.append(pltpu.make_async_copy(aux.at[pl.ds(parents * held, 1024)], live, sems.at[parents]))
    for fetch in fetches:
        fetch.start()

    def bring(p, which):
        at, shifted = sources[p][min(which, len(sources[p]) - 1)]
        column = arrays[at].shape[1] - nodes if shifted is None else pl.multiple_of(places[4] + start, 128)
        return pltpu.make_async_copy(
            arrays[at].at[:, pl.ds(column, nodes)],
            latents.at[pl.ds(p * features, features), :],
            sems.at[parents + 1 + p],
        )

    for p, source in enumerate(sources):
        for which in range(len(source)):

            @pl.when((places[3] == which) | (len(source) == 1))
            def _(p=p, which=which):
                bring(p, which).start()

    if segments is not None:
        fill_table(segments, table_step, places, coarse, w_parent, table, landed, landed_sems)
        move.start()
    for fetch in fetches:
        fetch.wait()
    for p in range(count):
        bring(p, 0).wait()
    if segments is None:
        move.wait()
    sublane = lax.broadcasted_iota(jnp.int32, (8, 128), 0)
    owns = [sublane >= 2 * j for j in range(4)]

    def begin(i):
        columns = pl.ds(pl.multiple_of(i * step, step), step)
        first = dot(latents[:, columns], w_latent[...], 0, 0) + bias[...]
        return first, scales[:, pl.ds(pl.multiple_of(i * step, step), step)].T

    def keep(first, scale_columns):
        width = first.shape[1] // 2
        fine[pl.ds(0, step, stride=2), :] = first[:, :128]
        fine[pl.ds(1, step, stride=2), :] = first[:, 128:width]
        later[...] = first[:, width:]
        scale_rows[pl.ds(0, step, stride=2), :] = scale_columns
        scale_rows[pl.ds(1, step, stride=2), :] = scale_columns

    def group(at, g):
        part = fine[pl.ds(g * 8, 8), :]
        scale = scale_rows[pl.ds(g * 8, 8), :]
        acc = None
        for k in range(parents):
            rows = None
            for j in range(4):
                loaded = table[pl.ds(slots[at + (k * step + g * 4 + j)], 8), :]
                rows = loaded if rows is None else jnp.where(owns[j], loaded, rows)
            hidden = jnp.maximum(part + rows, 0.0) * scale[:, k : k + 1]
            acc = hidden if acc is None else acc + hidden
        return acc

    def widened(ref):
        return jnp.concatenate([ref[...]] * (step // 128), axis=1)

    def finish(i, summed, own_part):
        at = pl.multiple_of(i * step, step)
        aggregate = dot(summed.astype(BF16), w_edge[...], 1, 0).astype(BF16)
        yield
        node_hidden = jnp.maximum(own_part + dot(aggregate, w_agg[...], 1, 0), 0.0).astype(BF16)
        yield
        output = dot(w_out_t[...], node_hidden, 1, 1)
        yield
        centered = output - jnp.mean(output, axis=0, keepdims=True)
        spread = jnp.mean(centered * centered, axis=0, keepdims=True)
        yield
        normed = centered * lax.rsqrt(spread + 1e-05) * widened(gain) + widened(shift)
        column = start + at + lax.broadcasted_iota(jnp.int32, (1, step), 1)
        moved = jnp.where(column < live[0], normed, 0.0)
        yield (latents[:, pl.ds(at, step)].astype(F32) + moved).astype(BF16)

    def last(parts):
        for value in parts:
            pass
        return value

    def write(i, result):
        for r in range(count):
            outs[r][:, pl.ds(pl.multiple_of(i * step, step), step)] = result[r * features : (r + 1) * features]

    def gathered():
        return jnp.concatenate([total[pl.ds(0, step, stride=2), :], total[pl.ds(1, step, stride=2), :]], axis=1)

    steps = nodes // step
    keep(*begin(0))

    def one_step(i, carry):
        before, after = jnp.maximum(i - 1, 0), jnp.minimum(i + 1, steps - 1)
        summed, own_part, current = gathered(), earlier[...], later[...]
        parts = finish(before, summed, own_part)
        base = pl.multiple_of(i * (parents * step), parents * step)
        begun, result = begin(after), None
        for first in range(0, step // 4, GROUPS):
            result = next(parts, result)
            sums = [group(base, g) for g in range(first, min(first + GROUPS, step // 4))]
            total[pl.ds(first * 8, len(sums) * 8), :] = jnp.concatenate(sums, axis=0)
        for value in parts:
            result = value
        write(before, result)
        earlier[...] = current
        keep(*begun)
        return carry

    lax.fori_loop(0, steps, one_step, 0)
    write(steps - 1, last(finish(steps - 1, gathered(), earlier[...])))
    if segments is not None:
        move.wait()


def by_step(aux, step):
    slots = aux[:-1].reshape(aux.shape[0] - 1, -1, step).transpose(1, 0, 2)
    return jnp.concatenate([slots.reshape(-1), aux[-1]])


def update(
    start, nodes, aux, arrays, sources, scales, params, places, table=None, segments=None, w_parent=None, coarse=()
):
    count, features = len(sources), arrays[0].shape[0]
    parents = aux.shape[0] - 1
    step = min(STEP, nodes)
    vmem = pl.BlockSpec(memory_space=pltpu.VMEM)
    smem = pl.BlockSpec(memory_space=pltpu.SMEM)
    far = pl.BlockSpec(memory_space=pl.ANY)
    hbm = pl.BlockSpec(memory_space=pltpu.HBM)
    out_shape = [jax.ShapeDtypeStruct((features, nodes), BF16)] * count
    operands = [places, by_step(aux, step), *arrays, scales, *params]
    specs = [smem, far] + [far] * (len(arrays) + 1 + len(params))
    scratch, table_step = [], 0
    if segments is None:
        operands, specs = operands + [table], specs + [hbm]
    else:
        operands, specs = operands + [w_parent, *coarse], specs + [vmem] + [far] * len(coarse)
        table_step = min(2048, segments[0][2])
        table = jax.ShapeDtypeStruct((2 * sum(segment[2] for segment in segments) + 2 * PAD, 128), F32)
        out_shape.append(table)
        scratch = [
            pltpu.VMEM((2, 2, w_parent.shape[0], table_step), BF16),
            pltpu.SemaphoreType.DMA((2, 2, len(segments[0][3]))),
        ]
    return pl.pallas_call(
        functools.partial(update_kernel, sources, step, start, segments, table_step),
        out_shape=out_shape,
        in_specs=specs,
        out_specs=[vmem] * count + [hbm] * (len(out_shape) - count),
        scratch_shapes=scratch
        + [
            pltpu.VMEM(table.shape, F32),
            pltpu.VMEM((count * features, nodes), BF16),
            pltpu.VMEM((2 * step, 128), F32),
            pltpu.VMEM((2 * step, 128), F32),
            pltpu.VMEM((step, 256), F32),
            pltpu.VMEM((step, 256), F32),
            pltpu.VMEM((2 * step, 8), F32),
            pltpu.SMEM((parents * nodes,), jnp.int32),
            pltpu.SMEM((1024,), jnp.int32),
            pltpu.SemaphoreType.DMA((parents + 2 + count,)),
            pltpu.SemaphoreType.DMA((1 + len(params),)),
            pltpu.VMEM((scales.shape[0], nodes), F32),
        ]
        + [pltpu.VMEM(param.shape, param.dtype) for param in params],
        compiler_params=pltpu.CompilerParams(vmem_limit_bytes=40 << 20),
        cost_estimate=pl.CostEstimate(flops=nodes * 700000, bytes_accessed=nodes * 2048, transcendentals=nodes),
    )(*operands)


def place_kernel(start, places, kept, first, second, *refs):
    result, sems = refs[-2:]
    half, length = result.shape[1] // 2, kept.shape[1]
    mine = places[4]
    for which, (here, there) in enumerate([(kept, first), (first, second)]):

        @pl.when(places[3] == which)
        def _(here=here, there=there):
            copies = [
                pltpu.make_async_copy(
                    piece, result.at[:, pl.ds(pl.multiple_of(column + start, 128), length)], sems.at[at]
                )
                for at, (piece, column) in enumerate([(here, mine), (there, half - mine)])
            ]
            for copy in copies:
                copy.start()
            for copy in copies:
                copy.wait()


def place(start, places, kept, first, second, shape, result=None):
    far = pl.BlockSpec(memory_space=pl.ANY)
    given = [] if result is None else [result]
    return pl.pallas_call(
        functools.partial(place_kernel, start),
        out_shape=shape,
        in_specs=[pl.BlockSpec(memory_space=pltpu.SMEM)] + [far] * (3 + len(given)),
        out_specs=pl.BlockSpec(memory_space=pltpu.HBM),
        scratch_shapes=[pltpu.SemaphoreType.DMA((2,))],
        input_output_aliases={4: 0} if given else {},
        cost_estimate=pl.CostEstimate(flops=0, bytes_accessed=4 * kept.size, transcendentals=0),
    )(places, kept, first, second, *given)


def after(value, *others):
    return lax.optimization_barrier((value, *others))[0]


def shares(nodes):
    first = nodes * SHARE // 8 // STEP * STEP
    return [(0, first), (first, nodes - first)]


def cut(array, at, size):
    return lax.dynamic_slice_in_dim(array, at, size, 1)


def plain(fine_latent, coarse_latent, aux, weights, w_parent, run):
    groups, domains = lax.axis_size("feat"), lax.axis_size("dom")
    rank = lax.axis_index("feat")
    per_device = fine_latent.shape[1] // groups
    forward = [(i, i + 1) for i in range(domains - 1)]
    backward = [(i + 1, i) for i in range(domains - 1)]

    def turn(value, r):
        return lax.ppermute(value, "feat", [(i, (i + r) % groups) for i in range(groups)])

    own = [coarse_latent] + [turn(coarse_latent, r) for r in range(1, groups)]
    low = [lax.ppermute(piece, "dom", forward) for piece in own]
    high = [lax.ppermute(piece, "dom", backward) for piece in own]
    first_row = rank * per_device
    rows = coarse_latent.shape[1]
    segments = [
        (w, 0, rows, [((w * groups + p,), 0) for p in range(groups)]) for w in range(3)
    ]
    making = dict(segments=segments, w_parent=w_parent, coarse=low + own + high)
    places = jnp.stack([0, 1, 2, 0, first_row]).astype(jnp.int32)
    sources = [((0, 0),)] + [((r, None),) for r in range(1, groups)]
    aux = cut(aux, first_row, per_device)
    aux = jnp.concatenate([aux[:-1], aux[-1:] - first_row])
    weights = cut(weights, first_row, per_device)
    result = fine_latent
    arrived = []
    for c, (start, length) in enumerate(shares(per_device)):
        pieces = [fine_latent]
        for r in range(1, groups):
            part = cut(fine_latent, ((rank + r) % groups) * per_device + start, length)
            pieces.append(turn(after(part, own[-1]), r))
        outs = run(start, length, aux, pieces, sources, weights, places, **(making if c == 0 else dict(table=table)))
        table = outs[-1] if c == 0 else table
        result = lax.dynamic_update_slice_in_dim(result, outs[0], first_row + start, 1)
        for r in range(1, groups):
            arrived.append((turn(outs[r], -r), ((rank + r) % groups) * per_device + start))
    for part, at in arrived:
        result = lax.dynamic_update_slice_in_dim(result, part, at, 1)
    return result


def paired(fine_latent, coarse_latent, aux, weights, w_parent, run):
    domains = lax.axis_size("dom")
    side, rank = lax.axis_index("dom") % 2, lax.axis_index("feat")
    matched = side == rank
    pairs = range(domains // 2)

    def send(value, moves):
        perm = [((2 * c + a) * 2 + b, (2 * c + x) * 2 + y) for c in pairs for (a, b), (x, y) in moves]
        return lax.ppermute(value, ("dom", "feat"), perm)

    def swap_rank(value):
        return send(value, [((k, f), (k, 1 - f)) for k in range(2) for f in range(2)])

    def swap_side(value):
        return send(value, [((k, f), (1 - k, f)) for k in range(2) for f in range(2)])

    def halo(value):
        perm = [((2 * c - 1) * 2, (2 * c) * 2) for c in pairs if c > 0]
        perm += [((2 * c + 2) * 2 + 1, (2 * c + 1) * 2 + 1) for c in pairs if c + 1 < len(pairs)]
        return lax.ppermute(value, ("dom", "feat"), perm)

    def hand_over(value):
        return send(value, [((0, 0), (1, 0)), ((1, 1), (0, 1))])

    to_first = [((0, 0), (1, 0)), ((1, 1), (0, 1)), ((0, 1), (0, 0)), ((1, 0), (1, 1))]
    from_first = [(b, a) for a, b in to_first]
    to_second = [((0, 1), (1, 0)), ((1, 0), (0, 1))]

    half = fine_latent.shape[1] // 2
    mine = side * half
    rows = coarse_latent.shape[1]
    part = rows // PARTS
    mate = []
    for i in range(PARTS):
        piece = lax.slice_in_dim(coarse_latent, i * part, (i + 1) * part, axis=1)
        mate.append(swap_rank(after(piece, mate[-1]) if mate else piece))
    halo_own, other = halo(coarse_latent), swap_side(after(coarse_latent, mate[-1]))
    halo_mate, other_mate = [halo(piece) for piece in mate], [swap_side(piece) for piece in mate]
    passed_own, passed_mate = hand_over(halo_own), [hand_over(piece) for piece in halo_mate]
    coarse = [coarse_latent, other, halo_own, passed_own, *mate, *other_mate, *halo_mate, *passed_mate]
    segments = []
    for window, own in enumerate([(0,), (1,), (2, 3)]):
        for i in range(PARTS):
            came = tuple(4 + (w + window) * PARTS + i for w in range(len(own)))
            segments.append((window, i * part, part, [(own, i * part), (came, 0)]))
    places = jnp.stack([side + 1 - rank, 2 - side - rank, 2 * rank, jnp.where(matched, 0, 1), mine])
    places = places.astype(jnp.int32)

    chunks = []
    for start, length in shares(half):
        extra = max(half // 2 - length, 0)
        first = cut(fine_latent, jnp.where(matched, half - mine, mine) + start - extra, length + extra)
        second = cut(fine_latent, half - mine + start - extra, length + extra)
        first, second = send(after(first, mate[-1]), to_first), send(after(second, mate[-1]), to_second)
        chunks.append([first, fine_latent, second])

    both = jnp.concatenate([aux.astype(F32), weights])
    both = jnp.where(matched, cut(both, mine, half), hand_over(cut(both, half - mine, half)))
    aux, weights = both[: aux.shape[0]].astype(jnp.int32), both[aux.shape[0] :]
    aux = jnp.concatenate([aux[:-1], aux[-1:] - mine])

    making = dict(segments=segments, w_parent=w_parent, coarse=coarse)
    sources = [((0, None),), ((1, 0), (2, None))]
    moved = []
    for c, (start, length) in enumerate(shares(half)):
        out, kept, *made = run(
            start, length, aux, chunks[c], sources, weights, places, **(making if c == 0 else dict(table=table))
        )
        table = made[0] if made else table
        moved.append((start, kept, send(out, from_first), send(kept, to_second)))
    result, shape = None, jax.ShapeDtypeStruct(fine_latent.shape, BF16)
    for start, kept, first, second in moved:
        result = place(start, places, kept, first, second, shape, result)
    return result


def shards(
    fine_latent,
    coarse_latent,
    parents,
    interp_weights,
    live_rows,
    w_fine,
    w_parent,
    w_edge_out,
    w_node_fine,
    w_node_agg,
    w_node_out,
    edge_bias,
    node_bias,
    norm_gain,
    norm_bias,
):
    groups, domains = lax.axis_size("feat"), lax.axis_size("dom")
    rank = lax.axis_index("feat")
    own_features = fine_latent.shape[0]
    owners = [(rank - r) % groups for r in range(groups)]
    pairing = groups == 2 and domains % 2 == 0
    flip = jnp.where(lax.axis_index("dom") % 2 == rank, 1, 0) if pairing else 0

    def ordered(weight, axis, flip=flip):
        parts = [lax.dynamic_slice_in_dim(weight, o * own_features, own_features, axis) for o in owners]
        if pairing:
            parts = [jnp.where(flip == 1, parts[1], parts[0]), jnp.where(flip == 1, parts[0], parts[1])]
        return jnp.concatenate(parts, axis=axis)

    params = (
        jnp.concatenate([ordered(w_fine, 0), ordered(w_node_fine, 0)], axis=1),
        w_edge_out,
        w_node_agg,
        ordered(w_node_out, 1).T,
        jnp.concatenate([edge_bias, node_bias])[None],
        jnp.broadcast_to(ordered(norm_gain, 0)[:, None], (norm_gain.shape[0], 128)),
        jnp.broadcast_to(ordered(norm_bias, 0)[:, None], (norm_bias.shape[0], 128)),
    )

    def run(start, nodes, aux, arrays, sources, weights, places, **table):
        scales = jnp.pad(weights, ((0, 8 - weights.shape[0]), (0, 0)))
        return update(start, nodes, aux, arrays, sources, scales, params, places, **table)

    count = parents.shape[1]
    slots = 2 * parents + (PAD - 2 * (jnp.arange(count, dtype=jnp.int32) % 4))
    aux = jnp.concatenate([slots, jnp.broadcast_to(live_rows[:, None], (1, count))])
    plan = paired if pairing else plain
    return plan(fine_latent, coarse_latent, aux, interp_weights, ordered(w_parent, 0, 0), run)


def solution(mesh):
    in_specs = (P("feat", "dom"), P("feat", "dom"), P(None, "dom"), P(None, "dom"), P("dom")) + (P(),) * 10
    return jax.shard_map(shards, mesh=mesh, in_specs=in_specs, out_specs=P("feat", "dom"), check_vma=False)
```

```python
import functools

import jax
import jax.numpy as jnp
from jax import lax
from jax.experimental import pallas as pl
from jax.experimental.pallas import tpu as pltpu
from jax.sharding import PartitionSpec as P

F32 = jnp.float32
BF16 = jnp.bfloat16
PAD = 8
SHARE = 4
PARTS = 1
STEP = 256
GROUPS = 13


def dot(a, b, ca, cb):
    return lax.dot_general(a, b, (((ca,), (cb,)), ((), ())), preferred_element_type=F32)


def fill_table(segments, step, places, refs, weight, table, landed, sems):
    rows = (table.shape[0] - 2 * PAD) // 6
    features = landed.shape[2] // sems.shape[2]
    table[pl.ds(0, PAD), :] = jnp.zeros((PAD, 128), F32)
    table[pl.ds(PAD + 6 * rows, PAD), :] = jnp.zeros((PAD, 128), F32)

    def copies(segment, i, slot, which):
        found = []
        for p, (sources, first) in enumerate(segments[segment][3]):
            at = pl.multiple_of(first + i * step, 128)
            found.append(
                pltpu.make_async_copy(
                    refs[sources[min(which, len(sources) - 1)]].at[:, pl.ds(at, step)],
                    landed.at[segment % 2, slot, pl.ds(p * features, features), :],
                    sems.at[segment % 2, slot, p],
                )
            )
        return found

    def start(segment, i, slot):
        if all(len(sources) == 1 for sources, _ in segments[segment][3]):
            for copy in copies(segment, i, slot, 0):
                copy.start()
            return
        for which in range(2):

            @pl.when(places[3] == which)
            def _(which=which):
                for copy in copies(segment, i, slot, which):
                    copy.start()

    start(0, 0, 0)
    for segment, (window, row, length, _) in enumerate(segments):
        steps = length // step
        if segment + 1 < len(segments):
            start(segment + 1, 0, 0)

        def one(i, carry, segment=segment, window=window, row=row, steps=steps):
            slot = lax.rem(i, 2)

            @pl.when(i + 1 < steps)
            def _():
                start(segment, i + 1, 1 - slot)

            for copy in copies(segment, i, slot, 0):
                copy.wait()
            projected = dot(landed[segment % 2, slot], weight[...], 0, 0)
            base = pl.multiple_of(PAD + 2 * (places[window] * rows + row + i * step), 8)
            table[pl.ds(base, step, stride=2), :] = projected[:, :128]
            table[pl.ds(base + 1, step, stride=2), :] = projected[:, 128:]
            return carry

        lax.fori_loop(0, steps, one, 0)


def update_kernel(sources, step, start, segments, table_step, places, aux, *refs):
    count = len(sources)
    given = 1 + max(at for source in sources for at, _ in source)
    arrays, refs = refs[:given], refs[given:]
    given, refs = refs[:10], refs[10:]
    held_here, refs = refs[-10:], refs[:-10]
    scales, w_fine, w_node, w_edge, w_agg, w_out_t, edge_bias, node_bias, gain, shift = held_here
    table, latents, fine, total, scale_rows, slots, live, sems, given_sems = refs[-9:]
    refs = refs[:-9]
    fetches = [
        pltpu.make_async_copy(far if at else far.at[:, pl.ds(start, near.shape[1])], near, given_sems.at[at])
        for at, (far, near) in enumerate(zip(given, held_here))
    ]
    features, nodes = latents.shape[0] // count, latents.shape[1]
    parents = slots.shape[0] // nodes
    if segments is None:
        kept, outs = refs[0], refs[1:]
        move = pltpu.make_async_copy(kept, table, sems.at[parents + 1 + count])
        move.start()
    else:
        w_parent, *coarse = refs[: -count - 3]
        *outs, kept, landed, landed_sems = refs[-count - 3 :]
        move = pltpu.make_async_copy(table, kept, sems.at[parents + 1 + count])
    held = aux.shape[0] // (parents + 1)
    fetches.append(pltpu.make_async_copy(aux.at[pl.ds(parents * start, parents * nodes)], slots, sems.at[0]))
    fetches.append(pltpu.make_async_copy(aux.at[pl.ds(parents * held, 1024)], live, sems.at[parents]))
    for fetch in fetches:
        fetch.start()

    def bring(p, which):
        at, shifted = sources[p][min(which, len(sources[p]) - 1)]
        column = arrays[at].shape[1] - nodes if shifted is None else pl.multiple_of(places[4] + start, 128)
        return pltpu.make_async_copy(
            arrays[at].at[:, pl.ds(column, nodes)],
            latents.at[pl.ds(p * features, features), :],
            sems.at[parents + 1 + p],
        )

    for p, source in enumerate(sources):
        for which in range(len(source)):

            @pl.when((places[3] == which) | (len(source) == 1))
            def _(p=p, which=which):
                bring(p, which).start()

    if segments is not None:
        fill_table(segments, table_step, places, coarse, w_parent, table, landed, landed_sems)
        move.start()
    for fetch in fetches:
        fetch.wait()
    for p in range(count):
        bring(p, 0).wait()
    if segments is None:
        move.wait()
    sublane = lax.broadcasted_iota(jnp.int32, (8, 128), 0)
    owns = [sublane >= 2 * j for j in range(4)]

    def begin(i):
        columns = pl.ds(pl.multiple_of(i * step, step), step)
        first = dot(latents[:, columns], w_fine[...], 0, 0) + edge_bias[...]
        return first, scales[:, pl.ds(pl.multiple_of(i * step, step), step)].T

    def keep(first, scale_columns):
        fine[pl.ds(0, step, stride=2), :] = first[:, :128]
        fine[pl.ds(1, step, stride=2), :] = first[:, 128:]
        scale_rows[pl.ds(0, step, stride=2), :] = scale_columns
        scale_rows[pl.ds(1, step, stride=2), :] = scale_columns

    def group(at, g):
        part = fine[pl.ds(g * 8, 8), :]
        scale = scale_rows[pl.ds(g * 8, 8), :]
        acc = None
        for k in range(parents):
            rows = None
            for j in range(4):
                loaded = table[pl.ds(slots[at + (k * step + g * 4 + j)], 8), :]
                rows = loaded if rows is None else jnp.where(owns[j], loaded, rows)
            hidden = jnp.maximum(part + rows, 0.0) * scale[:, k : k + 1]
            acc = hidden if acc is None else acc + hidden
        return acc

    def finish(i, summed):
        at = pl.multiple_of(i * step, step)
        own_part = dot(latents[:, pl.ds(at, step)], w_node[...], 0, 0)
        aggregate = dot(summed.astype(BF16), w_edge[...], 1, 0).astype(BF16)
        yield
        node_hidden = dot(aggregate, w_agg[...], 1, 0) + own_part + node_bias[...]
        node_hidden = jnp.maximum(node_hidden, 0.0).astype(BF16)
        yield
        output = dot(w_out_t[...], node_hidden, 1, 1)
        for lane in range(0, step, 128):
            yield
            columns = pl.ds(pl.multiple_of(at + lane, 128), 128)
            here = output[:, lane : lane + 128]
            centered = here - jnp.mean(here, axis=0, keepdims=True)
            spread = jnp.mean(centered * centered, axis=0, keepdims=True)
            normed = centered * lax.rsqrt(spread + 1e-05) * gain[...] + shift[...]
            column = start + at + lane + lax.broadcasted_iota(jnp.int32, (1, 128), 1)
            moved = jnp.where(column < live[0], normed, 0.0)
            result = (latents[:, columns].astype(F32) + moved).astype(BF16)
            for r in range(count):
                outs[r][:, columns] = result[r * features : (r + 1) * features]

    def gathered():
        return jnp.concatenate([total[pl.ds(0, step, stride=2), :], total[pl.ds(1, step, stride=2), :]], axis=1)

    steps = nodes // step
    keep(*begin(0))

    def one_step(i, carry):
        parts = finish(jnp.maximum(i - 1, 0), gathered())
        begun = begin(jnp.minimum(i + 1, steps - 1))
        base = pl.multiple_of(i * (parents * step), parents * step)
        for first in range(0, step // 4, GROUPS):
            next(parts, None)
            sums = [group(base, g) for g in range(first, min(first + GROUPS, step // 4))]
            total[pl.ds(first * 8, len(sums) * 8), :] = jnp.concatenate(sums, axis=0)
        for _ in parts:
            pass
        keep(*begun)
        return carry

    lax.fori_loop(0, steps, one_step, 0)
    for _ in finish(steps - 1, gathered()):
        pass
    if segments is not None:
        move.wait()


def by_step(aux, step):
    slots = aux[:-1].reshape(aux.shape[0] - 1, -1, step).transpose(1, 0, 2)
    return jnp.concatenate([slots.reshape(-1), aux[-1]])


def update(
    start, nodes, aux, arrays, sources, scales, params, places, table=None, segments=None, w_parent=None, coarse=()
):
    count, features = len(sources), arrays[0].shape[0]
    parents = aux.shape[0] - 1
    step = min(STEP, nodes)
    vmem = pl.BlockSpec(memory_space=pltpu.VMEM)
    smem = pl.BlockSpec(memory_space=pltpu.SMEM)
    far = pl.BlockSpec(memory_space=pltpu.HBM)
    anywhere = pl.BlockSpec(memory_space=pl.ANY)
    out_shape = [jax.ShapeDtypeStruct((features, nodes), BF16)] * count
    operands = [places, by_step(aux, step), *arrays, scales, *params]
    specs = [smem, far] + [anywhere] * len(arrays) + [far] * (1 + len(params))
    scratch, table_step = [], 0
    if segments is None:
        operands, specs = operands + [table], specs + [far]
    else:
        operands, specs = operands + [w_parent, *coarse], specs + [vmem] + [far] * len(coarse)
        table_step = min(2048, segments[0][2])
        table = jax.ShapeDtypeStruct((2 * sum(segment[2] for segment in segments) + 2 * PAD, 128), F32)
        out_shape.append(table)
        scratch = [
            pltpu.VMEM((2, 2, w_parent.shape[0], table_step), BF16),
            pltpu.SemaphoreType.DMA((2, 2, len(segments[0][3]))),
        ]
    return pl.pallas_call(
        functools.partial(update_kernel, sources, step, start, segments, table_step),
        out_shape=out_shape,
        in_specs=specs,
        out_specs=[vmem] * count + [far] * (len(out_shape) - count),
        scratch_shapes=scratch
        + [
            pltpu.VMEM(table.shape, F32),
            pltpu.VMEM((count * features, nodes), BF16),
            pltpu.VMEM((2 * step, 128), F32),
            pltpu.VMEM((2 * step, 128), F32),
            pltpu.VMEM((2 * step, 8), F32),
            pltpu.SMEM((parents * nodes,), jnp.int32),
            pltpu.SMEM((1024,), jnp.int32),
            pltpu.SemaphoreType.DMA((parents + 2 + count,)),
            pltpu.SemaphoreType.DMA((1 + len(params),)),
            pltpu.VMEM((scales.shape[0], nodes), F32),
        ]
        + [pltpu.VMEM(param.shape, param.dtype) for param in params],
        compiler_params=pltpu.CompilerParams(vmem_limit_bytes=40 << 20),
        cost_estimate=pl.CostEstimate(flops=nodes * 700000, bytes_accessed=nodes * 2048, transcendentals=nodes),
    )(*operands)


def after(value, *others):
    return lax.optimization_barrier((value, *others))[0]


def shares(nodes):
    first = nodes * SHARE // 8 // STEP * STEP
    return [(0, first), (first, nodes - first)]


def cut(array, at, size):
    return lax.dynamic_slice_in_dim(array, at, size, 1)


def plain(fine_latent, coarse_latent, aux, weights, w_parent, run):
    groups, domains = lax.axis_size("feat"), lax.axis_size("dom")
    rank = lax.axis_index("feat")
    per_device = fine_latent.shape[1] // groups
    forward = [(i, i + 1) for i in range(domains - 1)]
    backward = [(i + 1, i) for i in range(domains - 1)]

    def turn(value, r):
        return lax.ppermute(value, "feat", [(i, (i + r) % groups) for i in range(groups)])

    own = [coarse_latent] + [turn(coarse_latent, r) for r in range(1, groups)]
    low = [lax.ppermute(piece, "dom", forward) for piece in own]
    high = [lax.ppermute(piece, "dom", backward) for piece in own]
    first_row = rank * per_device
    rows = coarse_latent.shape[1]
    segments = [
        (w, 0, rows, [((w * groups + p,), 0) for p in range(groups)]) for w in range(3)
    ]
    making = dict(segments=segments, w_parent=w_parent, coarse=low + own + high)
    places = jnp.stack([0, 1, 2, 0, first_row]).astype(jnp.int32)
    sources = [((0, 0),)] + [((r, None),) for r in range(1, groups)]
    aux = cut(aux, first_row, per_device)
    aux = jnp.concatenate([aux[:-1], aux[-1:] - first_row])
    weights = cut(weights, first_row, per_device)
    result = fine_latent
    arrived = []
    for c, (start, length) in enumerate(shares(per_device)):
        pieces = [fine_latent]
        for r in range(1, groups):
            part = cut(fine_latent, ((rank + r) % groups) * per_device + start, length)
            pieces.append(turn(after(part, own[-1]), r))
        outs = run(start, length, aux, pieces, sources, weights, places, **(making if c == 0 else dict(table=table)))
        table = outs[-1] if c == 0 else table
        result = lax.dynamic_update_slice_in_dim(result, outs[0], first_row + start, 1)
        for r in range(1, groups):
            arrived.append((turn(outs[r], -r), ((rank + r) % groups) * per_device + start))
    for part, at in arrived:
        result = lax.dynamic_update_slice_in_dim(result, part, at, 1)
    return result


def paired(fine_latent, coarse_latent, aux, weights, w_parent, run):
    domains = lax.axis_size("dom")
    side, rank = lax.axis_index("dom") % 2, lax.axis_index("feat")
    matched = side == rank
    pairs = range(domains // 2)

    def send(value, moves):
        perm = [((2 * c + a) * 2 + b, (2 * c + x) * 2 + y) for c in pairs for (a, b), (x, y) in moves]
        return lax.ppermute(value, ("dom", "feat"), perm)

    def swap_rank(value):
        return send(value, [((k, f), (k, 1 - f)) for k in range(2) for f in range(2)])

    def swap_side(value):
        return send(value, [((k, f), (1 - k, f)) for k in range(2) for f in range(2)])

    def halo(value):
        perm = [((2 * c - 1) * 2, (2 * c) * 2) for c in pairs if c > 0]
        perm += [((2 * c + 2) * 2 + 1, (2 * c + 1) * 2 + 1) for c in pairs if c + 1 < len(pairs)]
        return lax.ppermute(value, ("dom", "feat"), perm)

    def hand_over(value):
        return send(value, [((0, 0), (1, 0)), ((1, 1), (0, 1))])

    to_first = [((0, 0), (1, 0)), ((1, 1), (0, 1)), ((0, 1), (0, 0)), ((1, 0), (1, 1))]
    from_first = [(b, a) for a, b in to_first]
    to_second = [((0, 1), (1, 0)), ((1, 0), (0, 1))]

    half = fine_latent.shape[1] // 2
    mine = side * half
    rows = coarse_latent.shape[1]
    part = rows // PARTS
    mate = []
    for i in range(PARTS):
        piece = lax.slice_in_dim(coarse_latent, i * part, (i + 1) * part, axis=1)
        mate.append(swap_rank(after(piece, mate[-1]) if mate else piece))
    halo_own, other = halo(coarse_latent), swap_side(after(coarse_latent, mate[-1]))
    halo_mate, other_mate = [halo(piece) for piece in mate], [swap_side(piece) for piece in mate]
    passed_own, passed_mate = hand_over(halo_own), [hand_over(piece) for piece in halo_mate]
    coarse = [coarse_latent, other, halo_own, passed_own, *mate, *other_mate, *halo_mate, *passed_mate]
    segments = []
    for window, own in enumerate([(0,), (1,), (2, 3)]):
        for i in range(PARTS):
            came = tuple(4 + (w + window) * PARTS + i for w in range(len(own)))
            segments.append((window, i * part, part, [(own, i * part), (came, 0)]))
    places = jnp.stack([side + 1 - rank, 2 - side - rank, 2 * rank, jnp.where(matched, 0, 1), mine])
    places = places.astype(jnp.int32)

    chunks = []
    for start, length in shares(half):
        extra = max(half // 2 - length, 0)
        first = cut(fine_latent, jnp.where(matched, half - mine, mine) + start - extra, length + extra)
        second = cut(fine_latent, half - mine + start - extra, length + extra)
        first, second = send(after(first, mate[-1]), to_first), send(after(second, mate[-1]), to_second)
        chunks.append([first, fine_latent, second])

    both = jnp.concatenate([aux.astype(F32), weights])
    both = jnp.where(matched, cut(both, mine, half), hand_over(cut(both, half - mine, half)))
    aux, weights = both[: aux.shape[0]].astype(jnp.int32), both[aux.shape[0] :]
    aux = jnp.concatenate([aux[:-1], aux[-1:] - mine])

    making = dict(segments=segments, w_parent=w_parent, coarse=coarse)
    sources = [((0, None),), ((1, 0), (2, None))]
    result = jnp.zeros_like(fine_latent)
    moved = []
    for c, (start, length) in enumerate(shares(half)):
        out, kept, *made = run(
            start, length, aux, chunks[c], sources, weights, places, **(making if c == 0 else dict(table=table))
        )
        table = made[0] if made else table
        moved.append((start, kept, send(out, from_first), send(kept, to_second)))
    for start, kept, first, second in moved:
        result = lax.dynamic_update_slice_in_dim(result, jnp.where(matched, kept, first), mine + start, 1)
        result = lax.dynamic_update_slice_in_dim(
            result, jnp.where(matched, first, second), half - mine + start, 1
        )
    return result


def shards(
    fine_latent,
    coarse_latent,
    parents,
    interp_weights,
    live_rows,
    w_fine,
    w_parent,
    w_edge_out,
    w_node_fine,
    w_node_agg,
    w_node_out,
    edge_bias,
    node_bias,
    norm_gain,
    norm_bias,
):
    groups, domains = lax.axis_size("feat"), lax.axis_size("dom")
    rank = lax.axis_index("feat")
    own_features = fine_latent.shape[0]
    owners = [(rank - r) % groups for r in range(groups)]
    pairing = groups == 2 and domains % 2 == 0
    flip = jnp.where(lax.axis_index("dom") % 2 == rank, 1, 0) if pairing else 0

    def ordered(weight, axis, flip=flip):
        parts = [lax.dynamic_slice_in_dim(weight, o * own_features, own_features, axis) for o in owners]
        if pairing:
            parts = [jnp.where(flip == 1, parts[1], parts[0]), jnp.where(flip == 1, parts[0], parts[1])]
        return jnp.concatenate(parts, axis=axis)

    params = (
        ordered(w_fine, 0),
        ordered(w_node_fine, 0),
        w_edge_out,
        w_node_agg,
        ordered(w_node_out, 1).T,
        edge_bias[None],
        node_bias[None],
        jnp.broadcast_to(ordered(norm_gain, 0)[:, None], (norm_gain.shape[0], 128)),
        jnp.broadcast_to(ordered(norm_bias, 0)[:, None], (norm_bias.shape[0], 128)),
    )

    def run(start, nodes, aux, arrays, sources, weights, places, **table):
        scales = jnp.pad(weights, ((0, 8 - weights.shape[0]), (0, 0)))
        return update(start, nodes, aux, arrays, sources, scales, params, places, **table)

    count = parents.shape[1]
    slots = 2 * parents + (PAD - 2 * (jnp.arange(count, dtype=jnp.int32) % 4))
    aux = jnp.concatenate([slots, jnp.broadcast_to(live_rows[:, None], (1, count))])
    plan = paired if pairing else plain
    return plan(fine_latent, coarse_latent, aux, interp_weights, ordered(w_parent, 0, 0), run)


def solution(mesh):
    in_specs = (P("feat", "dom"), P("feat", "dom"), P(None, "dom"), P(None, "dom"), P("dom")) + (P(),) * 10
    return jax.shard_map(shards, mesh=mesh, in_specs=in_specs, out_specs=P("feat", "dom"), check_vma=False)
```

```python
import functools

import jax
import jax.numpy as jnp
from jax import lax
from jax.experimental import pallas as pl
from jax.experimental.pallas import tpu as pltpu
from jax.sharding import PartitionSpec as P

F32 = jnp.float32
BF16 = jnp.bfloat16
PAD = 8
SHARE = 4
PARTS = 1
STEP = 256
GROUPS = 13


def dot(a, b, ca, cb):
    return lax.dot_general(a, b, (((ca,), (cb,)), ((), ())), preferred_element_type=F32)


def fill_table(segments, step, places, refs, weight, table, landed, sems):
    rows = (table.shape[0] - 2 * PAD) // 6
    features = landed.shape[2] // sems.shape[2]
    table[pl.ds(0, PAD), :] = jnp.zeros((PAD, 128), F32)
    table[pl.ds(PAD + 6 * rows, PAD), :] = jnp.zeros((PAD, 128), F32)

    def copies(segment, i, slot, which):
        found = []
        for p, (sources, first) in enumerate(segments[segment][3]):
            at = pl.multiple_of(first + i * step, 128)
            found.append(
                pltpu.make_async_copy(
                    refs[sources[min(which, len(sources) - 1)]].at[:, pl.ds(at, step)],
                    landed.at[segment % 2, slot, pl.ds(p * features, features), :],
                    sems.at[segment % 2, slot, p],
                )
            )
        return found

    def start(segment, i, slot):
        if all(len(sources) == 1 for sources, _ in segments[segment][3]):
            for copy in copies(segment, i, slot, 0):
                copy.start()
            return
        for which in range(2):

            @pl.when(places[3] == which)
            def _(which=which):
                for copy in copies(segment, i, slot, which):
                    copy.start()

    start(0, 0, 0)
    for segment, (window, row, length, _) in enumerate(segments):
        steps = length // step
        if segment + 1 < len(segments):
            start(segment + 1, 0, 0)

        def one(i, carry, segment=segment, window=window, row=row, steps=steps):
            slot = lax.rem(i, 2)

            @pl.when(i + 1 < steps)
            def _():
                start(segment, i + 1, 1 - slot)

            for copy in copies(segment, i, slot, 0):
                copy.wait()
            projected = dot(landed[segment % 2, slot], weight[...], 0, 0)
            base = pl.multiple_of(PAD + 2 * (places[window] * rows + row + i * step), 8)
            table[pl.ds(base, step, stride=2), :] = projected[:, :128]
            table[pl.ds(base + 1, step, stride=2), :] = projected[:, 128:]
            return carry

        lax.fori_loop(0, steps, one, 0)


def update_kernel(sources, step, start, segments, table_step, places, aux, *refs):
    count = len(sources)
    given = 1 + max(at for source in sources for at, _ in source)
    arrays, refs = refs[:given], refs[given:]
    given, refs = refs[:8], refs[8:]
    held_here, refs = refs[-8:], refs[:-8]
    scales, w_latent, w_edge, w_agg, w_out_t, bias, gain, shift = held_here
    table, latents, fine, total, earlier, later, scale_rows, slots, live, sems, given_sems = refs[-11:]
    refs = refs[:-11]
    fetches = [
        pltpu.make_async_copy(far if at else far.at[:, pl.ds(start, near.shape[1])], near, given_sems.at[at])
        for at, (far, near) in enumerate(zip(given, held_here))
    ]
    features, nodes = latents.shape[0] // count, latents.shape[1]
    parents = slots.shape[0] // nodes
    if segments is None:
        kept, outs = refs[0], refs[1:]
        move = pltpu.make_async_copy(kept, table, sems.at[parents + 1 + count])
        move.start()
    else:
        w_parent, *coarse = refs[: -count - 3]
        *outs, kept, landed, landed_sems = refs[-count - 3 :]
        move = pltpu.make_async_copy(table, kept, sems.at[parents + 1 + count])
    held = aux.shape[0] // (parents + 1)
    fetches.append(pltpu.make_async_copy(aux.at[pl.ds(parents * start, parents * nodes)], slots, sems.at[0]))
    fetches.append(pltpu.make_async_copy(aux.at[pl.ds(parents * held, 1024)], live, sems.at[parents]))
    for fetch in fetches:
        fetch.start()

    def bring(p, which):
        at, shifted = sources[p][min(which, len(sources[p]) - 1)]
        column = arrays[at].shape[1] - nodes if shifted is None else pl.multiple_of(places[4] + start, 128)
        return pltpu.make_async_copy(
            arrays[at].at[:, pl.ds(column, nodes)],
            latents.at[pl.ds(p * features, features), :],
            sems.at[parents + 1 + p],
        )

    for p, source in enumerate(sources):
        for which in range(len(source)):

            @pl.when((places[3] == which) | (len(source) == 1))
            def _(p=p, which=which):
                bring(p, which).start()

    if segments is not None:
        fill_table(segments, table_step, places, coarse, w_parent, table, landed, landed_sems)
        move.start()
    for fetch in fetches:
        fetch.wait()
    for p in range(count):
        bring(p, 0).wait()
    if segments is None:
        move.wait()
    sublane = lax.broadcasted_iota(jnp.int32, (8, 128), 0)
    owns = [sublane >= 2 * j for j in range(4)]

    def begin(i):
        columns = pl.ds(pl.multiple_of(i * step, step), step)
        first = dot(latents[:, columns], w_latent[...], 0, 0) + bias[...]
        return first, scales[:, pl.ds(pl.multiple_of(i * step, step), step)].T

    def keep(first, scale_columns):
        width = first.shape[1] // 2
        fine[pl.ds(0, step, stride=2), :] = first[:, :128]
        fine[pl.ds(1, step, stride=2), :] = first[:, 128:width]
        later[...] = first[:, width:]
        scale_rows[pl.ds(0, step, stride=2), :] = scale_columns
        scale_rows[pl.ds(1, step, stride=2), :] = scale_columns

    def group(at, g):
        part = fine[pl.ds(g * 8, 8), :]
        scale = scale_rows[pl.ds(g * 8, 8), :]
        acc = None
        for k in range(parents):
            low = high = None
            for j in range(4):
                word = slots[at + (k * step + g * 4 + j)]
                loaded = table[pl.ds(word & 0xFFFF, 8), :]
                low = loaded if low is None else jnp.where(owns[j], loaded, low)
                loaded = table[pl.ds(lax.shift_right_logical(word, 16), 8), :]
                high = loaded if high is None else jnp.where(owns[j], loaded, high)
            for way, rows in ((2 * k, low), (2 * k + 1, high)):
                hidden = jnp.maximum(part + rows, 0.0) * scale[:, way : way + 1]
                acc = hidden if acc is None else acc + hidden
        return acc

    def widened(ref):
        return jnp.concatenate([ref[...]] * (step // 128), axis=1)

    def finish(i, summed, own_part):
        at = pl.multiple_of(i * step, step)
        aggregate = dot(summed.astype(BF16), w_edge[...], 1, 0).astype(BF16)
        yield
        node_hidden = jnp.maximum(own_part + dot(aggregate, w_agg[...], 1, 0), 0.0).astype(BF16)
        yield
        output = dot(w_out_t[...], node_hidden, 1, 1)
        yield
        centered = output - jnp.mean(output, axis=0, keepdims=True)
        spread = jnp.mean(centered * centered, axis=0, keepdims=True)
        yield
        normed = centered * lax.rsqrt(spread + 1e-05) * widened(gain) + widened(shift)
        column = start + at + lax.broadcasted_iota(jnp.int32, (1, step), 1)
        moved = jnp.where(column < live[0], normed, 0.0)
        yield (latents[:, pl.ds(at, step)].astype(F32) + moved).astype(BF16)

    def last(parts):
        for value in parts:
            pass
        return value

    def write(i, result):
        for r in range(count):
            outs[r][:, pl.ds(pl.multiple_of(i * step, step), step)] = result[r * features : (r + 1) * features]

    def gathered():
        return jnp.concatenate([total[pl.ds(0, step, stride=2), :], total[pl.ds(1, step, stride=2), :]], axis=1)

    steps = nodes // step
    keep(*begin(0))

    def one_step(i, carry):
        before, after = jnp.maximum(i - 1, 0), jnp.minimum(i + 1, steps - 1)
        summed, own_part, current = gathered(), earlier[...], later[...]
        parts = finish(before, summed, own_part)
        base = pl.multiple_of(i * (parents * step), parents * step)
        begun = begin(after)
        for first in range(0, step // 4, GROUPS):
            result = next(parts, None) if first < 4 * GROUPS else last(parts)
            sums = [group(base, g) for g in range(first, min(first + GROUPS, step // 4))]
            total[pl.ds(first * 8, len(sums) * 8), :] = jnp.concatenate(sums, axis=0)
        write(before, result)
        earlier[...] = current
        keep(*begun)
        return carry

    lax.fori_loop(0, steps, one_step, 0)
    write(steps - 1, last(finish(steps - 1, gathered(), earlier[...])))
    if segments is not None:
        move.wait()


def by_step(aux, step):
    slots = aux[:-1].reshape(aux.shape[0] - 1, -1, step).transpose(1, 0, 2)
    return jnp.concatenate([slots.reshape(-1), aux[-1]])


def update(
    start, nodes, aux, arrays, sources, scales, params, places, table=None, segments=None, w_parent=None, coarse=()
):
    count, features = len(sources), arrays[0].shape[0]
    aux = jnp.concatenate([aux[0:-1:2] | (aux[1:-1:2] << 16), aux[-1:]])
    parents = aux.shape[0] - 1
    step = min(STEP, nodes)
    vmem = pl.BlockSpec(memory_space=pltpu.VMEM)
    smem = pl.BlockSpec(memory_space=pltpu.SMEM)
    far = pl.BlockSpec(memory_space=pltpu.HBM)
    out_shape = [jax.ShapeDtypeStruct((features, nodes), BF16)] * count
    operands = [places, by_step(aux, step), *arrays, scales, *params]
    specs = [smem, far] + [far] * (len(arrays) + 1 + len(params))
    scratch, table_step = [], 0
    if segments is None:
        operands, specs = operands + [table], specs + [far]
    else:
        operands, specs = operands + [w_parent, *coarse], specs + [vmem] + [far] * len(coarse)
        table_step = min(2048, segments[0][2])
        table = jax.ShapeDtypeStruct((2 * sum(segment[2] for segment in segments) + 2 * PAD, 128), F32)
        out_shape.append(table)
        scratch = [
            pltpu.VMEM((2, 2, w_parent.shape[0], table_step), BF16),
            pltpu.SemaphoreType.DMA((2, 2, len(segments[0][3]))),
        ]
    return pl.pallas_call(
        functools.partial(update_kernel, sources, step, start, segments, table_step),
        out_shape=out_shape,
        in_specs=specs,
        out_specs=[vmem] * count + [far] * (len(out_shape) - count),
        scratch_shapes=scratch
        + [
            pltpu.VMEM(table.shape, F32),
            pltpu.VMEM((count * features, nodes), BF16),
            pltpu.VMEM((2 * step, 128), F32),
            pltpu.VMEM((2 * step, 128), F32),
            pltpu.VMEM((step, 256), F32),
            pltpu.VMEM((step, 256), F32),
            pltpu.VMEM((2 * step, 8), F32),
            pltpu.SMEM((parents * nodes,), jnp.int32),
            pltpu.SMEM((1024,), jnp.int32),
            pltpu.SemaphoreType.DMA((parents + 2 + count,)),
            pltpu.SemaphoreType.DMA((1 + len(params),)),
            pltpu.VMEM((scales.shape[0], nodes), F32),
        ]
        + [pltpu.VMEM(param.shape, param.dtype) for param in params],
        compiler_params=pltpu.CompilerParams(vmem_limit_bytes=40 << 20),
        cost_estimate=pl.CostEstimate(flops=nodes * 700000, bytes_accessed=nodes * 2048, transcendentals=nodes),
    )(*operands)


def after(value, *others):
    return lax.optimization_barrier((value, *others))[0]


def shares(nodes):
    first = nodes * SHARE // 8 // STEP * STEP
    return [(0, first), (first, nodes - first)]


def cut(array, at, size):
    return lax.dynamic_slice_in_dim(array, at, size, 1)


def plain(fine_latent, coarse_latent, aux, weights, w_parent, run):
    groups, domains = lax.axis_size("feat"), lax.axis_size("dom")
    rank = lax.axis_index("feat")
    per_device = fine_latent.shape[1] // groups
    forward = [(i, i + 1) for i in range(domains - 1)]
    backward = [(i + 1, i) for i in range(domains - 1)]

    def turn(value, r):
        return lax.ppermute(value, "feat", [(i, (i + r) % groups) for i in range(groups)])

    own = [coarse_latent] + [turn(coarse_latent, r) for r in range(1, groups)]
    low = [lax.ppermute(piece, "dom", forward) for piece in own]
    high = [lax.ppermute(piece, "dom", backward) for piece in own]
    first_row = rank * per_device
    rows = coarse_latent.shape[1]
    segments = [
        (w, 0, rows, [((w * groups + p,), 0) for p in range(groups)]) for w in range(3)
    ]
    making = dict(segments=segments, w_parent=w_parent, coarse=low + own + high)
    places = jnp.stack([0, 1, 2, 0, first_row]).astype(jnp.int32)
    sources = [((0, 0),)] + [((r, None),) for r in range(1, groups)]
    aux = cut(aux, first_row, per_device)
    aux = jnp.concatenate([aux[:-1], aux[-1:] - first_row])
    weights = cut(weights, first_row, per_device)
    result = fine_latent
    arrived = []
    for c, (start, length) in enumerate(shares(per_device)):
        pieces = [fine_latent]
        for r in range(1, groups):
            part = cut(fine_latent, ((rank + r) % groups) * per_device + start, length)
            pieces.append(turn(after(part, own[-1]), r))
        outs = run(start, length, aux, pieces, sources, weights, places, **(making if c == 0 else dict(table=table)))
        table = outs[-1] if c == 0 else table
        result = lax.dynamic_update_slice_in_dim(result, outs[0], first_row + start, 1)
        for r in range(1, groups):
            arrived.append((turn(outs[r], -r), ((rank + r) % groups) * per_device + start))
    for part, at in arrived:
        result = lax.dynamic_update_slice_in_dim(result, part, at, 1)
    return result


def paired(fine_latent, coarse_latent, aux, weights, w_parent, run):
    domains = lax.axis_size("dom")
    side, rank = lax.axis_index("dom") % 2, lax.axis_index("feat")
    matched = side == rank
    pairs = range(domains // 2)

    def send(value, moves):
        perm = [((2 * c + a) * 2 + b, (2 * c + x) * 2 + y) for c in pairs for (a, b), (x, y) in moves]
        return lax.ppermute(value, ("dom", "feat"), perm)

    def swap_rank(value):
        return send(value, [((k, f), (k, 1 - f)) for k in range(2) for f in range(2)])

    def swap_side(value):
        return send(value, [((k, f), (1 - k, f)) for k in range(2) for f in range(2)])

    def halo(value):
        perm = [((2 * c - 1) * 2, (2 * c) * 2) for c in pairs if c > 0]
        perm += [((2 * c + 2) * 2 + 1, (2 * c + 1) * 2 + 1) for c in pairs if c + 1 < len(pairs)]
        return lax.ppermute(value, ("dom", "feat"), perm)

    def hand_over(value):
        return send(value, [((0, 0), (1, 0)), ((1, 1), (0, 1))])

    to_first = [((0, 0), (1, 0)), ((1, 1), (0, 1)), ((0, 1), (0, 0)), ((1, 0), (1, 1))]
    from_first = [(b, a) for a, b in to_first]
    to_second = [((0, 1), (1, 0)), ((1, 0), (0, 1))]

    half = fine_latent.shape[1] // 2
    mine = side * half
    rows = coarse_latent.shape[1]
    part = rows // PARTS
    mate = []
    for i in range(PARTS):
        piece = lax.slice_in_dim(coarse_latent, i * part, (i + 1) * part, axis=1)
        mate.append(swap_rank(after(piece, mate[-1]) if mate else piece))
    halo_own, other = halo(coarse_latent), swap_side(after(coarse_latent, mate[-1]))
    halo_mate, other_mate = [halo(piece) for piece in mate], [swap_side(piece) for piece in mate]
    passed_own, passed_mate = hand_over(halo_own), [hand_over(piece) for piece in halo_mate]
    coarse = [coarse_latent, other, halo_own, passed_own, *mate, *other_mate, *halo_mate, *passed_mate]
    segments = []
    for window, own in enumerate([(0,), (1,), (2, 3)]):
        for i in range(PARTS):
            came = tuple(4 + (w + window) * PARTS + i for w in range(len(own)))
            segments.append((window, i * part, part, [(own, i * part), (came, 0)]))
    places = jnp.stack([side + 1 - rank, 2 - side - rank, 2 * rank, jnp.where(matched, 0, 1), mine])
    places = places.astype(jnp.int32)

    chunks = []
    for start, length in shares(half):
        extra = max(half // 2 - length, 0)
        first = cut(fine_latent, jnp.where(matched, half - mine, mine) + start - extra, length + extra)
        second = cut(fine_latent, half - mine + start - extra, length + extra)
        first, second = send(after(first, mate[-1]), to_first), send(after(second, mate[-1]), to_second)
        chunks.append([first, fine_latent, second])

    both = jnp.concatenate([aux.astype(F32), weights])
    both = jnp.where(matched, cut(both, mine, half), hand_over(cut(both, half - mine, half)))
    aux, weights = both[: aux.shape[0]].astype(jnp.int32), both[aux.shape[0] :]
    aux = jnp.concatenate([aux[:-1], aux[-1:] - mine])

    making = dict(segments=segments, w_parent=w_parent, coarse=coarse)
    sources = [((0, None),), ((1, 0), (2, None))]
    result = jnp.zeros_like(fine_latent)
    moved = []
    for c, (start, length) in enumerate(shares(half)):
        out, kept, *made = run(
            start, length, aux, chunks[c], sources, weights, places, **(making if c == 0 else dict(table=table))
        )
        table = made[0] if made else table
        moved.append((start, kept, send(out, from_first), send(kept, to_second)))
    for start, kept, first, second in moved:
        result = lax.dynamic_update_slice_in_dim(result, jnp.where(matched, kept, first), mine + start, 1)
        result = lax.dynamic_update_slice_in_dim(
            result, jnp.where(matched, first, second), half - mine + start, 1
        )
    return result


def shards(
    fine_latent,
    coarse_latent,
    parents,
    interp_weights,
    live_rows,
    w_fine,
    w_parent,
    w_edge_out,
    w_node_fine,
    w_node_agg,
    w_node_out,
    edge_bias,
    node_bias,
    norm_gain,
    norm_bias,
):
    groups, domains = lax.axis_size("feat"), lax.axis_size("dom")
    rank = lax.axis_index("feat")
    own_features = fine_latent.shape[0]
    owners = [(rank - r) % groups for r in range(groups)]
    pairing = groups == 2 and domains % 2 == 0
    flip = jnp.where(lax.axis_index("dom") % 2 == rank, 1, 0) if pairing else 0

    def ordered(weight, axis, flip=flip):
        parts = [lax.dynamic_slice_in_dim(weight, o * own_features, own_features, axis) for o in owners]
        if pairing:
            parts = [jnp.where(flip == 1, parts[1], parts[0]), jnp.where(flip == 1, parts[0], parts[1])]
        return jnp.concatenate(parts, axis=axis)

    params = (
        jnp.concatenate([ordered(w_fine, 0), ordered(w_node_fine, 0)], axis=1),
        w_edge_out,
        w_node_agg,
        ordered(w_node_out, 1).T,
        jnp.concatenate([edge_bias, node_bias])[None],
        jnp.broadcast_to(ordered(norm_gain, 0)[:, None], (norm_gain.shape[0], 128)),
        jnp.broadcast_to(ordered(norm_bias, 0)[:, None], (norm_bias.shape[0], 128)),
    )

    def run(start, nodes, aux, arrays, sources, weights, places, **table):
        scales = jnp.pad(weights, ((0, 8 - weights.shape[0]), (0, 0)))
        return update(start, nodes, aux, arrays, sources, scales, params, places, **table)

    count = parents.shape[1]
    slots = 2 * parents + (PAD - 2 * (jnp.arange(count, dtype=jnp.int32) % 4))
    aux = jnp.concatenate([slots, jnp.broadcast_to(live_rows[:, None], (1, count))])
    plan = paired if pairing else plain
    return plan(fine_latent, coarse_latent, aux, interp_weights, ordered(w_parent, 0, 0), run)


def solution(mesh):
    in_specs = (P("feat", "dom"), P("feat", "dom"), P(None, "dom"), P(None, "dom"), P("dom")) + (P(),) * 10
    return jax.shard_map(shards, mesh=mesh, in_specs=in_specs, out_specs=P("feat", "dom"), check_vma=False)
```

```python
import functools

import jax
import jax.numpy as jnp
from jax import lax
from jax.experimental import pallas as pl
from jax.experimental.pallas import tpu as pltpu
from jax.sharding import PartitionSpec as P

F32 = jnp.float32
BF16 = jnp.bfloat16
PAD = 8
SHARE = 4
PARTS = 1
STEP = 256
GROUPS = 13


def dot(a, b, ca, cb):
    return lax.dot_general(a, b, (((ca,), (cb,)), ((), ())), preferred_element_type=F32)


def fill_table(segments, step, places, refs, weight, table, landed, sems):
    rows = (table.shape[0] - 2 * PAD) // 6
    features = landed.shape[2] // sems.shape[2]
    table[pl.ds(0, PAD), :] = jnp.zeros((PAD, 128), F32)
    table[pl.ds(PAD + 6 * rows, PAD), :] = jnp.zeros((PAD, 128), F32)

    def copies(segment, i, slot, which):
        found = []
        for p, (sources, first) in enumerate(segments[segment][3]):
            at = pl.multiple_of(first + i * step, 128)
            found.append(
                pltpu.make_async_copy(
                    refs[sources[min(which, len(sources) - 1)]].at[:, pl.ds(at, step)],
                    landed.at[segment % 2, slot, pl.ds(p * features, features), :],
                    sems.at[segment % 2, slot, p],
                )
            )
        return found

    def start(segment, i, slot):
        if all(len(sources) == 1 for sources, _ in segments[segment][3]):
            for copy in copies(segment, i, slot, 0):
                copy.start()
            return
        for which in range(2):

            @pl.when(places[3] == which)
            def _(which=which):
                for copy in copies(segment, i, slot, which):
                    copy.start()

    start(0, 0, 0)
    for segment, (window, row, length, _) in enumerate(segments):
        steps = length // step
        if segment + 1 < len(segments):
            start(segment + 1, 0, 0)

        def one(i, carry, segment=segment, window=window, row=row, steps=steps):
            slot = lax.rem(i, 2)

            @pl.when(i + 1 < steps)
            def _():
                start(segment, i + 1, 1 - slot)

            for copy in copies(segment, i, slot, 0):
                copy.wait()
            projected = dot(landed[segment % 2, slot], weight[...], 0, 0)
            base = pl.multiple_of(PAD + 2 * (places[window] * rows + row + i * step), 8)
            table[pl.ds(base, step, stride=2), :] = projected[:, :128]
            table[pl.ds(base + 1, step, stride=2), :] = projected[:, 128:]
            return carry

        lax.fori_loop(0, steps, one, 0)


def update_kernel(sources, step, start, segments, table_step, places, aux, *refs):
    count = len(sources)
    given = 1 + max(at for source in sources for at, _ in source)
    arrays, refs = refs[:given], refs[given:]
    given, refs = refs[:8], refs[8:]
    held_here, refs = refs[-8:], refs[:-8]
    scales, w_latent, w_edge, w_agg, w_out_t, bias, gain, shift = held_here
    table, latents, fine, total, earlier, later, scale_rows, slots, live, sems, given_sems, *buffers = refs[-13:]
    refs = refs[:-13]
    fetches = [
        pltpu.make_async_copy(far if at else far.at[:, pl.ds(start, near.shape[1])], near, given_sems.at[at])
        for at, (far, near) in enumerate(zip(given, held_here))
    ]
    features, nodes = latents.shape[0] // count, latents.shape[1]
    parents = slots.shape[0] // nodes
    if segments is None:
        kept, outs = refs[0], refs[1:]
        move = pltpu.make_async_copy(kept, table, sems.at[parents + 1 + count])
        move.start()
    else:
        w_parent, *coarse = refs[: -count - 3]
        *outs, kept, landed, landed_sems = refs[-count - 3 :]
        move = pltpu.make_async_copy(table, kept, sems.at[parents + 1 + count])
    held = aux.shape[0] // (parents + 1)
    fetches.append(pltpu.make_async_copy(aux.at[pl.ds(parents * start, parents * nodes)], slots, sems.at[0]))
    fetches.append(pltpu.make_async_copy(aux.at[pl.ds(parents * held, 1024)], live, sems.at[parents]))
    for fetch in fetches:
        fetch.start()

    def bring(p, which):
        at, shifted = sources[p][min(which, len(sources[p]) - 1)]
        column = arrays[at].shape[1] - nodes if shifted is None else pl.multiple_of(places[4] + start, 128)
        return pltpu.make_async_copy(
            arrays[at].at[:, pl.ds(column, nodes)],
            latents.at[pl.ds(p * features, features), :],
            sems.at[parents + 1 + p],
        )

    for p, source in enumerate(sources):
        for which in range(len(source)):

            @pl.when((places[3] == which) | (len(source) == 1))
            def _(p=p, which=which):
                bring(p, which).start()

    if segments is not None:
        fill_table(segments, table_step, places, coarse, w_parent, table, landed, landed_sems)
        move.start()
    for fetch in fetches:
        fetch.wait()
    for p in range(count):
        bring(p, 0).wait()
    if segments is None:
        move.wait()
    origin = places[0] // 8

    def begin(i):
        columns = pl.ds(pl.multiple_of(i * step, step), step)
        first = dot(latents[:, columns], w_latent[...], 0, 0) + bias[...]
        return first, scales[:, pl.ds(pl.multiple_of(i * step, step), step)].T

    def keep(first, scale_columns):
        width = first.shape[1] // 2
        fine[pl.ds(0, step, stride=2), :] = first[:, :128]
        fine[pl.ds(1, step, stride=2), :] = first[:, 128:width]
        later[...] = first[:, width:]
        scale_rows[pl.ds(0, step, stride=2), :] = scale_columns
        scale_rows[pl.ds(1, step, stride=2), :] = scale_columns

    def fetch_rows(at, groups, buffer):
        for here, g in enumerate(groups):
            for k in range(parents):
                for j in range(4):
                    to = origin + ((k * GROUPS + here) * 8 + 2 * j)
                    buffer[pl.ds(to, 2), :] = table[pl.ds(slots[at + (k * step + g * 4 + j)], 2), :]

    def sum_rows(groups, buffer):
        sums = []
        for here, g in enumerate(groups):
            part = fine[pl.ds(g * 8, 8), :]
            scale = scale_rows[pl.ds(g * 8, 8), :]
            acc = None
            for k in range(parents):
                rows = buffer[pl.ds((k * GROUPS + here) * 8, 8), :]
                hidden = jnp.maximum(part + rows, 0.0) * scale[:, k : k + 1]
                acc = hidden if acc is None else acc + hidden
            sums.append(acc)
        total[pl.ds(groups[0] * 8, len(sums) * 8), :] = jnp.concatenate(sums, axis=0)

    def widened(ref):
        return jnp.concatenate([ref[...]] * (step // 128), axis=1)

    def finish(i, summed, own_part):
        at = pl.multiple_of(i * step, step)
        aggregate = dot(summed.astype(BF16), w_edge[...], 1, 0).astype(BF16)
        yield
        node_hidden = jnp.maximum(own_part + dot(aggregate, w_agg[...], 1, 0), 0.0).astype(BF16)
        yield
        output = dot(w_out_t[...], node_hidden, 1, 1)
        yield
        centered = output - jnp.mean(output, axis=0, keepdims=True)
        spread = jnp.mean(centered * centered, axis=0, keepdims=True)
        yield
        normed = centered * lax.rsqrt(spread + 1e-05) * widened(gain) + widened(shift)
        column = start + at + lax.broadcasted_iota(jnp.int32, (1, step), 1)
        moved = jnp.where(column < live[0], normed, 0.0)
        yield (latents[:, pl.ds(at, step)].astype(F32) + moved).astype(BF16)

    def last(parts):
        for value in parts:
            pass
        return value

    def write(i, result):
        for r in range(count):
            outs[r][:, pl.ds(pl.multiple_of(i * step, step), step)] = result[r * features : (r + 1) * features]

    def gathered():
        return jnp.concatenate([total[pl.ds(0, step, stride=2), :], total[pl.ds(1, step, stride=2), :]], axis=1)

    steps = nodes // step
    keep(*begin(0))

    def one_step(i, carry):
        before, after = jnp.maximum(i - 1, 0), jnp.minimum(i + 1, steps - 1)
        summed, own_part, current = gathered(), earlier[...], later[...]
        parts = finish(before, summed, own_part)
        base = pl.multiple_of(i * (parents * step), parents * step)
        begun = begin(after)
        for at, first in enumerate(range(0, step // 4, GROUPS)):
            result = next(parts, None) if first < 4 * GROUPS else last(parts)
            groups = range(first, min(first + GROUPS, step // 4))
            fetch_rows(base, groups, buffers[at % 2])
            sum_rows(groups, buffers[at % 2])
        write(before, result)
        earlier[...] = current
        keep(*begun)
        return carry

    lax.fori_loop(0, steps, one_step, 0)
    write(steps - 1, last(finish(steps - 1, gathered(), earlier[...])))
    if segments is not None:
        move.wait()


def by_step(aux, step):
    slots = aux[:-1].reshape(aux.shape[0] - 1, -1, step).transpose(1, 0, 2)
    return jnp.concatenate([slots.reshape(-1), aux[-1]])


def update(
    start, nodes, aux, arrays, sources, scales, params, places, table=None, segments=None, w_parent=None, coarse=()
):
    count, features = len(sources), arrays[0].shape[0]
    parents = aux.shape[0] - 1
    step = min(STEP, nodes)
    vmem = pl.BlockSpec(memory_space=pltpu.VMEM)
    smem = pl.BlockSpec(memory_space=pltpu.SMEM)
    far = pl.BlockSpec(memory_space=pltpu.HBM)
    out_shape = [jax.ShapeDtypeStruct((features, nodes), BF16)] * count
    operands = [places, by_step(aux, step), *arrays, scales, *params]
    specs = [smem, far] + [far] * (len(arrays) + 1 + len(params))
    scratch, table_step = [], 0
    if segments is None:
        operands, specs = operands + [table], specs + [far]
    else:
        operands, specs = operands + [w_parent, *coarse], specs + [vmem] + [far] * len(coarse)
        table_step = min(2048, segments[0][2])
        table = jax.ShapeDtypeStruct((2 * sum(segment[2] for segment in segments) + 2 * PAD, 128), F32)
        out_shape.append(table)
        scratch = [
            pltpu.VMEM((2, 2, w_parent.shape[0], table_step), BF16),
            pltpu.SemaphoreType.DMA((2, 2, len(segments[0][3]))),
        ]
    return pl.pallas_call(
        functools.partial(update_kernel, sources, step, start, segments, table_step),
        out_shape=out_shape,
        in_specs=specs,
        out_specs=[vmem] * count + [far] * (len(out_shape) - count),
        scratch_shapes=scratch
        + [
            pltpu.VMEM(table.shape, F32),
            pltpu.VMEM((count * features, nodes), BF16),
            pltpu.VMEM((2 * step, 128), F32),
            pltpu.VMEM((2 * step, 128), F32),
            pltpu.VMEM((step, 256), F32),
            pltpu.VMEM((step, 256), F32),
            pltpu.VMEM((2 * step, 8), F32),
            pltpu.SMEM((parents * nodes,), jnp.int32),
            pltpu.SMEM((1024,), jnp.int32),
            pltpu.SemaphoreType.DMA((parents + 2 + count,)),
            pltpu.SemaphoreType.DMA((1 + len(params),)),
            pltpu.VMEM((parents * GROUPS * 8, 128), F32),
            pltpu.VMEM((parents * GROUPS * 8, 128), F32),
            pltpu.VMEM((scales.shape[0], nodes), F32),
        ]
        + [pltpu.VMEM(param.shape, param.dtype) for param in params],
        compiler_params=pltpu.CompilerParams(vmem_limit_bytes=40 << 20),
        cost_estimate=pl.CostEstimate(flops=nodes * 700000, bytes_accessed=nodes * 2048, transcendentals=nodes),
    )(*operands)


def after(value, *others):
    return lax.optimization_barrier((value, *others))[0]


def shares(nodes):
    first = nodes * SHARE // 8 // STEP * STEP
    return [(0, first), (first, nodes - first)]


def cut(array, at, size):
    return lax.dynamic_slice_in_dim(array, at, size, 1)


def plain(fine_latent, coarse_latent, aux, weights, w_parent, run):
    groups, domains = lax.axis_size("feat"), lax.axis_size("dom")
    rank = lax.axis_index("feat")
    per_device = fine_latent.shape[1] // groups
    forward = [(i, i + 1) for i in range(domains - 1)]
    backward = [(i + 1, i) for i in range(domains - 1)]

    def turn(value, r):
        return lax.ppermute(value, "feat", [(i, (i + r) % groups) for i in range(groups)])

    own = [coarse_latent] + [turn(coarse_latent, r) for r in range(1, groups)]
    low = [lax.ppermute(piece, "dom", forward) for piece in own]
    high = [lax.ppermute(piece, "dom", backward) for piece in own]
    first_row = rank * per_device
    rows = coarse_latent.shape[1]
    segments = [
        (w, 0, rows, [((w * groups + p,), 0) for p in range(groups)]) for w in range(3)
    ]
    making = dict(segments=segments, w_parent=w_parent, coarse=low + own + high)
    places = jnp.stack([0, 1, 2, 0, first_row]).astype(jnp.int32)
    sources = [((0, 0),)] + [((r, None),) for r in range(1, groups)]
    aux = cut(aux, first_row, per_device)
    aux = jnp.concatenate([aux[:-1], aux[-1:] - first_row])
    weights = cut(weights, first_row, per_device)
    result = fine_latent
    arrived = []
    for c, (start, length) in enumerate(shares(per_device)):
        pieces = [fine_latent]
        for r in range(1, groups):
            part = cut(fine_latent, ((rank + r) % groups) * per_device + start, length)
            pieces.append(turn(after(part, own[-1]), r))
        outs = run(start, length, aux, pieces, sources, weights, places, **(making if c == 0 else dict(table=table)))
        table = outs[-1] if c == 0 else table
        result = lax.dynamic_update_slice_in_dim(result, outs[0], first_row + start, 1)
        for r in range(1, groups):
            arrived.append((turn(outs[r], -r), ((rank + r) % groups) * per_device + start))
    for part, at in arrived:
        result = lax.dynamic_update_slice_in_dim(result, part, at, 1)
    return result


def paired(fine_latent, coarse_latent, aux, weights, w_parent, run):
    domains = lax.axis_size("dom")
    side, rank = lax.axis_index("dom") % 2, lax.axis_index("feat")
    matched = side == rank
    pairs = range(domains // 2)

    def send(value, moves):
        perm = [((2 * c + a) * 2 + b, (2 * c + x) * 2 + y) for c in pairs for (a, b), (x, y) in moves]
        return lax.ppermute(value, ("dom", "feat"), perm)

    def swap_rank(value):
        return send(value, [((k, f), (k, 1 - f)) for k in range(2) for f in range(2)])

    def swap_side(value):
        return send(value, [((k, f), (1 - k, f)) for k in range(2) for f in range(2)])

    def halo(value):
        perm = [((2 * c - 1) * 2, (2 * c) * 2) for c in pairs if c > 0]
        perm += [((2 * c + 2) * 2 + 1, (2 * c + 1) * 2 + 1) for c in pairs if c + 1 < len(pairs)]
        return lax.ppermute(value, ("dom", "feat"), perm)

    def hand_over(value):
        return send(value, [((0, 0), (1, 0)), ((1, 1), (0, 1))])

    to_first = [((0, 0), (1, 0)), ((1, 1), (0, 1)), ((0, 1), (0, 0)), ((1, 0), (1, 1))]
    from_first = [(b, a) for a, b in to_first]
    to_second = [((0, 1), (1, 0)), ((1, 0), (0, 1))]

    half = fine_latent.shape[1] // 2
    mine = side * half
    rows = coarse_latent.shape[1]
    part = rows // PARTS
    mate = []
    for i in range(PARTS):
        piece = lax.slice_in_dim(coarse_latent, i * part, (i + 1) * part, axis=1)
        mate.append(swap_rank(after(piece, mate[-1]) if mate else piece))
    halo_own, other = halo(coarse_latent), swap_side(after(coarse_latent, mate[-1]))
    halo_mate, other_mate = [halo(piece) for piece in mate], [swap_side(piece) for piece in mate]
    passed_own, passed_mate = hand_over(halo_own), [hand_over(piece) for piece in halo_mate]
    coarse = [coarse_latent, other, halo_own, passed_own, *mate, *other_mate, *halo_mate, *passed_mate]
    segments = []
    for window, own in enumerate([(0,), (1,), (2, 3)]):
        for i in range(PARTS):
            came = tuple(4 + (w + window) * PARTS + i for w in range(len(own)))
            segments.append((window, i * part, part, [(own, i * part), (came, 0)]))
    places = jnp.stack([side + 1 - rank, 2 - side - rank, 2 * rank, jnp.where(matched, 0, 1), mine])
    places = places.astype(jnp.int32)

    chunks = []
    for start, length in shares(half):
        extra = max(half // 2 - length, 0)
        first = cut(fine_latent, jnp.where(matched, half - mine, mine) + start - extra, length + extra)
        second = cut(fine_latent, half - mine + start - extra, length + extra)
        first, second = send(after(first, mate[-1]), to_first), send(after(second, mate[-1]), to_second)
        chunks.append([first, fine_latent, second])

    both = jnp.concatenate([aux.astype(F32), weights])
    both = jnp.where(matched, cut(both, mine, half), hand_over(cut(both, half - mine, half)))
    aux, weights = both[: aux.shape[0]].astype(jnp.int32), both[aux.shape[0] :]
    aux = jnp.concatenate([aux[:-1], aux[-1:] - mine])

    making = dict(segments=segments, w_parent=w_parent, coarse=coarse)
    sources = [((0, None),), ((1, 0), (2, None))]
    result = jnp.zeros_like(fine_latent)
    moved = []
    for c, (start, length) in enumerate(shares(half)):
        out, kept, *made = run(
            start, length, aux, chunks[c], sources, weights, places, **(making if c == 0 else dict(table=table))
        )
        table = made[0] if made else table
        moved.append((start, kept, send(out, from_first), send(kept, to_second)))
    for start, kept, first, second in moved:
        result = lax.dynamic_update_slice_in_dim(result, jnp.where(matched, kept, first), mine + start, 1)
        result = lax.dynamic_update_slice_in_dim(
            result, jnp.where(matched, first, second), half - mine + start, 1
        )
    return result


def shards(
    fine_latent,
    coarse_latent,
    parents,
    interp_weights,
    live_rows,
    w_fine,
    w_parent,
    w_edge_out,
    w_node_fine,
    w_node_agg,
    w_node_out,
    edge_bias,
    node_bias,
    norm_gain,
    norm_bias,
):
    groups, domains = lax.axis_size("feat"), lax.axis_size("dom")
    rank = lax.axis_index("feat")
    own_features = fine_latent.shape[0]
    owners = [(rank - r) % groups for r in range(groups)]
    pairing = groups == 2 and domains % 2 == 0
    flip = jnp.where(lax.axis_index("dom") % 2 == rank, 1, 0) if pairing else 0

    def ordered(weight, axis, flip=flip):
        parts = [lax.dynamic_slice_in_dim(weight, o * own_features, own_features, axis) for o in owners]
        if pairing:
            parts = [jnp.where(flip == 1, parts[1], parts[0]), jnp.where(flip == 1, parts[0], parts[1])]
        return jnp.concatenate(parts, axis=axis)

    params = (
        jnp.concatenate([ordered(w_fine, 0), ordered(w_node_fine, 0)], axis=1),
        w_edge_out,
        w_node_agg,
        ordered(w_node_out, 1).T,
        jnp.concatenate([edge_bias, node_bias])[None],
        jnp.broadcast_to(ordered(norm_gain, 0)[:, None], (norm_gain.shape[0], 128)),
        jnp.broadcast_to(ordered(norm_bias, 0)[:, None], (norm_bias.shape[0], 128)),
    )

    def run(start, nodes, aux, arrays, sources, weights, places, **table):
        scales = jnp.pad(weights, ((0, 8 - weights.shape[0]), (0, 0)))
        return update(start, nodes, aux, arrays, sources, scales, params, places, **table)

    count = parents.shape[1]
    slots = 2 * parents + PAD
    aux = jnp.concatenate([slots, jnp.broadcast_to(live_rows[:, None], (1, count))])
    plan = paired if pairing else plain
    return plan(fine_latent, coarse_latent, aux, interp_weights, ordered(w_parent, 0, 0), run)


def solution(mesh):
    in_specs = (P("feat", "dom"), P("feat", "dom"), P(None, "dom"), P(None, "dom"), P("dom")) + (P(),) * 10
    return jax.shard_map(shards, mesh=mesh, in_specs=in_specs, out_specs=P("feat", "dom"), check_vma=False)
```

```python
import functools

import jax
import jax.numpy as jnp
from jax import lax
from jax.experimental import pallas as pl
from jax.experimental.pallas import tpu as pltpu
from jax.sharding import PartitionSpec as P

F32 = jnp.float32
BF16 = jnp.bfloat16
PAD = 8
SHARE = 4
PARTS = 1
STEP = 256
GROUPS = 13


def dot(a, b, ca, cb):
    return lax.dot_general(a, b, (((ca,), (cb,)), ((), ())), preferred_element_type=F32)


def fill_table(segments, step, places, refs, weight, table, landed, sems):
    rows = (table.shape[0] - 2 * PAD) // 6
    features = landed.shape[2] // sems.shape[2]
    table[pl.ds(0, PAD), :] = jnp.zeros((PAD, 128), F32)
    table[pl.ds(PAD + 6 * rows, PAD), :] = jnp.zeros((PAD, 128), F32)

    def copies(segment, i, slot, which):
        found = []
        for p, (sources, first) in enumerate(segments[segment][3]):
            at = pl.multiple_of(first + i * step, 128)
            found.append(
                pltpu.make_async_copy(
                    refs[sources[min(which, len(sources) - 1)]].at[:, pl.ds(at, step)],
                    landed.at[segment % 2, slot, pl.ds(p * features, features), :],
                    sems.at[segment % 2, slot, p],
                )
            )
        return found

    def start(segment, i, slot):
        if all(len(sources) == 1 for sources, _ in segments[segment][3]):
            for copy in copies(segment, i, slot, 0):
                copy.start()
            return
        for which in range(2):

            @pl.when(places[3] == which)
            def _(which=which):
                for copy in copies(segment, i, slot, which):
                    copy.start()

    start(0, 0, 0)
    for segment, (window, row, length, _) in enumerate(segments):
        steps = length // step
        if segment + 1 < len(segments):
            start(segment + 1, 0, 0)

        def one(i, carry, segment=segment, window=window, row=row, steps=steps):
            slot = lax.rem(i, 2)

            @pl.when(i + 1 < steps)
            def _():
                start(segment, i + 1, 1 - slot)

            for copy in copies(segment, i, slot, 0):
                copy.wait()
            projected = dot(landed[segment % 2, slot], weight[...], 0, 0)
            base = pl.multiple_of(PAD + 2 * (places[window] * rows + row + i * step), 8)
            table[pl.ds(base, step, stride=2), :] = projected[:, :128]
            table[pl.ds(base + 1, step, stride=2), :] = projected[:, 128:]
            return carry

        lax.fori_loop(0, steps, one, 0)


def update_kernel(sources, step, start, segments, table_step, places, aux, *refs):
    count = len(sources)
    given = 1 + max(at for source in sources for at, _ in source)
    arrays, refs = refs[:given], refs[given:]
    given, refs = refs[:8], refs[8:]
    held_here, refs = refs[-8:], refs[:-8]
    scales, w_latent, w_edge, w_agg, w_out_t, bias, gain, shift = held_here
    table, latents, fine, total, earlier, later, scale_rows, slots, live, sems, given_sems = refs[-11:]
    refs = refs[:-11]
    fetches = [
        pltpu.make_async_copy(far if at else far.at[:, pl.ds(start, near.shape[1])], near, given_sems.at[at])
        for at, (far, near) in enumerate(zip(given, held_here))
    ]
    features, nodes = latents.shape[0] // count, latents.shape[1]
    parents = slots.shape[0] // nodes
    if segments is None:
        kept, outs = refs[0], refs[1:]
        move = pltpu.make_async_copy(kept, table, sems.at[parents + 1 + count])
        move.start()
    else:
        w_parent, *coarse = refs[: -count - 3]
        *outs, kept, landed, landed_sems = refs[-count - 3 :]
        move = pltpu.make_async_copy(table, kept, sems.at[parents + 1 + count])
    held = aux.shape[0] // (parents + 1)
    fetches.append(pltpu.make_async_copy(aux.at[pl.ds(parents * start, parents * nodes)], slots, sems.at[0]))
    fetches.append(pltpu.make_async_copy(aux.at[pl.ds(parents * held, 1024)], live, sems.at[parents]))
    for fetch in fetches:
        fetch.start()

    def bring(p, which):
        at, shifted = sources[p][min(which, len(sources[p]) - 1)]
        column = arrays[at].shape[1] - nodes if shifted is None else pl.multiple_of(places[4] + start, 128)
        return pltpu.make_async_copy(
            arrays[at].at[:, pl.ds(column, nodes)],
            latents.at[pl.ds(p * features, features), :],
            sems.at[parents + 1 + p],
        )

    for p, source in enumerate(sources):
        for which in range(len(source)):

            @pl.when((places[3] == which) | (len(source) == 1))
            def _(p=p, which=which):
                bring(p, which).start()

    if segments is not None:
        fill_table(segments, table_step, places, coarse, w_parent, table, landed, landed_sems)
        move.start()
    for fetch in fetches:
        fetch.wait()
    for p in range(count):
        bring(p, 0).wait()
    if segments is None:
        move.wait()
    sublane = lax.broadcasted_iota(jnp.int32, (8, 128), 0)
    owns = [sublane >= 2 * j for j in range(4)]

    def begin(i):
        columns = pl.ds(pl.multiple_of(i * step, step), step)
        first = dot(latents[:, columns], w_latent[...], 0, 0) + bias[...]
        return first, scales[:, pl.ds(pl.multiple_of(i * step, step), step)].T

    def keep(first, scale_columns):
        width = first.shape[1] // 2
        fine[pl.ds(0, step, stride=2), :] = first[:, :128]
        fine[pl.ds(1, step, stride=2), :] = first[:, 128:width]
        later[...] = first[:, width:]
        scale_rows[pl.ds(0, step, stride=2), :] = scale_columns
        scale_rows[pl.ds(1, step, stride=2), :] = scale_columns

    def group(at, g):
        part = fine[pl.ds(g * 8, 8), :]
        scale = scale_rows[pl.ds(g * 8, 8), :]
        acc = None
        for k in range(parents):
            rows = None
            for j in range(4):
                loaded = table[pl.ds(slots[at + (k * step + g * 4 + j)], 8), :]
                rows = loaded if rows is None else jnp.where(owns[j], loaded, rows)
            hidden = jnp.maximum(part + rows, 0.0) * scale[:, k : k + 1]
            acc = hidden if acc is None else acc + hidden
        return acc

    def widened(ref):
        return jnp.concatenate([ref[...]] * (step // 128), axis=1)

    def finish(i, summed, own_part):
        at = pl.multiple_of(i * step, step)
        aggregate = dot(summed.astype(BF16), w_edge[...], 1, 0).astype(BF16)
        yield
        node_hidden = jnp.maximum(own_part + dot(aggregate, w_agg[...], 1, 0), 0.0).astype(BF16)
        yield
        output = dot(w_out_t[...], node_hidden, 1, 1)
        yield
        centered = output - jnp.mean(output, axis=0, keepdims=True)
        spread = jnp.mean(centered * centered, axis=0, keepdims=True)
        yield
        normed = centered * lax.rsqrt(spread + 1e-05) * widened(gain) + widened(shift)
        column = start + at + lax.broadcasted_iota(jnp.int32, (1, step), 1)
        moved = jnp.where(column < live[0], normed, 0.0)
        yield (latents[:, pl.ds(at, step)].astype(F32) + moved).astype(BF16)

    def last(parts):
        for value in parts:
            pass
        return value

    def write(i, result):
        for r in range(count):
            outs[r][:, pl.ds(pl.multiple_of(i * step, step), step)] = result[r * features : (r + 1) * features]

    def gathered():
        return jnp.concatenate([total[pl.ds(0, step, stride=2), :], total[pl.ds(1, step, stride=2), :]], axis=1)

    steps = nodes // step
    keep(*begin(0))

    def one_step(i, carry):
        before, after = jnp.maximum(i - 1, 0), jnp.minimum(i + 1, steps - 1)
        summed, own_part, current = gathered(), earlier[...], later[...]
        parts = finish(before, summed, own_part)
        base = pl.multiple_of(i * (parents * step), parents * step)
        begun = begin(after)
        for first in range(0, step // 4, GROUPS):
            result = next(parts, None) if first < 4 * GROUPS else last(parts)
            sums = [group(base, g) for g in range(first, min(first + GROUPS, step // 4))]
            total[pl.ds(first * 8, len(sums) * 8), :] = jnp.concatenate(sums, axis=0)
        write(before, result)
        earlier[...] = current
        keep(*begun)
        return carry

    lax.fori_loop(0, steps, one_step, 0)
    write(steps - 1, last(finish(steps - 1, gathered(), earlier[...])))
    if segments is not None:
        move.wait()


def by_step(aux, step):
    slots = aux[:-1].reshape(aux.shape[0] - 1, -1, step).transpose(1, 0, 2)
    return jnp.concatenate([slots.reshape(-1), aux[-1]])


def update(
    start, nodes, aux, arrays, sources, scales, params, places, table=None, segments=None, w_parent=None, coarse=()
):
    count, features = len(sources), arrays[0].shape[0]
    parents = aux.shape[0] - 1
    step = min(STEP, nodes)
    vmem = pl.BlockSpec(memory_space=pltpu.VMEM)
    smem = pl.BlockSpec(memory_space=pltpu.SMEM)
    far = pl.BlockSpec(memory_space=pltpu.HBM)
    out_shape = [jax.ShapeDtypeStruct((features, nodes), BF16)] * count
    operands = [places, by_step(aux, step), *arrays, scales, *params]
    specs = [smem, far] + [far] * (len(arrays) + 1 + len(params))
    scratch, table_step = [], 0
    if segments is None:
        operands, specs = operands + [table], specs + [far]
    else:
        operands, specs = operands + [w_parent, *coarse], specs + [vmem] + [far] * len(coarse)
        table_step = min(2048, segments[0][2])
        table = jax.ShapeDtypeStruct((2 * sum(segment[2] for segment in segments) + 2 * PAD, 128), F32)
        out_shape.append(table)
        scratch = [
            pltpu.VMEM((2, 2, w_parent.shape[0], table_step), BF16),
            pltpu.SemaphoreType.DMA((2, 2, len(segments[0][3]))),
        ]
    return pl.pallas_call(
        functools.partial(update_kernel, sources, step, start, segments, table_step),
        out_shape=out_shape,
        in_specs=specs,
        out_specs=[vmem] * count + [far] * (len(out_shape) - count),
        scratch_shapes=scratch
        + [
            pltpu.VMEM(table.shape, F32),
            pltpu.VMEM((count * features, nodes), BF16),
            pltpu.VMEM((2 * step, 128), F32),
            pltpu.VMEM((2 * step, 128), F32),
            pltpu.VMEM((step, 256), F32),
            pltpu.VMEM((step, 256), F32),
            pltpu.VMEM((2 * step, 8), F32),
            pltpu.SMEM((parents * nodes,), jnp.int32),
            pltpu.SMEM((1024,), jnp.int32),
            pltpu.SemaphoreType.DMA((parents + 2 + count,)),
            pltpu.SemaphoreType.DMA((1 + len(params),)),
            pltpu.VMEM((scales.shape[0], nodes), F32),
        ]
        + [pltpu.VMEM(param.shape, param.dtype) for param in params],
        compiler_params=pltpu.CompilerParams(vmem_limit_bytes=40 << 20, fuse_transposed_lhs_in_matmul=True),
        cost_estimate=pl.CostEstimate(flops=nodes * 700000, bytes_accessed=nodes * 2048, transcendentals=nodes),
    )(*operands)


def after(value, *others):
    return lax.optimization_barrier((value, *others))[0]


def shares(nodes):
    first = nodes * SHARE // 8 // STEP * STEP
    return [(0, first), (first, nodes - first)]


def cut(array, at, size):
    return lax.dynamic_slice_in_dim(array, at, size, 1)


def plain(fine_latent, coarse_latent, aux, weights, w_parent, run):
    groups, domains = lax.axis_size("feat"), lax.axis_size("dom")
    rank = lax.axis_index("feat")
    per_device = fine_latent.shape[1] // groups
    forward = [(i, i + 1) for i in range(domains - 1)]
    backward = [(i + 1, i) for i in range(domains - 1)]

    def turn(value, r):
        return lax.ppermute(value, "feat", [(i, (i + r) % groups) for i in range(groups)])

    own = [coarse_latent] + [turn(coarse_latent, r) for r in range(1, groups)]
    low = [lax.ppermute(piece, "dom", forward) for piece in own]
    high = [lax.ppermute(piece, "dom", backward) for piece in own]
    first_row = rank * per_device
    rows = coarse_latent.shape[1]
    segments = [
        (w, 0, rows, [((w * groups + p,), 0) for p in range(groups)]) for w in range(3)
    ]
    making = dict(segments=segments, w_parent=w_parent, coarse=low + own + high)
    places = jnp.stack([0, 1, 2, 0, first_row]).astype(jnp.int32)
    sources = [((0, 0),)] + [((r, None),) for r in range(1, groups)]
    aux = cut(aux, first_row, per_device)
    aux = jnp.concatenate([aux[:-1], aux[-1:] - first_row])
    weights = cut(weights, first_row, per_device)
    result = fine_latent
    arrived = []
    for c, (start, length) in enumerate(shares(per_device)):
        pieces = [fine_latent]
        for r in range(1, groups):
            part = cut(fine_latent, ((rank + r) % groups) * per_device + start, length)
            pieces.append(turn(after(part, own[-1]), r))
        outs = run(start, length, aux, pieces, sources, weights, places, **(making if c == 0 else dict(table=table)))
        table = outs[-1] if c == 0 else table
        result = lax.dynamic_update_slice_in_dim(result, outs[0], first_row + start, 1)
        for r in range(1, groups):
            arrived.append((turn(outs[r], -r), ((rank + r) % groups) * per_device + start))
    for part, at in arrived:
        result = lax.dynamic_update_slice_in_dim(result, part, at, 1)
    return result


def paired(fine_latent, coarse_latent, aux, weights, w_parent, run):
    domains = lax.axis_size("dom")
    side, rank = lax.axis_index("dom") % 2, lax.axis_index("feat")
    matched = side == rank
    pairs = range(domains // 2)

    def send(value, moves):
        perm = [((2 * c + a) * 2 + b, (2 * c + x) * 2 + y) for c in pairs for (a, b), (x, y) in moves]
        return lax.ppermute(value, ("dom", "feat"), perm)

    def swap_rank(value):
        return send(value, [((k, f), (k, 1 - f)) for k in range(2) for f in range(2)])

    def swap_side(value):
        return send(value, [((k, f), (1 - k, f)) for k in range(2) for f in range(2)])

    def halo(value):
        perm = [((2 * c - 1) * 2, (2 * c) * 2) for c in pairs if c > 0]
        perm += [((2 * c + 2) * 2 + 1, (2 * c + 1) * 2 + 1) for c in pairs if c + 1 < len(pairs)]
        return lax.ppermute(value, ("dom", "feat"), perm)

    def hand_over(value):
        return send(value, [((0, 0), (1, 0)), ((1, 1), (0, 1))])

    to_first = [((0, 0), (1, 0)), ((1, 1), (0, 1)), ((0, 1), (0, 0)), ((1, 0), (1, 1))]
    from_first = [(b, a) for a, b in to_first]
    to_second = [((0, 1), (1, 0)), ((1, 0), (0, 1))]

    half = fine_latent.shape[1] // 2
    mine = side * half
    rows = coarse_latent.shape[1]
    part = rows // PARTS
    mate = []
    for i in range(PARTS):
        piece = lax.slice_in_dim(coarse_latent, i * part, (i + 1) * part, axis=1)
        mate.append(swap_rank(after(piece, mate[-1]) if mate else piece))
    halo_own, other = halo(coarse_latent), swap_side(after(coarse_latent, mate[-1]))
    halo_mate, other_mate = [halo(piece) for piece in mate], [swap_side(piece) for piece in mate]
    passed_own, passed_mate = hand_over(halo_own), [hand_over(piece) for piece in halo_mate]
    coarse = [coarse_latent, other, halo_own, passed_own, *mate, *other_mate, *halo_mate, *passed_mate]
    segments = []
    for window, own in enumerate([(0,), (1,), (2, 3)]):
        for i in range(PARTS):
            came = tuple(4 + (w + window) * PARTS + i for w in range(len(own)))
            segments.append((window, i * part, part, [(own, i * part), (came, 0)]))
    places = jnp.stack([side + 1 - rank, 2 - side - rank, 2 * rank, jnp.where(matched, 0, 1), mine])
    places = places.astype(jnp.int32)

    chunks = []
    for start, length in shares(half):
        extra = max(half // 2 - length, 0)
        first = cut(fine_latent, jnp.where(matched, half - mine, mine) + start - extra, length + extra)
        second = cut(fine_latent, half - mine + start - extra, length + extra)
        first, second = send(after(first, mate[-1]), to_first), send(after(second, mate[-1]), to_second)
        chunks.append([first, fine_latent, second])

    both = jnp.concatenate([aux.astype(F32), weights])
    both = jnp.where(matched, cut(both, mine, half), hand_over(cut(both, half - mine, half)))
    aux, weights = both[: aux.shape[0]].astype(jnp.int32), both[aux.shape[0] :]
    aux = jnp.concatenate([aux[:-1], aux[-1:] - mine])

    making = dict(segments=segments, w_parent=w_parent, coarse=coarse)
    sources = [((0, None),), ((1, 0), (2, None))]
    result = jnp.zeros_like(fine_latent)
    moved = []
    for c, (start, length) in enumerate(shares(half)):
        out, kept, *made = run(
            start, length, aux, chunks[c], sources, weights, places, **(making if c == 0 else dict(table=table))
        )
        table = made[0] if made else table
        moved.append((start, kept, send(out, from_first), send(kept, to_second)))
    for start, kept, first, second in moved:
        result = lax.dynamic_update_slice_in_dim(result, jnp.where(matched, kept, first), mine + start, 1)
        result = lax.dynamic_update_slice_in_dim(
            result, jnp.where(matched, first, second), half - mine + start, 1
        )
    return result


def shards(
    fine_latent,
    coarse_latent,
    parents,
    interp_weights,
    live_rows,
    w_fine,
    w_parent,
    w_edge_out,
    w_node_fine,
    w_node_agg,
    w_node_out,
    edge_bias,
    node_bias,
    norm_gain,
    norm_bias,
):
    groups, domains = lax.axis_size("feat"), lax.axis_size("dom")
    rank = lax.axis_index("feat")
    own_features = fine_latent.shape[0]
    owners = [(rank - r) % groups for r in range(groups)]
    pairing = groups == 2 and domains % 2 == 0
    flip = jnp.where(lax.axis_index("dom") % 2 == rank, 1, 0) if pairing else 0

    def ordered(weight, axis, flip=flip):
        parts = [lax.dynamic_slice_in_dim(weight, o * own_features, own_features, axis) for o in owners]
        if pairing:
            parts = [jnp.where(flip == 1, parts[1], parts[0]), jnp.where(flip == 1, parts[0], parts[1])]
        return jnp.concatenate(parts, axis=axis)

    params = (
        jnp.concatenate([ordered(w_fine, 0), ordered(w_node_fine, 0)], axis=1),
        w_edge_out,
        w_node_agg,
        ordered(w_node_out, 1).T,
        jnp.concatenate([edge_bias, node_bias])[None],
        jnp.broadcast_to(ordered(norm_gain, 0)[:, None], (norm_gain.shape[0], 128)),
        jnp.broadcast_to(ordered(norm_bias, 0)[:, None], (norm_bias.shape[0], 128)),
    )

    def run(start, nodes, aux, arrays, sources, weights, places, **table):
        scales = jnp.pad(weights, ((0, 8 - weights.shape[0]), (0, 0)))
        return update(start, nodes, aux, arrays, sources, scales, params, places, **table)

    count = parents.shape[1]
    slots = 2 * parents + (PAD - 2 * (jnp.arange(count, dtype=jnp.int32) % 4))
    aux = jnp.concatenate([slots, jnp.broadcast_to(live_rows[:, None], (1, count))])
    plan = paired if pairing else plain
    return plan(fine_latent, coarse_latent, aux, interp_weights, ordered(w_parent, 0, 0), run)


def solution(mesh):
    in_specs = (P("feat", "dom"), P("feat", "dom"), P(None, "dom"), P(None, "dom"), P("dom")) + (P(),) * 10
    return jax.shard_map(shards, mesh=mesh, in_specs=in_specs, out_specs=P("feat", "dom"), check_vma=False)
```
